32 devices in a mesh: section: 2 (over core), dp: 4 (over z), seq: 4 (over y, x).
Axes of the slice: x: 2, y: 2, z: 4, core: 2. Of those that a mesh axis runs over, the one named last changes fastest.
Arguments:
- inputs: bfloat16 [4, 4, 1024, 1280], P(None, 'dp', 'seq'), may hold values from -6 to 6
- lengths: int32 [4, 4], P(None, 'dp'), may hold values from 256 to 1024, as said below
- mlm_mask: int32 [4, 4, 1024], P(None, 'dp', 'seq'), may hold values 0 or 1
- true_types: int32 [4, 4, 1024], P(None, 'dp', 'seq'), may hold values from 0 to 29
- gain_in: bfloat16 [2, 1280], P('section'), may hold values from 0.25 to 1.75
- bias_in: bfloat16 [2, 1280], P('section'), may hold values from -3 to 3
- gain_mid: bfloat16 [2, 2, 640], P('section'), may hold values from 0.25 to 1.75
- bias_mid: bfloat16 [2, 2, 640], P('section'), may hold values from -3 to 3
- w_in: bfloat16 [2, 1280, 640], P('section'), may hold values from -0.15625 to 0.15625
- conv_w: bfloat16 [2, 5, 640, 640], P('section'), may hold values from -0.109375 to 0.109375
- w_out: bfloat16 [2, 640, 1280], P('section'), may hold values from -0.25 to 0.25
- decoder: bfloat16 [1280, 30], replicated, may hold values from -0.15625 to 0.15625
- cotangent: bfloat16 [4, 4, 1024, 1280], P(None, 'dp', 'seq'), may hold values from -6 to 6
Outputs:
- activations: bfloat16 [2, 4, 4, 1024, 1280], P('section', None, 'dp', 'seq')
- input_grads: bfloat16 [2, 4, 4, 1024, 1280], P('section', None, 'dp', 'seq')
- grad_gain_in: float32 [2, 1280], P('section')
- grad_bias_in: float32 [2, 1280], P('section')
- grad_gain_mid: float32 [2, 2, 640], P('section')
- grad_bias_mid: float32 [2, 2, 640], P('section')
- grad_w_in: float32 [2, 1280, 640], P('section')
- grad_conv_w: float32 [2, 5, 640, 640], P('section')
- grad_w_out: float32 [2, 640, 1280], P('section')
- counts: float32 [30], replicated
The draws below stay inside these ranges and needn't reach their ends.
Inputs may be any that keep to these rules, and one draw needn't show every extreme that they name: `lengths`: in every column one of the 4 sequences, drawn from the seed, has the full length 1024.
All inputs are finite; a program needn't handle non-finite values. No bound on the sum of `mlm_mask` on one device may be relied on, other than what follows from the above.
Results may differ from the reference program's by a relative error of at most 0.011.
Values may be sent and summed in bfloat16 or wider, within the bound.
A program may use at most 128 MiB of HBM per device.

```python
import jax
import jax.numpy as jnp
from jax import lax

D = 1280
H = 640
K = 5
V = 30
DILATION_ONE = 2
DILATION_SECOND = 128
MB = 4
B = 4
L = 1024


def draw_lengths(key, part):
    key = jax.random.fold_in(key, 5)
    first_key, second_key = jax.random.split(key)
    drawn = jax.random.randint(first_key, (MB, B), L // 4, L + 1)
    chosen = jax.random.randint(second_key, (1, B), 0, MB)
    batches = jnp.arange(MB, dtype=jnp.int32)[:, None]
    return jnp.where(batches == chosen, L, drawn).astype(jnp.int32)


def with_ends(values, own_key, least, top_value):
    spot = [jax.random.randint(jax.random.fold_in(own_key, axis), (), 0, length) for axis, length in enumerate(values.shape)]
    widest = values.shape.index(max(values.shape))
    neighbour = spot[:widest] + [(spot[widest] + 1) % values.shape[widest]] + spot[widest + 1:]
    return values.at[tuple(spot)].set(least).at[tuple(neighbour)].set(top_value)


def block_scale(own_key, dims, cuts, low, top_value):
    level = 1.0
    for dim, shards_of in cuts:
        heights = jax.random.uniform(jax.random.fold_in(jax.random.fold_in(own_key, 6), dim), (shards_of,), jnp.float32, low / len(cuts), top_value / len(cuts))
        level = level * jnp.repeat(jnp.exp(heights), dims[dim] // shards_of).reshape((-1,) + (1,) * (len(dims) - 1 - dim))
    return level


def noise(rng, extent, scale, bound, pieces=(), kind=jnp.bfloat16):
    level = block_scale(rng, extent, pieces, -0.22, 0.18) if pieces else 1.0
    values = jax.random.normal(rng, extent, jnp.float32) * scale * level
    return jnp.minimum(jnp.maximum(values, -bound), bound).astype(kind)


def setup_inputs(seed: int = 0) -> dict:
    arg_keys = jax.random.split(jax.random.key(seed), 14)
    return {
        "inputs": noise(arg_keys[0], (MB, B, L, D), 1.0, 6.0, ((1, 4), (2, 4))),
        "lengths": draw_lengths(jax.random.fold_in(arg_keys[13], 71), 0),
        "mlm_mask": with_ends((jax.random.randint(arg_keys[2], (MB, B, L), 0, 20) < 3).astype(jnp.int32), jax.random.fold_in(arg_keys[2], 1), 0, 1),
        "true_types": with_ends(jax.random.randint(arg_keys[3], (MB, B, L), 0, V), jax.random.fold_in(arg_keys[3], 1), 0, V - 1).astype(jnp.int32),
        "gain_in": jnp.clip(1.0 + 0.15 * jax.random.normal(arg_keys[4], (2, D), jnp.float32), 0.25, 1.75).astype(jnp.bfloat16),
        "bias_in": noise(arg_keys[5], (2, D), 0.5, 3.0, ((0, 2),)),
        "gain_mid": jnp.clip(1.0 + 0.15 * jax.random.normal(arg_keys[6], (2, 2, H), jnp.float32), 0.25, 1.75).astype(jnp.bfloat16),
        "bias_mid": noise(arg_keys[7], (2, 2, H), 0.5, 3.0, ((0, 2),)),
        "w_in": noise(arg_keys[8], (2, D, H), D ** -0.5, 0.15625, ((0, 2),)),
        "conv_w": noise(arg_keys[9], (2, K, H, H), (K * H) ** -0.5, 0.109375, ((0, 2),)),
        "w_out": noise(arg_keys[10], (2, H, D), H ** -0.5, 0.25, ((0, 2),)),
        "decoder": noise(arg_keys[11], (D, V), D ** -0.5, 0.15625),
        "cotangent": noise(arg_keys[12], (MB, B, L, D), 1.0, 6.0, ((1, 4), (2, 4))),
    }


EPS = 1e-05

@jax.custom_vjp
def low(v):
    return lax.optimization_barrier(v.astype(jnp.bfloat16)).astype(jnp.float32)

@jax.custom_vjp
def low_back(v):
    return v

def low_keep(v):
    return (low(v), None)

def low_pass(kept, grad):
    return (grad,)

def back_keep(v):
    return (v, None)

def back_low(kept, grad):
    return (low(grad),)
low.defvjp(low_keep, low_pass)
low_back.defvjp(back_keep, back_low)

def layer_norm(value_entries, gain, shift):
    middle_position = value_entries - lax.optimization_barrier(jnp.mean(value_entries, axis=-1, keepdims=True))
    spread = lax.optimization_barrier(jnp.mean(middle_position * middle_position, axis=-1, keepdims=True))
    return middle_position * lax.rsqrt(spread + EPS) * gain + shift

def matmul_high(left, right):
    return jnp.dot(left, right, precision=lax.Precision.HIGHEST, preferred_element_type=jnp.float32)

def residual_block(value_entries, layer_parameters, keep_flags, dilation_rate):
    gain_first, shift_first, gains_mid, shifts_mid, weight_first, kernel, weight_last = layer_parameters
    first = low(jax.nn.gelu(layer_norm(value_entries, gain_first, shift_first)))
    hidden = low_back(matmul_high(first, weight_first))
    second = low(jax.nn.gelu(layer_norm(hidden, gains_mid[0], shifts_mid[0])) * keep_flags)
    receptive_reach = K // 2 * dilation_rate
    padded = jnp.pad(second, ((receptive_reach, receptive_reach), (0, 0)))
    mixed = jnp.zeros((L, H), jnp.float32)
    for tap in range(K):
        mixed = mixed + matmul_high(padded[tap * dilation_rate:tap * dilation_rate + L], kernel[tap])
    mixed = low_back(mixed)
    third = low(jax.nn.gelu(layer_norm(mixed, gains_mid[1], shifts_mid[1])))
    return value_entries + matmul_high(third, weight_last)

def reference(inputs, lengths, mlm_mask, true_types, gain_in, bias_in, gain_mid, bias_mid, w_in, conv_w, w_out, decoder, cotangent):
    total = MB * B
    stacks = [p.astype(jnp.float32) for p in (gain_in, bias_in, gain_mid, bias_mid, w_in, conv_w, w_out)]
    params_one = tuple((p[0] for p in stacks))
    params_two = tuple((p[1] for p in stacks))
    seqs_in = inputs.astype(jnp.float32).reshape(total, L, D)
    seqs_cot = cotangent.astype(jnp.float32).reshape(total, L, D)
    seq_lengths = lengths.reshape(total)
    seq_masks = mlm_mask.reshape(total, L)
    seq_types = true_types.reshape(total, L)
    decoder32 = decoder.astype(jnp.float32)
    positions = jnp.arange(L, dtype=jnp.int32)
    labels = jnp.arange(V, dtype=jnp.int32)

    def one_sequence(carry, item):
        grads, counts = carry
        seq_in, seq_cot, length, mask_row, type_row = item
        keep_flags = (positions < length).astype(jnp.float32)[:, None]

        def layer_one(value_entries, *layer_parameters):
            return residual_block(value_entries, layer_parameters, keep_flags, DILATION_ONE)

        def layer_two(value_entries, *layer_parameters):
            return residual_block(value_entries, layer_parameters, keep_flags, DILATION_SECOND)
        out_one, back_one = jax.vjp(layer_one, seq_in, *params_one)
        out_one = low(out_one)
        out_two, back_two = jax.vjp(layer_two, out_one, *params_two)
        out_two = low(out_two)
        grads_two = back_two(seq_cot)
        grad_one = low(grads_two[0])
        grads_one = back_one(grad_one)
        grad_zero = low(grads_one[0])
        grads = tuple((acc + jnp.stack([first, second]) for acc, first, second in zip(grads, grads_one[1:], grads_two[1:])))
        probs = jax.nn.softmax(matmul_high(out_two, decoder32), axis=-1)
        onehot = (type_row[:, None] == labels[None, :]).astype(jnp.float32)
        chance = lax.optimization_barrier(jnp.sum(probs * onehot, axis=-1))
        weight = chance * mask_row.astype(jnp.float32) * keep_flags[:, 0]
        counts = counts + lax.optimization_barrier(jnp.sum(onehot * weight[:, None], axis=0))
        return ((grads, counts), (out_one, out_two, grad_zero, grad_one))
    zeros = tuple((jnp.zeros(p.shape, jnp.float32) for p in stacks))
    init = (zeros, jnp.zeros((V,), jnp.float32))
    (grads, counts), (outs_one, outs_two, grads_zero, grads_one) = lax.scan(one_sequence, init, (seqs_in, seqs_cot, seq_lengths, seq_masks, seq_types))
    shape = (MB, B, L, D)
    activations = jnp.stack([outs_one.reshape(shape), outs_two.reshape(shape)]).astype(jnp.bfloat16)
    input_grads = jnp.stack([grads_zero.reshape(shape), grads_one.reshape(shape)]).astype(jnp.bfloat16)
    return (activations, input_grads, grads[0], grads[1], grads[2], grads[3], grads[4], grads[5], grads[6], counts)
```

```python
import functools

import jax
import jax.numpy as jnp
from jax import lax
from jax.experimental import pallas as pl
from jax.experimental.pallas import tpu as pltpu
from jax.sharding import PartitionSpec as P

EPS = 1e-05
BF, F32 = jnp.bfloat16, jnp.float32
MESH = pl.DeviceIdType.MESH
G0 = 0.7978845608028654
G1 = 0.044715
DIL = 2
HALO = 16
CH = 16


def dot(a, b):
    return lax.dot_general(a, b, (((1,), (0,)), ((), ())), preferred_element_type=F32)


def dot_nt(a, b):
    return lax.dot_general(a, b, (((1,), (1,)), ((), ())), preferred_element_type=F32)


def dot_tn(a, b):
    return lax.dot_general(a, b, (((0,), (0,)), ((), ())), preferred_element_type=F32)


def chunks(rows, fn, size=CH):
    def one(i, _):
        fn(pl.multiple_of(i * size, size))
        return 0

    lax.fori_loop(0, rows // size, one, 0)


def normed(v):
    centre = v - jnp.mean(v, axis=-1, keepdims=True)
    var = jnp.mean(centre * centre, axis=-1, keepdims=True)
    rstd = lax.rsqrt(var + EPS)
    return centre * rstd, rstd


def gelu(u):
    t = jnp.tanh(u * (G0 + (G0 * G1) * (u * u)))
    h = 0.5 * u
    return h + h * t


def gelu_slope(u):
    w = u * u
    t = jnp.tanh(u * (G0 + (G0 * G1) * w))
    return 0.5 * (1.0 + t) + (0.5 * u) * (1.0 - t * t) * (G0 + (3.0 * G0 * G1) * w)


def fold(v):
    rows, width = v.shape
    return jnp.sum(v.reshape(rows // 8, 8, width), axis=0)


def norm_gelu_back(v, dy, gain, shift, dgain, dshift):
    hat, rstd = normed(v)
    du = dy * gelu_slope(hat * gain + shift)
    dhat_raw = du * hat
    if dgain is not None:
        dgain[...] += fold(dhat_raw)
        dshift[...] += fold(du)
    dh = du * gain
    m1 = jnp.mean(dh, axis=-1, keepdims=True)
    m2 = jnp.mean(dh * hat, axis=-1, keepdims=True)
    return rstd * (dh - m1 - hat * m2)


def put_grad(g_ref, unit, value, col0=0):
    m, n = value.shape
    per = m // 32
    value = value.astype(BF)
    for j in range(n // 128):
        block = value[:, j * 128 : (j + 1) * 128].reshape(m // 16, 16, 128)
        for h in range(2):
            g_ref[h, pl.ds(unit + (col0 + j) * per, per)] = block[h * per : (h + 1) * per]


CONV0, OUT0, IN0, EXTRA0, UNITS = 0, 500, 700, 900, 912


def k1(xe, cot, scal, w_in1, conv1, w_out1, w_in2, w_out2, gi1, bi1, gm1, bm1, gi2, bi2, gm2, bm2,
       out1, first1, hidden1, sec1, mixed1, third1, first2, hidden2, sec2, dthird2, fe, he, me):
    base = scal[0]
    rows, seg = xe.shape[1], out1.shape[1]
    for m in range(2):
        def a(i):
            hat, _ = normed(xe[m, pl.ds(i, CH)].astype(F32))
            fe[pl.ds(i, CH)] = gelu(hat * gi1[...] + bi1[...]).astype(BF)

        chunks(rows, a)
        first1[m] = fe[pl.ds(HALO, seg)]
        he[...] = dot(fe[...], w_in1[0])
        hidden1[m] = he[pl.ds(HALO, seg)]
        sec1[m, pl.ds(0, 8)] = jnp.zeros((8, sec1.shape[2]), F32)
        sec1[m, pl.ds(rows + 8, 8)] = jnp.zeros((8, sec1.shape[2]), F32)
        length = scal[1 + m]

        def b(i):
            hat, _ = normed(he[pl.ds(i, CH)])
            pos = base - HALO + i + lax.broadcasted_iota(jnp.int32, (CH, 1), 0)
            keep = jnp.logical_and(pos >= 0, pos < length)
            val = gelu(hat * gm1[pl.ds(0, 1)] + bm1[pl.ds(0, 1)])
            sec1[m, pl.ds(i + 8, CH)] = jnp.where(keep, val, 0.0).astype(BF).astype(F32)

        chunks(rows, b)
        acc = None
        for k in range(5):
            term = dot(sec1[m, pl.ds(8 + DIL * (k - 2), rows)].astype(BF), conv1[0, k])
            acc = term if acc is None else acc + term
        mixed1[m] = acc

        def c(i):
            hat, _ = normed(mixed1[m, pl.ds(i + HALO, CH)])
            third1[m, pl.ds(i, CH)] = gelu(hat * gm1[pl.ds(1, 1)] + bm1[pl.ds(1, 1)]).astype(BF)

        chunks(seg, c)
        he[pl.ds(0, seg)] = dot(third1[m], w_out1[0, :, :640])
        me[...] = dot(third1[m], w_out1[0, :, 640:])

        def d(i):
            br = jnp.concatenate([he[pl.ds(i, CH)], me[pl.ds(i, CH)]], axis=1)
            res = (xe[m, pl.ds(i + HALO, CH)].astype(F32) + br).astype(BF)
            out1[m, pl.ds(i, CH)] = res
            hat, _ = normed(res.astype(F32))
            first2[m, pl.ds(i, CH)] = gelu(hat * gi2[...] + bi2[...]).astype(BF)

        chunks(seg, d)
        hidden2[m] = dot(first2[m], w_in2[0])

        def e(i):
            hat, _ = normed(hidden2[m, pl.ds(i, CH)])
            pos = base + i + lax.broadcasted_iota(jnp.int32, (CH, 1), 0)
            val = gelu(hat * gm2[pl.ds(0, 1)] + bm2[pl.ds(0, 1)])
            sec2[m, pl.ds(i, CH)] = jnp.where(pos < length, val, 0.0).astype(BF)

        chunks(seg, e)
        dthird2[m] = dot_nt(cot[m], w_out2[0]).astype(BF)


def k2(sec, dthird, conv2, gm2, bm2, third, dsec, dgb, g_ref, sp, dp, mx, acc_ref):
    rows, w = sec.shape
    pad = 128
    z = jnp.zeros((pad, w), BF)
    for ref in (sp, dp):
        ref[pl.ds(0, pad)] = z
        ref[pl.ds(pad + rows, pad)] = z
    sp[pl.ds(pad, rows)] = sec[...]
    for r in range(0, rows, 256):
        acc = None
        for k in range(5):
            term = dot(sp[pl.ds(64 * k + r, 256)], conv2[0, k])
            acc = term if acc is None else acc + term
        mx[pl.ds(r, 256)] = acc
    dgb[...] = jnp.zeros_like(dgb)

    def a(i):
        v = mx[pl.ds(i, CH)]
        hat, rstd = normed(v)
        gain, shift = gm2[pl.ds(1, 1)], bm2[pl.ds(1, 1)]
        third[pl.ds(i, CH)] = gelu(hat * gain + shift).astype(BF)
        dm = norm_gelu_back(v, dthird[pl.ds(i, CH)].astype(F32), gain, shift, dgb.at[0], dgb.at[1])
        dp[pl.ds(pad + i, CH)] = dm.astype(BF)

    chunks(rows, a)
    dm = dp[pl.ds(pad, rows)]
    for k in range(5):
        put_grad(g_ref, CONV0 + k * 100, dot_tn(sp[pl.ds(64 * k, rows)], dm))
    for r in range(0, rows, 256):
        acc = None
        for k in range(5):
            term = dot_nt(dp[pl.ds(64 * (4 - k) + r, 256)], conv2[0, k])
            acc = term if acc is None else acc + term
        dsec[pl.ds(r, 256)] = acc.astype(BF)


def k3(out1, third2, dsec2, cot, first2, hidden2, w_in2, w_out2, dec, gi2, bi2, gm2, bm2, scal, mask, types,
       out2, grad2, dgbi, dgbm, counts, g_ref, he, me, dh):
    base = scal[0]
    seg = out1.shape[1]
    rows = 2 * seg
    classes = dec.shape[1]
    for ref in (dgbi, dgbm, counts):
        ref[...] = jnp.zeros_like(ref)
    labels = lax.broadcasted_iota(jnp.int32, (1, 128), 1)
    for m in range(2):
        length = scal[1 + m]
        he[...] = dot(third2[m], w_out2[0, :, :640])
        me[...] = dot(third2[m], w_out2[0, :, 640:])

        def a(i):
            br = jnp.concatenate([he[pl.ds(i, CH)], me[pl.ds(i, CH)]], axis=1)
            out2[m, pl.ds(i, CH)] = (out1[m, pl.ds(i, CH)].astype(F32) + br).astype(BF)

        chunks(seg, a)
        logits = dot(out2[m], dec[...])
        logits = jnp.where(labels < 30, logits, -1e30)
        top = jnp.max(logits, axis=-1, keepdims=True)
        ex = jnp.exp(logits - top)
        probs = ex / jnp.sum(ex, axis=-1, keepdims=True)
        pos = base + lax.broadcasted_iota(jnp.int32, (seg, 1), 0)
        weight = jnp.where(pos < length, mask[m].astype(F32), 0.0)
        hit = types[m] == labels
        counts[...] += fold(jnp.where(hit, probs * weight, 0.0))

        def b(i):
            pos = base + i + lax.broadcasted_iota(jnp.int32, (CH, 1), 0)
            ds = jnp.where(pos < length, dsec2[m, pl.ds(i, CH)].astype(F32), 0.0)
            dv = norm_gelu_back(hidden2[m, pl.ds(i, CH)], ds, gm2[pl.ds(0, 1)], bm2[pl.ds(0, 1)], dgbm.at[0], dgbm.at[1])
            dh[m, pl.ds(i, CH)] = dv.astype(BF)

        chunks(seg, b)
        he[...] = dot_nt(dh[m], w_in2[0, :640])
        me[...] = dot_nt(dh[m], w_in2[0, 640:])

        def c(i):
            df = jnp.concatenate([he[pl.ds(i, CH)], me[pl.ds(i, CH)]], axis=1)
            dv = norm_gelu_back(out1[m, pl.ds(i, CH)].astype(F32), df, gi2[...], bi2[...], dgbi.at[0], dgbi.at[1])
            grad2[m, pl.ds(i, CH)] = (cot[m, pl.ds(i, CH)].astype(F32) + dv).astype(BF)

        chunks(seg, c)
    flat = lambda ref: ref[...].reshape(rows, ref.shape[2])
    t2, g2 = flat(third2), flat(cot)
    for j in range(2):
        put_grad(g_ref, 0, dot_tn(t2, g2[:, j * 640 : (j + 1) * 640]), 5 * j)
    f2, d2 = flat(first2), flat(dh)
    put_grad(g_ref, 200, dot_tn(f2, d2))


def k4(xe, ge, scal, first1, hidden1, sec1, mixed1, third1, w_in1, conv1, w_out1, gi1, bi1, gm1, bm1,
       grad1, dgbi, dgbm, g_ref, he, me, dme, dh, dm, swin):
    base = scal[0]
    rows, seg = xe.shape[1], grad1.shape[1]
    for ref in (dgbi, dgbm):
        ref[...] = jnp.zeros_like(ref)
    for m in range(2):
        length = scal[1 + m]
        he[...] = dot_nt(ge[m], w_out1[0])
        gain, shift = gm1[pl.ds(1, 1)], bm1[pl.ds(1, 1)]

        def a(i):
            dv = norm_gelu_back(mixed1[m, pl.ds(i + HALO, CH)], he[pl.ds(i + HALO, CH)], gain, shift, dgbm.at[2], dgbm.at[3])
            dme[pl.ds(i + HALO, CH)] = dv.astype(BF).astype(F32)
            dm[m, pl.ds(i, CH)] = dv.astype(BF)

        chunks(seg, a)
        for edge in (0, rows - HALO):
            dv = norm_gelu_back(mixed1[m, pl.ds(edge, HALO)], he[pl.ds(edge, HALO)], gain, shift, None, None)
            pos = base - HALO + edge + lax.broadcasted_iota(jnp.int32, (HALO, 1), 0)
            inside = jnp.logical_and(pos >= 0, pos < 1024)
            dme[pl.ds(edge, HALO)] = jnp.where(inside, dv, 0.0).astype(BF).astype(F32)
        acc = None
        for k in range(5):
            term = dot_nt(dme[pl.ds(HALO - DIL * (k - 2), seg)].astype(BF), conv1[0, k])
            acc = term if acc is None else acc + term
        he[pl.ds(0, seg)] = acc

        def b(i):
            pos = base + i + lax.broadcasted_iota(jnp.int32, (CH, 1), 0)
            ds = jnp.where(pos < length, he[pl.ds(i, CH)], 0.0)
            dv = norm_gelu_back(hidden1[m, pl.ds(i, CH)], ds, gm1[pl.ds(0, 1)], bm1[pl.ds(0, 1)], dgbm.at[0], dgbm.at[1])
            dh[m, pl.ds(i, CH)] = dv.astype(BF)

        chunks(seg, b)
        he[pl.ds(0, seg)] = dot_nt(dh[m], w_in1[0, :640])
        me[...] = dot_nt(dh[m], w_in1[0, 640:])

        def c(i):
            df = jnp.concatenate([he[pl.ds(i, CH)], me[pl.ds(i, CH)]], axis=1)
            dv = norm_gelu_back(xe[m, pl.ds(i + HALO, CH)].astype(F32), df, gi1[...], bi1[...], dgbi.at[0], dgbi.at[1])
            grad1[m, pl.ds(i, CH)] = (ge[m, pl.ds(i + HALO, CH)].astype(F32) + dv).astype(BF)

        chunks(seg, c)
    flat = lambda v: v.reshape(2 * seg, v.shape[-1])
    t1 = flat(third1[...])
    for j in range(2):
        g1 = flat(ge[:, pl.ds(HALO, seg), pl.ds(j * 640, 640)])
        put_grad(g_ref, OUT0, dot_tn(t1, g1), 5 * j)
    d1 = flat(dm[...])
    for k in range(5):
        for m in range(2):
            swin[pl.ds(m * seg, seg)] = sec1[m, pl.ds(8 + HALO + DIL * (k - 2), seg)].astype(BF)
        put_grad(g_ref, CONV0 + k * 100, dot_tn(swin[...], d1))
    put_grad(g_ref, IN0, dot_tn(flat(first1[...]), flat(dh[...])))


class Ring:
    def __init__(self, N, PU, QU):
        self.N, self.PU, self.QU, self.U = N, PU, QU, PU + QU
        self.kinds = ["D","P1","P2","PZ1","PZ2","PT1","PT2","PT3","G1","G2","Q1","Q2","X1","X2","X3","X4","QT1","QT2","QT3","F"]
    def scratch(self):
        N2, PU, QU, U = 2*self.N, self.PU, self.QU, self.U
        b = lambda u: pltpu.VMEM((N2, u, 16, 128), BF)
        nk = len(self.kinds)
        return [b(U), b(PU//2), b(PU//4), b(PU//4), b(PU//8), b(QU), b(QU//2), b(QU//4), b(QU//8), b(U),
                pltpu.SemaphoreType.DMA((nk, N2)), pltpu.SemaphoreType.DMA((nk, N2))]
    def bind(self, G, two, one, out, D, RP1, RP2, RZ1, RZ2, RQ1, RQ2, RX1, RX2, R, ss, rs):
        N, PU, QU, U = self.N, self.PU, self.QU, self.U
        c, z, q = lax.axis_index("section"), lax.axis_index("dp"), lax.axis_index("seq")
        xb, yb = lax.rem(q, 2), lax.div(q, 2)
        f = jnp.where(c == 0, xb, yb); s = jnp.where(c == 0, yb, xb)
        qx = xb ^ 1;
        nx = (c, z, yb*2 + 1 - xb); ny = (c, z, (1-yb)*2 + xb)
        n1 = (c, z, jnp.where(c == 0, nx[2], ny[2])); n2 = (c, z, jnp.where(c == 0, ny[2], nx[2]))
        side = lax.div(z, 2)
        zp = (c, side*2 + 1 - lax.rem(z, 2), q)
        far = (c, 3 - z, q)
        peer = (1 - c, z, q)
        inner = jnp.logical_or(z == 1, z == 2)
        outer = jnp.logical_not(inner)
        K = {k: i for i, k in enumerate(self.kinds)}
        def cp(k, i, src, dst, dev):
            return pltpu.make_async_remote_copy(src_ref=src, dst_ref=dst, send_sem=ss.at[K[k], i], recv_sem=rs.at[K[k], i], device_id=dev, device_id_type=MESH)
        ds = pl.ds
        H, Q4, E8 = PU//2, PU//4, PU//8
        h, q4, e8 = QU//2, QU//8, QU//8
        def add(dst, a, *bs):
            acc = a[...].astype(F32)
            for b in bs: acc = acc + b[...].astype(F32)
            dst[...] = acc.astype(BF)
        pq = lambda ff, s2: ds((2*ff + s2)*Q4, Q4)
        pch = lambda k: ds((2*f + s)*Q4 + k*E8, E8)
        def qn(k): return ds(PU + k*h, h)
        def qhalf(k, ff): return ds(PU + k*h + ff*(h//2), h//2)
        def qquart(k, ff, s2): return ds(PU + k*h + (2*ff+s2)*(h//4), h//4)
        near, farc = side, 1 - side
        C = dict(
          D=lambda i: cp("D", i, two.at[1-c, i], D.at[i], peer),
          E=lambda i: cp("D", i, one.at[1-c, i-N], D.at[i], peer),
          W=lambda i: cp("D", i, G.at[i], D.at[i], peer),
          P1=lambda i: cp("P1", i, D.at[i, ds((1-f)*H, H)], RP1.at[i], n1),
          P2=lambda i: cp("P2", i, D.at[i, pq(f, 1-s)], RP2.at[i], n2),
          PZ1=lambda i: cp("PZ1", i, D.at[i, pq(f, s)], RZ1.at[i], zp),
          PZ2=lambda i: cp("PZ2", i, D.at[i, pch(farc)], RZ2.at[i], far),
          PT1=lambda i: cp("PT1", i, R.at[i, pch(near)], R.at[i, pch(near)], far),
          PT2=lambda i: cp("PT2", i, R.at[i, pch(near)], R.at[i, pch(near)], zp),
          PT3=lambda i: cp("PT3", i, R.at[i, pch(farc)], R.at[i, pch(farc)], zp),
          G1=lambda i: cp("G1", i, R.at[i, pq(f, s)], R.at[i, pq(f, s)], n2),
          G2=lambda i: cp("G2", i, R.at[i, ds(f*H, H)], R.at[i, ds(f*H, H)], n1),
          Q1=lambda i: cp("Q1", i, D.at[i, ds(PU, QU)], RQ1.at[i], zp),
          Q2=lambda i: cp("Q2", i, D.at[i, qn(farc)], RQ2.at[i], far),
          X1=lambda i: cp("X1", i, D.at[i, qhalf(near, 1-f)], RX1.at[i], n1),
          X2=lambda i: cp("X2", i, D.at[i, qquart(near, f, 1-s)], RX2.at[i], n2),
          X3=lambda i: cp("X3", i, R.at[i, qquart(near, f, s)], R.at[i, qquart(near, f, s)], n2),
          X4=lambda i: cp("X4", i, R.at[i, qhalf(near, f)], R.at[i, qhalf(near, f)], n1),
          QT1=lambda i: cp("QT1", i, R.at[i, qn(near)], R.at[i, qn(near)], far),
          QT2=lambda i: cp("QT2", i, R.at[i, qn(near)], R.at[i, qn(near)], zp),
          QT3=lambda i: cp("QT3", i, R.at[i, qn(farc)], R.at[i, qn(farc)], zp),
        )
        def mine(i): return jnp.where(i < N, 1, 0) == c
        def slot(i): return jnp.where(i < N, i, i - N)
        Fr = lambda i: cp("F", i, R.at[i], out.at[c, slot(i)], peer)
        Fl = lambda i: pltpu.make_async_copy(R.at[i], out.at[c, slot(i)], ss.at[K["F"], i])
        def S0(i):
            @pl.when(i < N)
            def _(): C["D"](i).start()
            @pl.when(i >= N)
            def _(): C["E"](i).start()
        def S1(i):
            C["W"](i).wait()
            add(D.at[i], D.at[i], G.at[i])
            C["P1"](i).start()
            @pl.when(outer)
            def _(): C["Q1"](i).start()
        def S2(i):
            @pl.when(inner)
            def _():
                C["Q1"](i).wait_recv()
                add(D.at[i, qn(farc)], D.at[i, qn(farc)], RQ1.at[i, ds(farc*h, h)])
                C["Q2"](i).start()
            C["P1"](i).wait()
            add(D.at[i, ds(f*H, H)], D.at[i, ds(f*H, H)], RP1.at[i])
            C["P2"](i).start()
            @pl.when(outer)
            def _(): C["Q1"](i).wait_send()
        def S3(i):
            C["P2"](i).wait()
            add(D.at[i, pq(f, s)], D.at[i, pq(f, s)], RP2.at[i])
            @pl.when(outer)
            def _(): C["PZ1"](i).start()
            @pl.when(inner)
            def _():
                C["Q2"](i).wait()
                add(D.at[i, qn(near)], D.at[i, qn(near)], RQ1.at[i, ds(near*h, h)], RQ2.at[i])
                C["X1"](i).start()
        def S4(i):
            @pl.when(inner)
            def _():
                C["PZ1"](i).wait_recv()
                add(D.at[i, pch(farc)], D.at[i, pch(farc)], RZ1.at[i, ds(farc*E8, E8)])
                C["PZ2"](i).start()
                C["X1"](i).wait()
                add(D.at[i, qhalf(near, f)], D.at[i, qhalf(near, f)], RX1.at[i])
                C["X2"](i).start()
            @pl.when(outer)
            def _(): C["PZ1"](i).wait_send()
        def S5(i):
            @pl.when(inner)
            def _():
                C["PZ2"](i).wait()
                add(R.at[i, pch(near)], D.at[i, pch(near)], RZ1.at[i, ds(near*E8, E8)], RZ2.at[i])
                C["PT1"](i).start(); C["PT2"](i).start()
                C["X2"](i).wait()
                add(R.at[i, qquart(near, f, s)], D.at[i, qquart(near, f, s)], RX2.at[i])
                C["X3"](i).start()
        def S6(i):
            @pl.when(inner)
            def _():
                C["PT1"](i).wait()
                C["PT3"](i).start()
                C["X3"](i).wait()
                C["X4"](i).start()
        def S7(i):
            @pl.when(outer)
            def _():
                C["PT2"](i).wait_recv(); C["PT3"](i).wait_recv()
            @pl.when(inner)
            def _():
                C["PT2"](i).wait_send(); C["PT3"](i).wait_send()
            C["G1"](i).start()
            @pl.when(inner)
            def _():
                C["X4"](i).wait()
                C["QT1"](i).start(); C["QT2"](i).start()
        def S8(i):
            C["G1"](i).wait()
            C["G2"](i).start()
            @pl.when(inner)
            def _():
                C["QT1"](i).wait()
                C["QT3"](i).start()
        def S9(i):
            C["G2"](i).wait()
            @pl.when(outer)
            def _():
                C["QT2"](i).wait_recv(); C["QT3"](i).wait_recv()
            @pl.when(inner)
            def _():
                C["QT2"](i).wait_send(); C["QT3"](i).wait_send()
            m = mine(i)
            @pl.when(m)
            def _(): Fl(i).start()
            @pl.when(jnp.logical_not(m))
            def _(): Fr(i).start()
        def S10(i):
            m = mine(i)
            @pl.when(m)
            def _(): Fl(i).wait()
            @pl.when(jnp.logical_not(m))
            def _(): Fr(i).wait_send()
        stages = [S0,S1,S2,S3,S4,S5,S6,S7,S8,S9,S10]
        def step(t):
            for si in range(len(stages)):
                i = t - si
                @pl.when(jnp.logical_and(i >= 0, i < 2*N))
                def _(): stages[si](i)
        def recv_final():
            def body(j, _):
                i = jnp.where(c == 1, j, j + N)
                Fr(i).wait_recv()
                return 0
            lax.fori_loop(0, N, body, 0)
        def barrier():
            b = pltpu.get_barrier_semaphore()
            for d in (peer, n1, n2, zp):
                pl.semaphore_signal(b, inc=1, device_id=d, device_id_type=MESH)
            @pl.when(inner)
            def _():
                pl.semaphore_signal(b, inc=1, device_id=far, device_id_type=MESH)
                pl.semaphore_wait(b, 5)
            @pl.when(outer)
            def _(): pl.semaphore_wait(b, 4)
        self.R = R
        self.barrier, self.step, self.recv_final, self.iters = barrier, step, recv_final, 2*N + len(stages) - 1


def ar_kernel(ring, one, two, out, cnt, G, gsem, *scr):
    N = ring.N
    c = lax.axis_index("section")
    loads = [pltpu.make_async_copy(two.at[c], G.at[pl.ds(0, N)], gsem.at[0]), pltpu.make_async_copy(one.at[c], G.at[pl.ds(N, N)], gsem.at[1])]
    for cp in loads:
        cp.start()
    ring.bind(G, two, one, out, *scr)
    ring.barrier()
    for cp in loads:
        cp.wait()

    def body(t, _):
        ring.step(t)
        return 0

    lax.fori_loop(0, ring.iters, body, 0)
    ring.recv_final()
    cnt[...] = ring.R[N - 1, pl.ds(ring.U - 12, 12)]


def allreduce(one, two, N, PU, QU):
    ring = Ring(N, PU, QU)
    U = PU + QU
    any_ = pl.BlockSpec(memory_space=pl.ANY)
    split = lambda g: g.reshape(2, N, U, 16, 128)
    return pl.pallas_call(
        functools.partial(ar_kernel, ring),
        out_shape=[jax.ShapeDtypeStruct((2, N, U, 16, 128), BF), jax.ShapeDtypeStruct((12, 16, 128), BF)],
        in_specs=[any_, any_],
        out_specs=[any_, pl.BlockSpec(memory_space=pltpu.VMEM)],
        scratch_shapes=[pltpu.VMEM((2 * N, U, 16, 128), BF), pltpu.SemaphoreType.DMA((2,))] + ring.scratch(),
        compiler_params=pltpu.CompilerParams(collective_id=0, has_side_effects=True, vmem_limit_bytes=60 * 2**20),
    )(split(one), split(two))


def plane(c, z, q):
    out = []
    for i in range(1, 8):
        n = lax.rem(c * 4 + q + i, 8)
        out.append((lax.div(n, 4), z, lax.rem(n, 4)))
    return out


def greet(ids):
    barrier = pltpu.get_barrier_semaphore()
    for d in ids:
        pl.semaphore_signal(barrier, inc=1, device_id=d, device_id_type=MESH)
    pl.semaphore_wait(barrier, len(ids))


def spread_kernel(n, *refs):
    srcs, dsts, ss, rs, ls = refs[:n], refs[n : 2 * n], refs[-3], refs[-2], refs[-1]
    c, z, q = lax.axis_index("section"), lax.axis_index("dp"), lax.axis_index("seq")
    greet(plane(c, z, q))
    from_core = lax.div(q, 2)
    for phase in (0, 1):
        for a in range(n):
            for ml in range(2):
                for h in range(2):
                    local = jnp.logical_and(h == c, 2 * c + ml == q)
                    src, dst = srcs[a].at[ml, :, h], dsts[a].at[q]
                    j = 2 * ml + h
                    far = pltpu.make_async_remote_copy(src_ref=src, dst_ref=dst, send_sem=ss.at[a, j], recv_sem=rs.at[a, q],
                                                       device_id=(h, z, 2 * c + ml), device_id_type=MESH)
                    near = pltpu.make_async_copy(src, dst, ls.at[a])

                    @pl.when(local)
                    def _():
                        near.start() if phase == 0 else near.wait()

                    @pl.when(jnp.logical_not(local))
                    def _():
                        far.start() if phase == 0 else far.wait_send()
            if phase == 1:
                for p in range(4):
                    @pl.when(jnp.logical_not(jnp.logical_and(c == from_core, p == q)))
                    def _():
                        pltpu.make_async_remote_copy(src_ref=srcs[a].at[0, :, 0], dst_ref=dsts[a].at[p], send_sem=ss.at[a, 0],
                                                     recv_sem=rs.at[a, p], device_id=(from_core, z, p), device_id_type=MESH).wait_recv()


def gather_kernel(n, *refs):
    srcs, dsts, ss, rs, ls = refs[:n], refs[n : 2 * n], refs[-3], refs[-2], refs[-1]
    c, z, q = lax.axis_index("section"), lax.axis_index("dp"), lax.axis_index("seq")
    greet(plane(c, z, q))
    to_core, slot = lax.div(q, 2), lax.rem(q, 2)
    for phase in (0, 1):
        for a in range(n):
            for p in range(4):
                local = jnp.logical_and(to_core == c, p == q)
                src, dst = srcs[a].at[p], dsts[a].at[slot, :, c]
                far = pltpu.make_async_remote_copy(src_ref=src, dst_ref=dst, send_sem=ss.at[a, p], recv_sem=rs.at[a, 2 * slot + c],
                                                   device_id=(to_core, z, p), device_id_type=MESH)
                near = pltpu.make_async_copy(src, dst, ls.at[a])

                @pl.when(local)
                def _():
                    near.start() if phase == 0 else near.wait()

                @pl.when(jnp.logical_not(local))
                def _():
                    far.start() if phase == 0 else far.wait_send()
            if phase == 1:
                for ml in range(2):
                    for h in range(2):
                        @pl.when(jnp.logical_not(jnp.logical_and(h == c, 2 * c + ml == q)))
                        def _():
                            pltpu.make_async_remote_copy(src_ref=srcs[a].at[0], dst_ref=dsts[a].at[ml, :, h], send_sem=ss.at[a, 0],
                                                         recv_sem=rs.at[a, 2 * ml + h], device_id=(h, z, 2 * c + ml), device_id_type=MESH).wait_recv()


def exchange(kernel, arrays, shape, cid):
    n = len(arrays)
    any_ = pl.BlockSpec(memory_space=pl.ANY)
    return pl.pallas_call(
        functools.partial(kernel, n),
        out_shape=[jax.ShapeDtypeStruct(shape, BF)] * n,
        in_specs=[any_] * n,
        out_specs=[any_] * n,
        scratch_shapes=[pltpu.SemaphoreType.DMA((n, 4)), pltpu.SemaphoreType.DMA((n, 4)), pltpu.SemaphoreType.DMA((n,))],
        compiler_params=pltpu.CompilerParams(collective_id=cid, has_side_effects=True),
    )(*arrays)


def call(fn, outs, scratch, args, scal_at=(), layer={}):
    vm = pl.BlockSpec(memory_space=pltpu.VMEM)
    whole, place = [], []
    for a in args:
        if not any(a is w for w in whole):
            whole.append(a)
        place.append(next(i for i, w in enumerate(whole) if w is a))
    specs = [pl.BlockSpec(memory_space=pltpu.SMEM) if place.index(i) in scal_at else vm for i in range(len(whole))]

    def kernel(*refs):
        ins = [refs[p].at[pl.ds(layer[i], 1)] if i in layer else refs[p] for i, p in enumerate(place)]
        fn(*ins, *refs[len(whole):])

    return pl.pallas_call(
        kernel,
        out_shape=[jax.ShapeDtypeStruct(s, d) for s, d in outs],
        in_specs=specs,
        out_specs=[vm] * len(outs),
        scratch_shapes=[pltpu.VMEM(s, d) for s, d in scratch],
        compiler_params=pltpu.CompilerParams(vmem_limit_bytes=60 * 2**20),
    )(*whole)


def body(inputs, lengths, mlm_mask, true_types, gain_in, bias_in, gain_mid, bias_mid, w_in, conv_w, w_out, decoder, cotangent, fast):
    c, q = lax.axis_index("section"), lax.axis_index("seq")
    seg, D, H = inputs.shape[2], inputs.shape[3], w_in.shape[2]
    rows = seg + 2 * HALO
    both = lambda w: lax.all_gather(w, "section", axis=0, tiled=True)
    w_in, conv_w, w_out = both(w_in), both(conv_w), both(w_out)
    gi, bi, gm, bm = (both(v.astype(F32)) for v in (gain_in, bias_in, gain_mid, bias_mid))
    mine = lambda v: lax.dynamic_slice_in_dim(v[:, 0], 2 * c, 2, 0)
    x, cot = mine(inputs), mine(cotangent)
    mask, types = mine(mlm_mask)[..., None], mine(true_types)[..., None]
    scal = jnp.concatenate([jnp.reshape(q * seg, (1,)), lax.dynamic_slice_in_dim(lengths[:, 0], 2 * c, 2, 0)]).astype(jnp.int32)
    n = lax.axis_size("seq")
    up = [(i, i + 1) for i in range(n - 1)]
    down = [(j, i) for i, j in up]

    def haloed(v):
        before = lax.ppermute(v[:, seg - HALO :], "seq", up)
        after = lax.ppermute(v[:, :HALO], "seq", down)
        return jnp.concatenate([before, v, after], axis=1)

    g1_, b1_, g2_, b2_ = gi[0:1], bi[0:1], gi[1:2], bi[1:2]
    xe = haloed(x)
    out1, first1, hidden1, sec1, mixed1, third1, first2, hidden2, sec2, dthird2 = call(
        k1,
        [((2, seg, D), BF), ((2, seg, D), BF), ((2, seg, H), F32), ((2, rows + 16, H), F32), ((2, rows, H), F32), ((2, seg, H), BF),
         ((2, seg, D), BF), ((2, seg, H), F32), ((2, seg, H), BF), ((2, seg, H), BF)],
        [((rows, D), BF), ((rows, H), F32), ((seg, H), F32)],
        (xe, cot, scal, w_in, conv_w, w_out, w_in, w_out, g1_, b1_, gm[0], bm[0], g2_, b2_, gm[1], bm[1]),
        (2,), {3: 0, 4: 0, 5: 0, 6: 1, 7: 1})
    split = lambda v: v.reshape(2, 2, 2, 64, H)
    sec_r, dthird_r = exchange(spread_kernel, [split(sec2), split(dthird2)], (4, 2, 64, H), 1)
    line = lambda v: v.reshape(8 * 64, H)
    units = lambda u: ((2, u, 16, 128), BF)
    third_r, dsec_r, dgb2, g_conv = call(
        k2,
        [((512, H), BF), ((512, H), BF), ((2, 8, H), F32), units(500)],
        [((768, H), BF), ((768, H), BF), ((512, H), F32), ((8, H), F32)],
        (line(sec_r), line(dthird_r), conv_w, gm[1], bm[1]), (), {2: 1})
    block = lambda v: v.reshape(4, 2, 64, H)
    third2, dsec2 = exchange(gather_kernel, [block(third_r), block(dsec_r)], (2, 2, 2, 64, H), 2)
    join = lambda v: v.reshape(2, seg, H)
    dec = jnp.pad(decoder, ((0, 0), (0, 128 - decoder.shape[1])))
    out2, grad2, dgbi2, dgbm2, counts, g_rest = call(
        k3,
        [((2, seg, D), BF), ((2, seg, D), BF), ((2, 8, D), F32), ((2, 8, H), F32), ((8, 128), F32), units(400)],
        [((seg, H), F32), ((seg, H), F32), ((2, seg, H), BF)],
        (out1, join(third2), join(dsec2), cot, first2, hidden2, w_in, w_out, dec, g2_, b2_, gm[1], bm[1], scal, mask, types),
        (13,), {6: 1, 7: 1})
    ge = haloed(grad2)
    grad1, dgbi1, dgbm1, g_one = call(
        k4,
        [((2, seg, D), BF), ((2, 8, D), F32), ((4, 8, H), F32), units(900)],
        [((rows, H), F32), ((seg, H), F32), ((rows, H), F32), ((2, seg, H), BF), ((2, seg, H), BF), ((2 * seg, H), BF)],
        (xe, ge, scal, first1, hidden1, sec1, mixed1, third1, w_in, conv_w, w_out, g1_, b1_, gm[0], bm[0]),
        (2,), {8: 0, 9: 0, 10: 0})

    def extra(dgbi, dgbm, cnt):
        flat = jnp.concatenate([dgbi.sum(1).reshape(-1), dgbm.sum(1).reshape(-1), cnt.sum(0)])
        flat = jnp.pad(flat, (0, 12 * 2048 - flat.shape[0])).astype(BF).reshape(1, 12, 16, 128)
        return jnp.concatenate([flat, flat], 0)

    g_two = jnp.concatenate([g_conv, g_rest, extra(dgbi2, jnp.concatenate([dgbm2, dgb2]), counts)], 1)
    g_one = jnp.concatenate([g_one, extra(dgbi1, dgbm1, jnp.zeros_like(counts))], 1)
    if fast:
        N, PU, QU = 6, 88, 64
        total, cnt = allreduce(g_one, g_two, N, PU, QU)
        total = total.reshape(2, UNITS, 16, 128)
    else:
        own, other = jnp.where(c == 0, g_one, g_two), jnp.where(c == 0, g_two, g_one)
        got = lax.ppermute(other, "section", [(0, 1), (1, 0)])
        total = lax.psum(own.astype(F32) + got.astype(F32), ("dp", "seq"))
        cnt = lax.psum(g_two[0, EXTRA0:].astype(F32), ("section", "dp", "seq"))
    total = total.astype(F32)
    s_conv = total[:, :OUT0].reshape(2, 5, 5, H // 2, 128).transpose(1, 0, 3, 2, 4).reshape(1, 5, H, H)
    s_out = total[:, OUT0:IN0].reshape(2, D // 128, H // 2, 128).transpose(0, 2, 1, 3).reshape(1, H, D)
    s_in = total[:, IN0:EXTRA0].reshape(2, H // 128, D // 2, 128).transpose(0, 2, 1, 3).reshape(1, D, H)
    small = total[0, EXTRA0 : EXTRA0 + 3].reshape(-1)
    s_bi = small[: 2 * D].reshape(2, D)
    s_bm = small[2 * D : 2 * D + 4 * H].reshape(2, 2, H)
    s_cnt = cnt[:3].astype(F32).reshape(-1)[2 * D + 4 * H : 2 * D + 4 * H + decoder.shape[1]]

    def placed(one, two):
        own, other = jnp.where(c == 0, one, two), jnp.where(c == 0, two, one)
        got = lax.ppermute(other, "section", [(0, 1), (1, 0)])
        return jnp.where(c == 0, jnp.concatenate([own, got]), jnp.concatenate([got, own]))[None, :, None]

    return (placed(out1, out2), placed(grad1, grad2), s_bi[0:1], s_bi[1:2], s_bm[None, :, 0], s_bm[None, :, 1],
            s_in, s_conv, s_out, s_cnt)


def solution(mesh):
    fast = mesh.shape["dp"] == 4 and mesh.shape["seq"] == 4
    return jax.shard_map(
        functools.partial(body, fast=fast),
        mesh=mesh,
        in_specs=(P(None, "dp", "seq", None), P(None, "dp"), P(None, "dp", "seq"), P(None, "dp", "seq"), P("section", None),
                  P("section", None), P("section", None, None), P("section", None, None), P("section", None, None),
                  P("section", None, None, None), P("section", None, None), P(), P(None, "dp", "seq", None)),
        out_specs=(P("section", None, "dp", "seq", None), P("section", None, "dp", "seq", None), P("section", None), P("section", None),
                   P("section", None, None), P("section", None, None), P("section", None, None), P("section", None, None, None),
                   P("section", None, None), P()),
        check_vma=False,
    )
```

```python
import functools

import jax
import jax.numpy as jnp
from jax import lax
from jax.experimental import pallas as pl
from jax.experimental.pallas import tpu as pltpu
from jax.sharding import PartitionSpec as P

EPS = 1e-05
BF, F32 = jnp.bfloat16, jnp.float32
MESH = pl.DeviceIdType.MESH
G0 = 0.7978845608028654
G1 = 0.044715
DIL = 2
HALO = 16
CH = 16


def dot(a, b):
    return lax.dot_general(a, b, (((1,), (0,)), ((), ())), preferred_element_type=F32)


def dot_nt(a, b):
    return lax.dot_general(a, b, (((1,), (1,)), ((), ())), preferred_element_type=F32)


def dot_tn(a, b):
    return lax.dot_general(a, b, (((0,), (0,)), ((), ())), preferred_element_type=F32)


def chunks(rows, fn, size=None):
    size = size or (96 if rows % 96 == 0 else 64)

    def one(i, _):
        fn(pl.multiple_of(i * size, size), size)
        return 0

    lax.fori_loop(0, rows // size, one, 0)


def cols(j):
    return pl.ds(j * 128, 128)


def stats(load, n):
    total = load(0)
    for j in range(1, n):
        total = total + load(j)
    mean = jnp.sum(total, axis=-1, keepdims=True) * (1.0 / (128 * n))
    square = None
    for j in range(n):
        d = load(j) - mean
        square = d * d if square is None else square + d * d
    var = jnp.sum(square, axis=-1, keepdims=True) * (1.0 / (128 * n))
    return mean, lax.rsqrt(var + EPS)


def norm_gelu(load, n, gain, shift, store):
    mean, rstd = stats(load, n)
    for j in range(n):
        u = (load(j) - mean) * rstd * gain(j) + shift(j)
        t = jnp.tanh(u * (G0 + (G0 * G1) * (u * u)))
        h = 0.5 * u
        store(j, h + h * t)


def fold(v):
    rows, width = v.shape
    return jnp.sum(v.reshape(rows // 8, 8, width), axis=0)


def norm_gelu_back(load, dy, n, gain, shift, dgain, dshift, hold, store):
    mean, rstd = stats(load, n)
    s1 = s2 = None
    for j in range(n):
        g = gain(j)
        hat = (load(j) - mean) * rstd
        u = hat * g + shift(j)
        w = u * u
        t = jnp.tanh(u * (G0 + (G0 * G1) * w))
        slope = 0.5 + 0.5 * t + u * (1.0 - t * t) * (0.5 * G0 + (1.5 * G0 * G1) * w)
        du = dy(j) * slope
        if dgain is not None:
            dgain[:, cols(j)] += fold(du * hat)
            dshift[:, cols(j)] += fold(du)
        dh = du * g
        hold[0, :, cols(j)] = hat
        hold[1, :, cols(j)] = dh
        p = dh * hat
        s1 = dh if s1 is None else s1 + dh
        s2 = p if s2 is None else s2 + p
    m1 = jnp.sum(s1, axis=-1, keepdims=True) * (1.0 / (128 * n))
    m2 = jnp.sum(s2, axis=-1, keepdims=True) * (1.0 / (128 * n))
    for j in range(n):
        store(j, rstd * (hold[1, :, cols(j)] - m1 - hold[0, :, cols(j)] * m2))


def row(ref, k):
    return lambda j: ref[pl.ds(k, 1), cols(j)]


def view(ref, *at):
    return lambda j: ref[(*at, cols(j))].astype(F32)


def put_grad(g_ref, unit, value, col0=0):
    m, n = value.shape
    per = m // 32
    value = value.astype(BF)
    for j in range(n // 128):
        block = value[:, j * 128 : (j + 1) * 128].reshape(m // 16, 16, 128)
        for h in range(2):
            g_ref[h, pl.ds(unit + (col0 + j) * per, per)] = block[h * per : (h + 1) * per]


OUT0, IN0, CONV0, EXTRA0, UNITS = 0, 200, 400, 900, 912


def put(ref, *at):
    def store(j, v):
        ref[(*at, cols(j))] = v.astype(ref.dtype)

    return store


def positions(first, i, size):
    return first + i + lax.broadcasted_iota(jnp.int32, (size, 1), 0)


def k4(xe, ge, scal, first1, hidden1, sec1, mixed1, third1, w_in1, conv1, w_out1, gi1, bi1, gm1, bm1,
       grad1, dgbi, dgbm, g_ref, he, me, dme, dh, dm, swin, hold):
    base = scal[0]
    rows, D = xe.shape[1:]
    seg, H = grad1.shape[1], hidden1.shape[2]
    nd, nh = D // 128, H // 128
    for ref in (dgbi, dgbm):
        ref[...] = jnp.zeros_like(ref)

    def micro(m, _):
        length = scal[1 + m]
        he[...] = dot_nt(ge[m], w_out1[0])

        def a(i, size):
            r = pl.ds(i + HALO, size)

            def store(j, v):
                v = v.astype(BF)
                dme[r, cols(j)] = v.astype(F32)
                dm[m, pl.ds(i, size), cols(j)] = v

            norm_gelu_back(view(mixed1, m, r), view(he, r), nh, row(gm1, 1), row(bm1, 1), dgbm.at[2], dgbm.at[3], hold, store)

        chunks(seg, a)
        for edge in (0, rows - HALO):
            r = pl.ds(edge, HALO)
            pos = positions(base - HALO, edge, HALO)
            inside = jnp.logical_and(pos >= 0, pos < 1024)

            def store(j, v):
                dme[r, cols(j)] = jnp.where(inside, v, 0.0).astype(BF).astype(F32)

            norm_gelu_back(view(mixed1, m, r), view(he, r), nh, row(gm1, 1), row(bm1, 1), None, None, hold.at[:, pl.ds(0, HALO)], store)
        acc = None
        for k in range(5):
            term = dot_nt(dme[pl.ds(HALO - DIL * (k - 2), seg)].astype(BF), conv1[0, k])
            acc = term if acc is None else acc + term
        he[pl.ds(0, seg)] = acc

        def b(i, size):
            r = pl.ds(i, size)
            pos = positions(base, i, size)
            ds = lambda j: jnp.where(pos < length, he[r, cols(j)], 0.0)
            norm_gelu_back(view(hidden1, m, r), ds, nh, row(gm1, 0), row(bm1, 0), dgbm.at[0], dgbm.at[1], hold, put(dh, m, r))

        chunks(seg, b)
        he[pl.ds(0, seg)] = dot_nt(dh[m], w_in1[0, :H])
        me[...] = dot_nt(dh[m], w_in1[0, H:])

        def c(i, size):
            r, e = pl.ds(i, size), pl.ds(i + HALO, size)
            df = lambda j: he[r, cols(j)] if j < nh else me[r, cols(j - nh)]

            def store(j, v):
                grad1[m, r, cols(j)] = (ge[m, e, cols(j)].astype(F32) + v).astype(BF)

            norm_gelu_back(view(xe, m, e), df, nd, row(gi1, 0), row(bi1, 0), dgbi.at[0], dgbi.at[1], hold, store)

        chunks(seg, c)
        return 0

    lax.fori_loop(0, 2, micro, 0)
    flat = lambda v: v.reshape(2 * seg, v.shape[-1])
    t1 = flat(third1[...])
    for j in range(2):
        g1 = flat(ge[:, pl.ds(HALO, seg), pl.ds(j * H, H)])
        put_grad(g_ref, OUT0, dot_tn(t1, g1), nh * j)
    d1 = flat(dm[...])
    for k in range(5):
        for m in range(2):
            swin[pl.ds(m * seg, seg)] = sec1[m, pl.ds(8 + HALO + DIL * (k - 2), seg)].astype(BF)
        put_grad(g_ref, CONV0 + k * 100, dot_tn(swin[...], d1))
    put_grad(g_ref, IN0, dot_tn(flat(first1[...]), flat(dh[...])))


class Ring:
    def __init__(self, N, PU, QU):
        self.N, self.PU, self.QU, self.U = N, PU, QU, PU + QU
        self.kinds = ["D","P1","P2","PZ1","PZ2","PT1","PT2","PT3","G1","G2","Q1","Q2","X1","X2","X3","X4","QT1","QT2","QT3","F"]
    def scratch(self):
        N2, PU, QU, U = 2*self.N, self.PU, self.QU, self.U
        b = lambda u: pltpu.VMEM((N2, u, 16, 128), BF)
        nk = len(self.kinds)
        return [b(U), b(PU//2), b(PU//4), b(PU//4), b(PU//8), b(QU), b(QU//2), b(QU//4), b(QU//8), b(U),
                pltpu.SemaphoreType.DMA((nk, N2)), pltpu.SemaphoreType.DMA((nk, N2))]
    def bind(self, G, two, one, out, D, RP1, RP2, RZ1, RZ2, RQ1, RQ2, RX1, RX2, R, ss, rs):
        N, PU, QU, U = self.N, self.PU, self.QU, self.U
        c, z, q = lax.axis_index("section"), lax.axis_index("dp"), lax.axis_index("seq")
        xb, yb = lax.rem(q, 2), lax.div(q, 2)
        f = jnp.where(c == 0, xb, yb); s = jnp.where(c == 0, yb, xb)
        qx = xb ^ 1;
        nx = (c, z, yb*2 + 1 - xb); ny = (c, z, (1-yb)*2 + xb)
        n1 = (c, z, jnp.where(c == 0, nx[2], ny[2])); n2 = (c, z, jnp.where(c == 0, ny[2], nx[2]))
        side = lax.div(z, 2)
        zp = (c, side*2 + 1 - lax.rem(z, 2), q)
        far = (c, 3 - z, q)
        peer = (1 - c, z, q)
        inner = jnp.logical_or(z == 1, z == 2)
        outer = jnp.logical_not(inner)
        K = {k: i for i, k in enumerate(self.kinds)}
        def cp(k, i, src, dst, dev):
            return pltpu.make_async_remote_copy(src_ref=src, dst_ref=dst, send_sem=ss.at[K[k], i], recv_sem=rs.at[K[k], i], device_id=dev, device_id_type=MESH)
        ds = pl.ds
        H, Q4, E8 = PU//2, PU//4, PU//8
        h, q4, e8 = QU//2, QU//8, QU//8
        def add(dst, a, *bs):
            acc = a[...].astype(F32)
            for b in bs: acc = acc + b[...].astype(F32)
            dst[...] = acc.astype(BF)
        pq = lambda ff, s2: ds((2*ff + s2)*Q4, Q4)
        pch = lambda k: ds((2*f + s)*Q4 + k*E8, E8)
        def qn(k): return ds(PU + k*h, h)
        def qhalf(k, ff): return ds(PU + k*h + ff*(h//2), h//2)
        def qquart(k, ff, s2): return ds(PU + k*h + (2*ff+s2)*(h//4), h//4)
        near, farc = side, 1 - side
        C = dict(
          D=lambda i: cp("D", i, two.at[1-c, i], D.at[i], peer),
          E=lambda i: cp("D", i, one.at[1-c, i-N], D.at[i], peer),
          W=lambda i: cp("D", i, G.at[i], D.at[i], peer),
          P1=lambda i: cp("P1", i, D.at[i, ds((1-f)*H, H)], RP1.at[i], n1),
          P2=lambda i: cp("P2", i, D.at[i, pq(f, 1-s)], RP2.at[i], n2),
          PZ1=lambda i: cp("PZ1", i, D.at[i, pq(f, s)], RZ1.at[i], zp),
          PZ2=lambda i: cp("PZ2", i, D.at[i, pch(farc)], RZ2.at[i], far),
          PT1=lambda i: cp("PT1", i, R.at[i, pch(near)], R.at[i, pch(near)], far),
          PT2=lambda i: cp("PT2", i, R.at[i, pch(near)], R.at[i, pch(near)], zp),
          PT3=lambda i: cp("PT3", i, R.at[i, pch(farc)], R.at[i, pch(farc)], zp),
          G1=lambda i: cp("G1", i, R.at[i, pq(f, s)], R.at[i, pq(f, s)], n2),
          G2=lambda i: cp("G2", i, R.at[i, ds(f*H, H)], R.at[i, ds(f*H, H)], n1),
          Q1=lambda i: cp("Q1", i, D.at[i, ds(PU, QU)], RQ1.at[i], zp),
          Q2=lambda i: cp("Q2", i, D.at[i, qn(farc)], RQ2.at[i], far),
          X1=lambda i: cp("X1", i, D.at[i, qhalf(near, 1-f)], RX1.at[i], n1),
          X2=lambda i: cp("X2", i, D.at[i, qquart(near, f, 1-s)], RX2.at[i], n2),
          X3=lambda i: cp("X3", i, R.at[i, qquart(near, f, s)], R.at[i, qquart(near, f, s)], n2),
          X4=lambda i: cp("X4", i, R.at[i, qhalf(near, f)], R.at[i, qhalf(near, f)], n1),
          QT1=lambda i: cp("QT1", i, R.at[i, qn(near)], R.at[i, qn(near)], far),
          QT2=lambda i: cp("QT2", i, R.at[i, qn(near)], R.at[i, qn(near)], zp),
          QT3=lambda i: cp("QT3", i, R.at[i, qn(farc)], R.at[i, qn(farc)], zp),
        )
        def mine(i): return jnp.where(i < N, 1, 0) == c
        def slot(i): return jnp.where(i < N, i, i - N)
        Fr = lambda i: cp("F", i, R.at[i], out.at[c, slot(i)], peer)
        Fl = lambda i: pltpu.make_async_copy(R.at[i], out.at[c, slot(i)], ss.at[K["F"], i])
        def S0(i):
            @pl.when(i < N)
            def _(): C["D"](i).start()
            @pl.when(i >= N)
            def _(): C["E"](i).start()
        def S1(i):
            C["W"](i).wait()
            add(D.at[i], D.at[i], G.at[i])
            C["P1"](i).start()
            @pl.when(outer)
            def _(): C["Q1"](i).start()
        def S2(i):
            @pl.when(inner)
            def _():
                C["Q1"](i).wait_recv()
                add(D.at[i, qn(farc)], D.at[i, qn(farc)], RQ1.at[i, ds(farc*h, h)])
                C["Q2"](i).start()
            C["P1"](i).wait()
            add(D.at[i, ds(f*H, H)], D.at[i, ds(f*H, H)], RP1.at[i])
            C["P2"](i).start()
            @pl.when(outer)
            def _(): C["Q1"](i).wait_send()
        def S3(i):
            C["P2"](i).wait()
            add(D.at[i, pq(f, s)], D.at[i, pq(f, s)], RP2.at[i])
            @pl.when(outer)
            def _(): C["PZ1"](i).start()
            @pl.when(inner)
            def _():
                C["Q2"](i).wait()
                add(D.at[i, qn(near)], D.at[i, qn(near)], RQ1.at[i, ds(near*h, h)], RQ2.at[i])
                C["X1"](i).start()
        def S4(i):
            @pl.when(inner)
            def _():
                C["PZ1"](i).wait_recv()
                add(D.at[i, pch(farc)], D.at[i, pch(farc)], RZ1.at[i, ds(farc*E8, E8)])
                C["PZ2"](i).start()
                C["X1"](i).wait()
                add(D.at[i, qhalf(near, f)], D.at[i, qhalf(near, f)], RX1.at[i])
                C["X2"](i).start()
            @pl.when(outer)
            def _(): C["PZ1"](i).wait_send()
        def S5(i):
            @pl.when(inner)
            def _():
                C["PZ2"](i).wait()
                add(R.at[i, pch(near)], D.at[i, pch(near)], RZ1.at[i, ds(near*E8, E8)], RZ2.at[i])
                C["PT1"](i).start(); C["PT2"](i).start()
                C["X2"](i).wait()
                add(R.at[i, qquart(near, f, s)], D.at[i, qquart(near, f, s)], RX2.at[i])
                C["X3"](i).start()
        def S6(i):
            @pl.when(inner)
            def _():
                C["PT1"](i).wait()
                C["PT3"](i).start()
                C["X3"](i).wait()
                C["X4"](i).start()
        def S7(i):
            @pl.when(outer)
            def _():
                C["PT2"](i).wait_recv(); C["PT3"](i).wait_recv()
            @pl.when(inner)
            def _():
                C["PT2"](i).wait_send(); C["PT3"](i).wait_send()
            C["G1"](i).start()
            @pl.when(inner)
            def _():
                C["X4"](i).wait()
                C["QT1"](i).start(); C["QT2"](i).start()
        def S8(i):
            C["G1"](i).wait()
            C["G2"](i).start()
            @pl.when(inner)
            def _():
                C["QT1"](i).wait()
                C["QT3"](i).start()
        def S9(i):
            C["G2"](i).wait()
            @pl.when(outer)
            def _():
                C["QT2"](i).wait_recv(); C["QT3"](i).wait_recv()
            @pl.when(inner)
            def _():
                C["QT2"](i).wait_send(); C["QT3"](i).wait_send()
            m = mine(i)
            @pl.when(m)
            def _(): Fl(i).start()
            @pl.when(jnp.logical_not(m))
            def _(): Fr(i).start()
        def S10(i):
            m = mine(i)
            @pl.when(m)
            def _(): Fl(i).wait()
            @pl.when(jnp.logical_not(m))
            def _(): Fr(i).wait_send()
        stages = [S0,S1,S2,S3,S4,S5,S6,S7,S8,S9,S10]
        def step(t):
            for si in range(len(stages)):
                i = t - si
                @pl.when(jnp.logical_and(i >= 0, i < 2*N))
                def _(): stages[si](i)
        def recv_final():
            def body(j, _):
                i = jnp.where(c == 1, j, j + N)
                Fr(i).wait_recv()
                return 0
            lax.fori_loop(0, N, body, 0)
        def barrier():
            b = pltpu.get_barrier_semaphore()
            for d in (peer, n1, n2, zp):
                pl.semaphore_signal(b, inc=1, device_id=d, device_id_type=MESH)
            @pl.when(inner)
            def _():
                pl.semaphore_signal(b, inc=1, device_id=far, device_id_type=MESH)
                pl.semaphore_wait(b, 5)
            @pl.when(outer)
            def _(): pl.semaphore_wait(b, 4)
        self.R = R
        self.barrier, self.step, self.recv_final, self.iters = barrier, step, recv_final, 2*N + len(stages) - 1


def ar_kernel(ring, one, two, out, cnt, G, gsem, *scr):
    N = ring.N
    c = lax.axis_index("section")
    loads = [pltpu.make_async_copy(two.at[c], G.at[pl.ds(0, N)], gsem.at[0]), pltpu.make_async_copy(one.at[c], G.at[pl.ds(N, N)], gsem.at[1])]
    for cp in loads:
        cp.start()
    ring.bind(G, two, one, out, *scr)
    ring.barrier()
    for cp in loads:
        cp.wait()

    def body(t, _):
        ring.step(t)
        return 0

    lax.fori_loop(0, ring.iters, body, 0)
    ring.recv_final()
    cnt[...] = ring.R[N - 1, pl.ds(ring.U - 12, 12)]


def allreduce(one, two, N, PU, QU):
    ring = Ring(N, PU, QU)
    U = PU + QU
    any_ = pl.BlockSpec(memory_space=pl.ANY)
    split = lambda g: g.reshape(2, N, U, 16, 128)
    return pl.pallas_call(
        functools.partial(ar_kernel, ring),
        out_shape=[jax.ShapeDtypeStruct((2, N, U, 16, 128), BF), jax.ShapeDtypeStruct((12, 16, 128), BF)],
        in_specs=[any_, any_],
        out_specs=[any_, pl.BlockSpec(memory_space=pltpu.VMEM)],
        scratch_shapes=[pltpu.VMEM((2 * N, U, 16, 128), BF), pltpu.SemaphoreType.DMA((2,))] + ring.scratch(),
        compiler_params=pltpu.CompilerParams(collective_id=0, has_side_effects=True, vmem_limit_bytes=60 * 2**20),
    )(split(one), split(two))


def plane(c, z, q):
    out = []
    for i in range(1, 8):
        n = lax.rem(c * 4 + q + i, 8)
        out.append((lax.div(n, 4), z, lax.rem(n, 4)))
    return out


def greet(ids):
    barrier = pltpu.get_barrier_semaphore()
    for d in ids:
        pl.semaphore_signal(barrier, inc=1, device_id=d, device_id_type=MESH)
    pl.semaphore_wait(barrier, len(ids))


def remote(src, dst, ss, rs, dev):
    return pltpu.make_async_remote_copy(src_ref=src, dst_ref=dst, send_sem=ss, recv_sem=rs, device_id=dev, device_id_type=MESH)


def both_ways(cond, here, there):
    @pl.when(cond)
    def _():
        here()

    @pl.when(jnp.logical_not(cond))
    def _():
        there()


class Spread:
    def __init__(self, c, z, q, ss, rs, ls):
        self.c, self.z, self.q, self.ss, self.rs, self.ls = c, z, q, ss, rs, ls

    def go(self, a, src, dst, m, start):
        c, z, q = self.c, self.z, self.q
        for h in range(2):
            s, d, j = src.at[m, :, h], dst(q), 2 * m + h
            far = remote(s, d, self.ss.at[a, j], self.rs.at[a, q], (jnp.int32(h), z, 2 * c + m))
            near = pltpu.make_async_copy(s, d, self.ls.at[a])
            both_ways(jnp.logical_and(h == c, 2 * c + m == q), near.start if start else near.wait, far.start if start else far.wait_send)

    def arrive(self, a, src, dst):
        c, z, q = self.c, self.z, self.q
        fc = lax.div(q, 2)
        for p in range(4):
            @pl.when(jnp.logical_not(jnp.logical_and(c == fc, p == q)))
            def _():
                remote(src.at[0, :, 0], dst(p), self.ss.at[a, 0], self.rs.at[a, p], (fc, z, jnp.int32(p))).wait_recv()

    def back(self, a, src, dst, p, start):
        c, z, q = self.c, self.z, self.q
        tc, slot = lax.div(q, 2), lax.rem(q, 2)
        s, d = src.at[pl.ds(2 * p, 2)], dst.at[slot, :, c]
        far = remote(s, d, self.ss.at[a, p], self.rs.at[a, 2 * slot + c], (tc, z, jnp.int32(p)))
        near = pltpu.make_async_copy(s, d, self.ls.at[a])
        both_ways(jnp.logical_and(tc == c, p == q), near.start if start else near.wait, far.start if start else far.wait_send)

    def back_arrive(self, a, src, dst, m):
        c, z, q = self.c, self.z, self.q
        for h in range(2):
            @pl.when(jnp.logical_not(jnp.logical_and(h == c, 2 * c + m == q)))
            def _():
                remote(src.at[pl.ds(0, 2)], dst.at[m, :, h], self.ss.at[a, 0], self.rs.at[a, 2 * m + h], (jnp.int32(h), z, 2 * c + m)).wait_recv()


def edges(ref, m, seg, ss, rs, z, q, c):
    before = remote(ref.at[m, pl.ds(HALO, HALO)], ref.at[m, pl.ds(HALO + seg, HALO)], ss.at[0, m], rs.at[0, m], (c, z, q - 1))
    after = remote(ref.at[m, pl.ds(seg, HALO)], ref.at[m, pl.ds(0, HALO)], ss.at[1, m], rs.at[1, m], (c, z, q + 1))
    return ((q > 0, q < 3, before), (q < 3, q > 0, after))


def front(lengths, inputs, cot_all, params, w_in, conv_w, w_out, dec, mask, types,
          act, xe_o, ge_o, first1_o, hidden1_o, sec1_o, mixed1_o, third1_o, w_in1_o, conv1_o, w_out1_o, g_o, dgbi, dgbm, dgb, counts,
          WI, WC, WO, PR, xe, cot, out1, first1, hidden1, sec1, mixed1, third1, first2, hidden2, sec2, dth2, sp, dthr, thirdr, dpad, dsecr,
          third2, dsec2, out2, ge, G, fe, he, me, mx, dh, hold,
          ws, wr, wl, xs, xr, xl, ss, rs, ls, gs, gr, os_, acs, acr):
    c, z, q = lax.axis_index("section"), lax.axis_index("dp"), lax.axis_index("seq")
    peer = (1 - c, z, q)
    seg, D = cot.shape[1:]
    H = mixed1.shape[2]
    nd, nh = D // 128, H // 128
    rows = seg + 2 * HALO
    base = q * seg
    own = [pltpu.make_async_copy(inputs.at[2 * c + m, 0], xe.at[m, pl.ds(HALO, seg)], xl.at[m]) for m in range(2)]
    own += [pltpu.make_async_copy(cot_all.at[2 * c + m, 0], cot.at[m], xl.at[2 + m]) for m in range(2)]
    mats = [(params, PR.at[c]), (w_in.at[0], WI.at[c])] + [(conv_w.at[0, k], WC.at[c, k]) for k in range(5)] + [(w_out.at[0], WO.at[c])]
    loads = [pltpu.make_async_copy(s, d, wl.at[i]) for i, (s, d) in enumerate(mats)]
    for cp in own[:2] + loads + own[2:]:
        cp.start()
    greet(plane(c, z, q))
    sends = [remote(s, d, ws.at[i], wr.at[i], peer) for i, (s, d) in enumerate(mats)]
    halos = []
    for m in range(2):
        x = inputs.at[2 * c + m, 0]
        halos.append((q > 0, q < 3, remote(x.at[pl.ds(0, HALO)], xe.at[m, pl.ds(HALO + seg, HALO)], xs.at[0, m], xr.at[0, m], (c, z, q - 1))))
        halos.append((q < 3, q > 0, remote(x.at[pl.ds(seg - HALO, HALO)], xe.at[m, pl.ds(0, HALO)], xs.at[1, m], xr.at[1, m], (c, z, q + 1))))
    for cond, _, cp in halos:
        pl.when(cond)(cp.start)
    for cp in sends:
        cp.start()

    @pl.when(q == 0)
    def _():
        xe[:, pl.ds(0, HALO)] = jnp.zeros((2, HALO, D), BF)
        ge[:, pl.ds(0, HALO)] = jnp.zeros((2, HALO, D), BF)

    @pl.when(q == 3)
    def _():
        xe[:, pl.ds(HALO + seg, HALO)] = jnp.zeros((2, HALO, D), BF)
        ge[:, pl.ds(HALO + seg, HALO)] = jnp.zeros((2, HALO, D), BF)

    def have(i):
        loads[i].wait()
        sends[i].wait_recv()

    for ref in (dgbi, dgbm, dgb, counts):
        ref[...] = jnp.zeros_like(ref)
    zero = jnp.zeros((2, 64, H), BF)
    for ref in (sp, dpad):
        ref[pl.ds(0, 2)] = zero
        ref[pl.ds(10, 2)] = zero
    sec1[:, pl.ds(0, 8)] = jnp.zeros((2, 8, H), F32)
    sec1[:, pl.ds(rows + 8, 8)] = jnp.zeros((2, 8, H), F32)
    spread = Spread(c, z, q, ss, rs, ls)
    sp_at = lambda p: sp.at[pl.ds(2 + 2 * p, 2)]
    dthr_at = lambda p: dthr.at[pl.ds(2 * p, 2)]
    gi, bi = lambda l: row(PR.at[l], 0), lambda l: row(PR.at[l], 1)
    gm = lambda l, k: (lambda j: PR[l, pl.ds(2, 1), cols(k * nh + j)])
    bm = lambda l, k: (lambda j: PR[l, pl.ds(3, 1), cols(k * nh + j)])
    out_sem = [0]

    def out_copy(src, dst):
        cp = pltpu.make_async_copy(src, dst, os_.at[out_sem[0]])
        out_sem[0] += 1
        return cp

    have(0)
    for m in range(2):
        own[m].wait()
    for _, cond, cp in halos:
        pl.when(cond)(cp.wait_recv)
    have(1)

    def forward(m, _):
        length = lengths[2 * c + m]

        def a(i, size):
            r = pl.ds(i, size)
            norm_gelu(view(xe, m, r), nd, gi(0), bi(0), put(fe, r))

        chunks(rows, a)
        first1[m] = fe[pl.ds(HALO, seg)]
        he[...] = dot(fe[...], WI[0])
        hidden1[m] = he[pl.ds(HALO, seg)]

        def b(i, size):
            pos = positions(base - HALO, i, size)
            keep = jnp.logical_and(pos >= 0, pos < length)

            def store(j, v):
                sec1[m, pl.ds(i + 8, size), cols(j)] = jnp.where(keep, v, 0.0).astype(BF).astype(F32)

            norm_gelu(view(he, pl.ds(i, size)), nh, gm(0, 0), bm(0, 0), store)

        chunks(rows, b)

        @pl.when(m == 0)
        def _():
            for k in range(5):
                have(2 + k)

        acc = None
        for k in range(5):
            term = dot(sec1[m, pl.ds(8 + DIL * (k - 2), rows)].astype(BF), WC[0, k])
            acc = term if acc is None else acc + term
        mixed1[m] = acc

        def e(i, size):
            norm_gelu(view(mixed1, m, pl.ds(i + HALO, size)), nh, gm(0, 1), bm(0, 1), put(third1, m, pl.ds(i, size)))

        chunks(seg, e)

        @pl.when(m == 0)
        def _():
            have(7)

        he[pl.ds(0, seg)] = dot(third1[m], WO[0, :, :H])
        me[...] = dot(third1[m], WO[0, :, H:])

        def d(i, size):
            r = pl.ds(i, size)
            for j in range(nd):
                br = he[r, cols(j)] if j < nh else me[r, cols(j - nh)]
                out1[m, r, cols(j)] = (xe[m, pl.ds(i + HALO, size), cols(j)].astype(F32) + br).astype(BF)
            norm_gelu(view(out1, m, r), nd, gi(1), bi(1), put(first2, m, r))

        chunks(seg, d)
        hidden2[m] = dot(first2[m], WI[1])

        def f(jj, _):
            i = pl.multiple_of(jj * 64, 64)
            pos = positions(base, i, 64)

            def store(j, v):
                sec2[m, lax.div(jj, 2), lax.rem(jj, 2), :, cols(j)] = jnp.where(pos < length, v, 0.0).astype(BF)

            norm_gelu(view(hidden2, m, pl.ds(i, 64)), nh, gm(1, 0), bm(1, 0), store)
            return 0

        lax.fori_loop(0, seg // 64, f, 0)
        spread.go(0, sec2, sp_at, m, True)
        return 0

    lax.fori_loop(0, 2, forward, 0)
    for m in range(2):
        own[2 + m].wait()

    def third_grad(m, _):
        dth2[m] = dot_nt(cot[m], WO[1]).astype(BF).reshape(2, 2, 64, H)
        spread.go(1, dth2, dthr_at, m, True)
        return 0

    lax.fori_loop(0, 2, third_grad, 0)
    saves = [out_copy(s, d) for s, d in ((xe, xe_o), (first1, first1_o), (hidden1, hidden1_o), (sec1, sec1_o), (mixed1, mixed1_o),
                                         (third1, third1_o), (WI.at[0], w_in1_o), (WC.at[0], conv1_o), (WO.at[0], w_out1_o))]
    for cp in saves:
        cp.start()

    def place(i, src, layer):
        here = out_copy(src, act.at[pl.ds(2 * c, 2)])
        there = remote(src, act.at[pl.ds(2 * c, 2)], acs.at[i], acr.at[0], peer)
        both_ways(c == layer, here.start, there.start)
        return lambda: both_ways(c == layer, here.wait, there.wait_send)

    done1 = place(0, out1, 0)
    for m in range(2):
        spread.go(0, sec2, sp_at, m, False)
    spread.arrive(0, sec2, sp_at)

    def conv(r, _):
        acc = None
        for k in range(5):
            term = dot(sp[pl.ds(4 * r + k, 4)].reshape(256, H), WC[1, k])
            acc = term if acc is None else acc + term
        mx[pl.ds(4 * r, 4)] = acc.reshape(4, 64, H)
        return 0

    lax.fori_loop(0, 2, conv, 0)
    for m in range(2):
        spread.go(1, dth2, dthr_at, m, False)
    spread.arrive(1, dth2, dthr_at)

    def mid(i, _):
        every = pl.ds(0, 64)
        norm_gelu(view(mx, i, every), nh, gm(1, 1), bm(1, 1), put(thirdr, i, every))
        norm_gelu_back(view(mx, i, every), view(dthr, i, every), nh, gm(1, 1), bm(1, 1), dgb.at[0], dgb.at[1], hold, put(dpad, i + 2, every))
        return 0

    lax.fori_loop(0, 8, mid, 0)
    for p in range(4):
        spread.back(2, thirdr, third2, p, True)

    def conv_back(r, _):
        acc = None
        for k in range(5):
            term = dot_nt(dpad[pl.ds(4 * r + 4 - k, 4)].reshape(256, H), WC[1, k])
            acc = term if acc is None else acc + term
        dsecr[pl.ds(4 * r, 4)] = acc.astype(BF).reshape(4, 64, H)
        return 0

    lax.fori_loop(0, 2, conv_back, 0)
    for p in range(4):
        spread.back(3, dsecr, dsec2, p, True)
    dm = dpad[pl.ds(2, 8)].reshape(512, H)

    def conv_grads(k, _):
        put_grad(G, CONV0 + k * 100, dot_tn(sp[pl.ds(k, 8)].reshape(512, H), dm))
        return 0

    lax.fori_loop(0, 5, conv_grads, 0)
    g_conv = out_copy(G.at[:, pl.ds(CONV0, 500)], g_o.at[:, pl.ds(CONV0, 500)])
    g_conv.start()
    for p in range(4):
        spread.back(2, thirdr, third2, p, False)
        spread.back(3, dsecr, dsec2, p, False)
    for m in range(2):
        spread.back_arrive(2, thirdr, third2, m)
        spread.back_arrive(3, dsecr, dsec2, m)
    labels = lax.broadcasted_iota(jnp.int32, (1, 128), 1)

    def backward(m, _):
        length = lengths[2 * c + m]
        t = third2[m].reshape(seg, H)
        he[pl.ds(0, seg)] = dot(t, WO[1, :, :H])
        me[...] = dot(t, WO[1, :, H:])

        def a(i, size):
            r = pl.ds(i, size)
            for j in range(nd):
                br = he[r, cols(j)] if j < nh else me[r, cols(j - nh)]
                out2[m, r, cols(j)] = (out1[m, r, cols(j)].astype(F32) + br).astype(BF)

        chunks(seg, a)
        logits = jnp.where(labels < 30, dot(out2[m], dec[...]), -1e30)
        ex = jnp.exp(logits - jnp.max(logits, axis=-1, keepdims=True))
        probs = ex / jnp.sum(ex, axis=-1, keepdims=True)
        weight = jnp.where(positions(base, 0, seg) < length, mask[2 * c + m].astype(F32), 0.0)
        counts[...] += fold(jnp.where(types[2 * c + m] == labels, probs * weight, 0.0))

        def b(jj, _):
            r = pl.ds(pl.multiple_of(jj * 64, 64), 64)
            pos = positions(base, jj * 64, 64)
            u, h = lax.div(jj, 2), lax.rem(jj, 2)
            ds = lambda j: jnp.where(pos < length, dsec2[m, u, h, :, cols(j)].astype(F32), 0.0)
            norm_gelu_back(view(hidden2, m, r), ds, nh, gm(1, 0), bm(1, 0), dgbm.at[0], dgbm.at[1], hold, put(dh, m, r))
            return 0

        lax.fori_loop(0, seg // 64, b, 0)
        he[pl.ds(0, seg)] = dot_nt(dh[m], WI[1, :H])
        me[...] = dot_nt(dh[m], WI[1, H:])

        def e(i, size):
            r = pl.ds(i, size)
            df = lambda j: he[r, cols(j)] if j < nh else me[r, cols(j - nh)]

            def store(j, v):
                ge[m, pl.ds(i + HALO, size), cols(j)] = (cot[m, r, cols(j)].astype(F32) + v).astype(BF)

            norm_gelu_back(view(out1, m, r), df, nd, gi(1), bi(1), dgbi.at[0], dgbi.at[1], hold, store)

        chunks(seg, e)
        for cond, _, cp in edges(ge, m, seg, gs, gr, z, q, c):
            pl.when(cond)(cp.start)
        return 0

    lax.fori_loop(0, 2, backward, 0)
    done2 = place(1, out2, 1)
    flat = lambda v: v.reshape(2 * seg, v.shape[-1])
    t2 = flat(third2[...])
    for j in range(2):
        put_grad(G, OUT0, dot_tn(t2, flat(cot[:, :, pl.ds(j * H, H)])), nh * j)
    put_grad(G, IN0, dot_tn(flat(first2[...]), flat(dh[...])))
    g_rest = out_copy(G.at[:, pl.ds(0, CONV0)], g_o.at[:, pl.ds(0, CONV0)])
    g_rest.start()
    for m in range(2):
        for s_cond, r_cond, cp in edges(ge, m, seg, gs, gr, z, q, c):
            pl.when(s_cond)(cp.wait_send)
            pl.when(r_cond)(cp.wait_recv)
    g_ge = out_copy(ge, ge_o)
    g_ge.start()
    for cp in saves + [g_conv, g_rest, g_ge]:
        cp.wait()
    done1()
    done2()
    remote(out1, act.at[pl.ds(2 * (1 - c), 2)], acs.at[0], acr.at[0], peer).wait_recv()
    for cp in sends:
        cp.wait_send()
    for cond, _, cp in halos:
        pl.when(cond)(cp.wait_send)


def run_front(lengths, inputs, cot, params, w_in, conv_w, w_out, dec, mask, types):
    seg, D, H = inputs.shape[2], inputs.shape[3], w_in.shape[2]
    rows = seg + 2 * HALO
    any_, vm, sm = (pl.BlockSpec(memory_space=s) for s in (pl.ANY, pltpu.VMEM, pltpu.SMEM))
    sh = jax.ShapeDtypeStruct
    dma = lambda *s: pltpu.SemaphoreType.DMA(s)
    saved = [((2, rows, D), BF), ((2, rows, D), BF), ((2, seg, D), BF), ((2, seg, H), F32), ((2, rows + 16, H), F32), ((2, rows, H), F32),
             ((2, seg, H), BF), ((D, H), BF), ((5, H, H), BF), ((H, D), BF), ((2, UNITS, 16, 128), BF)]
    small = [((2, 8, D), F32), ((2, 8, H), F32), ((2, 8, H), F32), ((8, 128), F32)]
    part = (2, 2, 2, 64, H)
    scratch = [((2, D, H), BF), ((2, 5, H, H), BF), ((2, H, D), BF), ((2, 8, D), F32), ((2, rows, D), BF), ((2, seg, D), BF),
               ((2, seg, D), BF), ((2, seg, D), BF), ((2, seg, H), F32), ((2, rows + 16, H), F32), ((2, rows, H), F32), ((2, seg, H), BF),
               ((2, seg, D), BF), ((2, seg, H), F32), (part, BF), (part, BF), ((12, 64, H), BF), ((8, 64, H), BF), ((8, 64, H), BF),
               ((12, 64, H), BF), ((8, 64, H), BF), (part, BF), (part, BF), ((2, seg, D), BF), ((2, rows, D), BF), ((2, UNITS, 16, 128), BF),
               ((rows, D), BF), ((rows, H), F32), ((seg, H), F32), ((8, 64, H), F32), ((2, seg, H), BF), ((2, 64, D), F32)]
    return pl.pallas_call(
        front,
        out_shape=[sh((4, seg, D), BF)] + [sh(s, d) for s, d in saved + small],
        in_specs=[sm, any_, any_, any_, any_, any_, any_, vm, vm, vm],
        out_specs=[any_] * (1 + len(saved)) + [vm] * len(small),
        scratch_shapes=[pltpu.VMEM(s, d) for s, d in scratch]
        + [dma(8), dma(8), dma(8), dma(2, 2), dma(2, 2), dma(4), dma(4, 4), dma(4, 4), dma(4), dma(2, 2), dma(2, 2), dma(16), dma(2), dma(1)],
        compiler_params=pltpu.CompilerParams(collective_id=1, has_side_effects=True, vmem_limit_bytes=62 * 2**20),
    )(lengths, inputs, cot, params, w_in, conv_w, w_out, dec, mask, types)


def call(fn, outs, scratch, args, scal_at=(), layer={}):
    vm = pl.BlockSpec(memory_space=pltpu.VMEM)
    whole, place = [], []
    for a in args:
        if not any(a is w for w in whole):
            whole.append(a)
        place.append(next(i for i, w in enumerate(whole) if w is a))
    specs = [pl.BlockSpec(memory_space=pltpu.SMEM) if place.index(i) in scal_at else vm for i in range(len(whole))]

    def kernel(*refs):
        ins = [refs[p].at[pl.ds(layer[i], 1)] if i in layer else refs[p] for i, p in enumerate(place)]
        fn(*ins, *refs[len(whole):])

    return pl.pallas_call(
        kernel,
        out_shape=[jax.ShapeDtypeStruct(s, d) for s, d in outs],
        in_specs=specs,
        out_specs=[vm] * len(outs),
        scratch_shapes=[pltpu.VMEM(s, d) for s, d in scratch],
        compiler_params=pltpu.CompilerParams(vmem_limit_bytes=60 * 2**20),
    )(*whole)


def unpack_kernel(conv, w_out, w_in, extra, cnt, s_conv, s_out, s_in, gi, bi, gm, bm, counts):
    H = s_conv.shape[-1]
    for j in range(5):
        for h in range(2):
            s_conv[0, 0, pl.ds(h * 320, 320), cols(j)] = conv[h, pl.ds(j * 20, 20)].reshape(320, 128).astype(F32)
    for j in range(2):
        for h in range(2):
            s_out[0, pl.ds(h * 320, 320), cols(j)] = w_out[h, pl.ds(j * 20, 20)].reshape(320, 128).astype(F32)
    for h in range(2):
        s_in[0, pl.ds(h * 640, 640)] = w_in[h].reshape(640, 128).astype(F32)

    @pl.when(pl.program_id(0) == 0)
    def _():
        small = extra[0].reshape(192, 128).astype(F32)
        for j in range(10):
            gi[:, cols(j)] = small[j : j + 1]
            bi[:, cols(j)] = small[10 + j : 11 + j]
        for k in range(2):
            for j in range(5):
                gm[0, pl.ds(k, 1), cols(j)] = small[20 + 10 * k + j : 21 + 10 * k + j]
                bm[0, pl.ds(k, 1), cols(j)] = small[25 + 10 * k + j : 26 + 10 * k + j]
        counts[...] = cnt[...].reshape(192, 128)[40:41].astype(F32)


def unpack(total, cnt, D, H):
    def spec(units, first):
        return pl.BlockSpec((2, units, 16, 128), lambda k: (0, first + k, 0, 0))

    def full(*s):
        return pl.BlockSpec(s, lambda k: (0,) * len(s))

    sh = lambda *s: jax.ShapeDtypeStruct(s, F32)
    return pl.pallas_call(
        unpack_kernel,
        grid=(5,),
        out_shape=[sh(1, 5, H, H), sh(1, H, D), sh(1, D, H), sh(1, D), sh(1, D), sh(1, 2, H), sh(1, 2, H), sh(1, 128)],
        in_specs=[spec(100, CONV0 // 100), spec(40, 0), spec(40, 5), pl.BlockSpec((2, 12, 16, 128), lambda k: (0, 75, 0, 0)), full(12, 16, 128)],
        out_specs=[pl.BlockSpec((1, 1, H, H), lambda k: (0, k, 0, 0)), pl.BlockSpec((1, H, 256), lambda k: (0, 0, k)),
                   pl.BlockSpec((1, D, 128), lambda k: (0, 0, k)), full(1, D), full(1, D), full(1, 2, H), full(1, 2, H), full(1, 128)],
        compiler_params=pltpu.CompilerParams(vmem_limit_bytes=60 * 2**20),
    )(total, total, total, total, cnt)


def body(inputs, lengths, mlm_mask, true_types, gain_in, bias_in, gain_mid, bias_mid, w_in, conv_w, w_out, decoder, cotangent, fast):
    c = lax.axis_index("section")
    seg, D, H = inputs.shape[2], inputs.shape[3], w_in.shape[2]
    rows = seg + 2 * HALO
    params = jnp.concatenate([gain_in, bias_in, gain_mid.reshape(1, D), bias_mid.reshape(1, D), jnp.zeros((4, D), BF)]).astype(F32)
    dec = jnp.pad(decoder, ((0, 0), (0, 128 - decoder.shape[1])))
    (act, xe, ge, first1, hidden1, sec1, mixed1, third1, w_in1, conv1, w_out1, g_two, dgbi2, dgbm2, dgb2, counts) = run_front(
        lengths[:, 0], inputs, cotangent, params, w_in, conv_w, w_out, dec, mlm_mask[:, 0][..., None], true_types[:, 0][..., None])
    q = lax.axis_index("seq")
    scal = jnp.concatenate([jnp.reshape(q * seg, (1,)), lax.dynamic_slice_in_dim(lengths[:, 0], 2 * c, 2, 0)]).astype(jnp.int32)
    both = lambda w: lax.all_gather(w, "section", axis=0, tiled=True)
    gi, bi, gm, bm = (both(v.astype(F32)) for v in (gain_in, bias_in, gain_mid, bias_mid))
    grad1, dgbi1, dgbm1, g_one = call(
        k4,
        [((2, seg, D), BF), ((2, 8, D), F32), ((4, 8, H), F32), ((2, 900, 16, 128), BF)],
        [((rows, H), F32), ((seg, H), F32), ((rows, H), F32), ((2, seg, H), BF), ((2, seg, H), BF), ((2 * seg, H), BF), ((2, 64, D), F32)],
        (xe, ge, scal, first1, hidden1, sec1, mixed1, third1, w_in1[None], conv1[None], w_out1[None], gi[:1], bi[:1], gm[0], bm[0]),
        (2,), {8: 0, 9: 0, 10: 0})

    def extra(dgbi, dgbm, cnt):
        flat = jnp.concatenate([dgbi.sum(1).reshape(-1), dgbm.sum(1).reshape(-1), cnt.sum(0)])
        flat = jnp.pad(flat, (0, 12 * 2048 - flat.shape[0])).astype(BF).reshape(1, 12, 16, 128)
        return jnp.concatenate([flat, flat], 0)

    g_two = jnp.concatenate([g_two[:, :EXTRA0], extra(dgbi2, jnp.concatenate([dgbm2, dgb2]), counts)], 1)
    g_one = jnp.concatenate([g_one, extra(dgbi1, dgbm1, jnp.zeros_like(counts))], 1)
    if fast:
        N, PU, QU = 6, 88, 64
        total, cnt = allreduce(g_one, g_two, N, PU, QU)
        total = total.reshape(2, UNITS, 16, 128)
    else:
        own, other = jnp.where(c == 0, g_one, g_two), jnp.where(c == 0, g_two, g_one)
        got = lax.ppermute(other, "section", [(0, 1), (1, 0)])
        total = lax.psum(own.astype(F32) + got.astype(F32), ("dp", "seq")).astype(BF)
        cnt = lax.psum(g_two[0, EXTRA0:].astype(F32), ("section", "dp", "seq")).astype(BF)
    s_conv, s_out, s_in, s_gi, s_bi, s_gm, s_bm, s_cnt = unpack(total, cnt, D, H)

    def placed(one, two):
        own, other = jnp.where(c == 0, one, two), jnp.where(c == 0, two, one)
        got = lax.ppermute(other, "section", [(0, 1), (1, 0)])
        return jnp.where(c == 0, jnp.concatenate([own, got]), jnp.concatenate([got, own]))[None, :, None]

    return (act[None, :, None], placed(grad1, ge[:, HALO : HALO + seg]), s_gi, s_bi, s_gm, s_bm, s_in, s_conv, s_out, s_cnt[0, : decoder.shape[1]])


def solution(mesh):
    fast = mesh.shape["dp"] == 4 and mesh.shape["seq"] == 4
    return jax.shard_map(
        functools.partial(body, fast=fast),
        mesh=mesh,
        in_specs=(P(None, "dp", "seq", None), P(None, "dp"), P(None, "dp", "seq"), P(None, "dp", "seq"), P("section", None),
                  P("section", None), P("section", None, None), P("section", None, None), P("section", None, None),
                  P("section", None, None, None), P("section", None, None), P(), P(None, "dp", "seq", None)),
        out_specs=(P("section", None, "dp", "seq", None), P("section", None, "dp", "seq", None), P("section", None), P("section", None),
                   P("section", None, None), P("section", None, None), P("section", None, None), P("section", None, None, None),
                   P("section", None, None), P()),
        check_vma=False,
    )
```

```python
import functools

import jax
import jax.numpy as jnp
from jax import lax
from jax.experimental import pallas as pl
from jax.experimental.pallas import tpu as pltpu
from jax.sharding import PartitionSpec as P

EPS = 1e-05
BF, F32 = jnp.bfloat16, jnp.float32
MESH = pl.DeviceIdType.MESH
G0 = 0.7978845608028654
G1 = 0.044715
DIL = 2
HALO = 16
CH = 16


def dot(a, b):
    return lax.dot_general(a, b, (((1,), (0,)), ((), ())), preferred_element_type=F32)


def dot_nt(a, b):
    return lax.dot_general(a, b, (((1,), (1,)), ((), ())), preferred_element_type=F32)


def dot_tn(a, b):
    return lax.dot_general(a, b, (((0,), (0,)), ((), ())), preferred_element_type=F32)


def chunks(rows, fn, size=None):
    size = size or (96 if rows % 96 == 0 else 64)

    def one(i, _):
        fn(pl.multiple_of(i * size, size), size)
        return 0

    lax.fori_loop(0, rows // size, one, 0)


def cols(j):
    return pl.ds(j * 128, 128)


def stats(load, n):
    total = load(0)
    for j in range(1, n):
        total = total + load(j)
    mean = jnp.sum(total, axis=-1, keepdims=True) * (1.0 / (128 * n))
    square = None
    for j in range(n):
        d = load(j) - mean
        square = d * d if square is None else square + d * d
    var = jnp.sum(square, axis=-1, keepdims=True) * (1.0 / (128 * n))
    return mean, lax.rsqrt(var + EPS)


def norm_gelu(load, n, gain, shift, store):
    mean, rstd = stats(load, n)
    for j in range(n):
        u = (load(j) - mean) * rstd * gain(j) + shift(j)
        t = jnp.tanh(u * (G0 + (G0 * G1) * (u * u)))
        h = 0.5 * u
        store(j, h + h * t)


def fold(v):
    rows, width = v.shape
    return jnp.sum(v.reshape(rows // 8, 8, width), axis=0)


def norm_gelu_back(load, dy, n, gain, shift, dgain, dshift, hold, store):
    mean, rstd = stats(load, n)
    s1 = s2 = None
    for j in range(n):
        g = gain(j)
        hat = (load(j) - mean) * rstd
        u = hat * g + shift(j)
        w = u * u
        t = jnp.tanh(u * (G0 + (G0 * G1) * w))
        slope = 0.5 + 0.5 * t + u * (1.0 - t * t) * (0.5 * G0 + (1.5 * G0 * G1) * w)
        du = dy(j) * slope
        if dgain is not None:
            dgain[:, cols(j)] += fold(du * hat)
            dshift[:, cols(j)] += fold(du)
        dh = du * g
        hold[0, :, cols(j)] = hat
        hold[1, :, cols(j)] = dh
        p = dh * hat
        s1 = dh if s1 is None else s1 + dh
        s2 = p if s2 is None else s2 + p
    m1 = jnp.sum(s1, axis=-1, keepdims=True) * (1.0 / (128 * n))
    m2 = jnp.sum(s2, axis=-1, keepdims=True) * (1.0 / (128 * n))
    for j in range(n):
        store(j, rstd * (hold[1, :, cols(j)] - m1 - hold[0, :, cols(j)] * m2))


def row(ref, k):
    return lambda j: ref[pl.ds(k, 1), cols(j)]


def view(ref, *at):
    return lambda j: ref[(*at, cols(j))].astype(F32)


def put_grad(g_ref, unit, value, col0=0):
    m, n = value.shape
    per = m // 32
    value = value.astype(BF)
    for j in range(n // 128):
        block = value[:, j * 128 : (j + 1) * 128].reshape(m // 16, 16, 128)
        for h in range(2):
            g_ref[h, pl.ds(unit + (col0 + j) * per, per)] = block[h * per : (h + 1) * per]


EXTRA0, OUT0, IN0, CONV0, UNITS = 0, 12, 212, 412, 912


def put(ref, *at):
    def store(j, v):
        ref[(*at, cols(j))] = v.astype(ref.dtype)

    return store


def positions(first, i, size):
    return first + i + lax.broadcasted_iota(jnp.int32, (size, 1), 0)


class Ring:
    def __init__(self, N, PU, QU, M, gap):
        self.M, self.gap = M, gap
        self.N, self.PU, self.QU, self.U = N, PU, QU, PU + QU
        self.out_units = N * self.U
        self.kinds = ["D","P1","P2","PZ1","PZ2","PT1","PT2","PT3","G1","G2","Q1","Q2","X1","X2","X3","X4","QT1","QT2","QT3","F"]
    def scratch(self):
        N2, PU, QU, U = 2 * self.N, self.PU, self.QU, self.U
        b = lambda u, n=N2: pltpu.VMEM((n, u, 16, 128), BF)
        nk = len(self.kinds)
        return [b(U), b(U, 4), b(PU//2), b(PU//4), b(PU//4), b(PU//8), b(QU), b(QU//2), b(QU//4), b(QU//8), b(PU//4), b(QU//8),
                pltpu.SemaphoreType.DMA((nk, N2)), pltpu.SemaphoreType.DMA((nk, N2))]
    def bind(self, conv, GV, out, D, RD, RP1, RP2, RZ1, RZ2, RQ1, RQ2, RX1, RX2, TQ, TX, ss, rs):
        N, PU, QU, U, M = self.N, self.PU, self.QU, self.U, self.M
        R = D
        c, z, q = lax.axis_index("section"), lax.axis_index("dp"), lax.axis_index("seq")
        xb, yb = lax.rem(q, 2), lax.div(q, 2)
        f = jnp.where(c == 0, xb, yb); s = jnp.where(c == 0, yb, xb)
        nx = (c, z, yb*2 + 1 - xb); ny = (c, z, (1-yb)*2 + xb)
        n1 = (c, z, jnp.where(c == 0, nx[2], ny[2])); n2 = (c, z, jnp.where(c == 0, ny[2], nx[2]))
        side = lax.div(z, 2)
        zp = (c, side*2 + 1 - lax.rem(z, 2), q)
        far = (c, 3 - z, q)
        peer = (1 - c, z, q)
        inner = jnp.logical_or(z == 1, z == 2)
        outer = jnp.logical_not(inner)
        ds = pl.ds
        K = {k: i for i, k in enumerate(self.kinds)}
        def cp(k, i, src, dst, dev):
            return pltpu.make_async_remote_copy(src_ref=src, dst_ref=dst, send_sem=ss.at[K[k], i], recv_sem=rs.at[K[k], i], device_id=dev, device_id_type=MESH)
        H, Q4, E8 = PU//2, PU//4, PU//8
        h, q4, e8 = QU//2, QU//8, QU//8
        def add(dst, a, *bs):
            acc = a[...].astype(F32)
            for b in bs: acc = acc + b[...].astype(F32)
            dst[...] = acc.astype(BF)
        pq = lambda ff, s2: ds((2*ff + s2)*Q4, Q4)
        pch = lambda k: ds((2*f + s)*Q4 + k*E8, E8)
        tch = lambda k: ds(k*E8, E8)
        def qn(k): return ds(PU + k*h, h)
        def qhalf(k, ff): return ds(PU + k*h + ff*(h//2), h//2)
        def qquart(k, ff, s2): return ds(PU + k*h + (2*ff+s2)*(h//4), h//4)
        near, farc = side, 1 - side
        C = dict(
          D=lambda i: cp("D", i, GV.at[1-c, ds((i-M)*U, U)], RD.at[lax.rem(i, 4)], peer),
          E=lambda i: cp("D", i, conv.at[1-c, pl.ds(self.first + i*U, U)], RD.at[lax.rem(i, 4)], peer),
          W=lambda i: cp("D", i, D.at[i], RD.at[lax.rem(i, 4)], peer),
          P1=lambda i: cp("P1", i, D.at[i, ds((1-f)*H, H)], RP1.at[i], n1),
          P2=lambda i: cp("P2", i, D.at[i, pq(f, 1-s)], RP2.at[i], n2),
          PZ1=lambda i: cp("PZ1", i, D.at[i, pq(f, s)], RZ1.at[i], zp),
          PZ2=lambda i: cp("PZ2", i, D.at[i, pch(farc)], RZ2.at[i], far),
          PT1=lambda i: cp("PT1", i, TQ.at[i, tch(near)], TQ.at[i, tch(near)], far),
          PT2=lambda i: cp("PT2", i, TQ.at[i, tch(near)], TQ.at[i, tch(near)], zp),
          PT3=lambda i: cp("PT3", i, TQ.at[i, tch(farc)], TQ.at[i, tch(farc)], zp),
          G1=lambda i: cp("G1", i, R.at[i, pq(f, s)], R.at[i, pq(f, s)], n2),
          G2=lambda i: cp("G2", i, R.at[i, ds(f*H, H)], R.at[i, ds(f*H, H)], n1),
          Q1=lambda i: cp("Q1", i, D.at[i, ds(PU, QU)], RQ1.at[i], zp),
          Q2=lambda i: cp("Q2", i, D.at[i, qn(farc)], RQ2.at[i], far),
          X1=lambda i: cp("X1", i, D.at[i, qhalf(near, 1-f)], RX1.at[i], n1),
          X2=lambda i: cp("X2", i, D.at[i, qquart(near, f, 1-s)], RX2.at[i], n2),
          X3=lambda i: cp("X3", i, R.at[i, qquart(near, f, s)], TX.at[i], n2),
          X4=lambda i: cp("X4", i, R.at[i, qhalf(near, f)], R.at[i, qhalf(near, f)], n1),
          QT1=lambda i: cp("QT1", i, R.at[i, qn(near)], R.at[i, qn(near)], far),
          QT2=lambda i: cp("QT2", i, R.at[i, qn(near)], R.at[i, qn(near)], zp),
          QT3=lambda i: cp("QT3", i, R.at[i, qn(farc)], R.at[i, qn(farc)], zp),
        )
        def mine(i): return jnp.where(i < N, 1, 0) == c
        def slot(i): return jnp.where(i < N, lax.rem(i + N - M, N), i - N)
        Fr = lambda i: cp("F", i, R.at[i], out.at[c, ds(slot(i)*U, U)], peer)
        Fl = lambda i: pltpu.make_async_copy(R.at[i], out.at[c, ds(slot(i)*U, U)], ss.at[K["F"], i])
        def S0(i):
            @pl.when(i < M)
            def _(): C["E"](i).start()
            @pl.when(i >= M)
            def _(): C["D"](i).start()
        def S1(i):
            C["W"](i).wait()
            @pl.when(i < M)
            def _(): add(D.at[i], D.at[i], RD.at[lax.rem(i, 4)])
            @pl.when(i >= M)
            def _(): add(D.at[i], GV.at[c, ds((i-M)*U, U)], RD.at[lax.rem(i, 4)])
            C["P1"](i).start()
            @pl.when(outer)
            def _(): C["Q1"](i).start()
        def S2(i):
            @pl.when(inner)
            def _():
                C["Q1"](i).wait_recv()
                add(D.at[i, qn(farc)], D.at[i, qn(farc)], RQ1.at[i, ds(farc*h, h)])
                C["Q2"](i).start()
            C["P1"](i).wait()
            add(D.at[i, ds(f*H, H)], D.at[i, ds(f*H, H)], RP1.at[i])
            C["P2"](i).start()
            @pl.when(outer)
            def _(): C["Q1"](i).wait_send()
        def S3(i):
            C["P2"](i).wait()
            add(D.at[i, pq(f, s)], D.at[i, pq(f, s)], RP2.at[i])
            @pl.when(outer)
            def _(): C["PZ1"](i).start()
            @pl.when(inner)
            def _():
                C["Q2"](i).wait()
                add(D.at[i, qn(near)], D.at[i, qn(near)], RQ1.at[i, ds(near*h, h)], RQ2.at[i])
                C["X1"](i).start()
        def S4(i):
            @pl.when(inner)
            def _():
                C["PZ1"](i).wait_recv()
                add(D.at[i, pch(farc)], D.at[i, pch(farc)], RZ1.at[i, ds(farc*E8, E8)])
                C["PZ2"](i).start()
                C["X1"](i).wait()
                add(D.at[i, qhalf(near, f)], D.at[i, qhalf(near, f)], RX1.at[i])
                C["X2"](i).start()
            @pl.when(outer)
            def _(): C["PZ1"](i).wait_send()
        def S5(i):
            @pl.when(inner)
            def _():
                C["PZ2"](i).wait()
                add(TQ.at[i, tch(near)], D.at[i, pch(near)], RZ1.at[i, ds(near*E8, E8)], RZ2.at[i])
                C["PT1"](i).start(); C["PT2"](i).start()
                C["X2"](i).wait()
                add(R.at[i, qquart(near, f, s)], D.at[i, qquart(near, f, s)], RX2.at[i])
                C["X3"](i).start()
        def S6(i):
            @pl.when(inner)
            def _():
                C["PT1"](i).wait()
                C["PT3"](i).start()
                C["X3"](i).wait()
                D[i, qquart(near, f, 1-s)] = TX[i]
                C["X4"](i).start()
        def S7(i):
            @pl.when(outer)
            def _():
                C["PT2"](i).wait_recv(); C["PT3"](i).wait_recv()
            @pl.when(inner)
            def _():
                C["PT2"](i).wait_send(); C["PT3"](i).wait_send()
            D[i, pq(f, s)] = TQ[i]
            C["G1"](i).start()
            @pl.when(inner)
            def _():
                C["X4"](i).wait()
                C["QT1"](i).start(); C["QT2"](i).start()
        def S8(i):
            C["G1"](i).wait()
            C["G2"](i).start()
            @pl.when(inner)
            def _():
                C["QT1"](i).wait()
                C["QT3"](i).start()
        def S9(i):
            C["G2"](i).wait()
            @pl.when(outer)
            def _():
                C["QT2"](i).wait_recv(); C["QT3"](i).wait_recv()
            @pl.when(inner)
            def _():
                C["QT2"](i).wait_send(); C["QT3"](i).wait_send()
            m = mine(i)
            @pl.when(m)
            def _(): Fl(i).start()
            @pl.when(jnp.logical_not(m))
            def _(): Fr(i).start()
        def S10(i):
            m = mine(i)
            @pl.when(m)
            def _(): Fl(i).wait()
            @pl.when(jnp.logical_not(m))
            def _(): Fr(i).wait_send()
        stages = [S0,S1,S2,S3,S4,S5,S6,S7,S8,S9,S10]
        def step(t):
            for si, stage in enumerate(stages):
                j = t - si
                first, second = jnp.logical_and(j >= 0, j < N), jnp.logical_and(j >= N + self.gap, j < 2*N + self.gap)
                i = jnp.where(j < N, j, j - self.gap)
                pl.when(jnp.logical_or(first, second))(functools.partial(stage, i))
        def recv_final():
            def body(j, _):
                i = jnp.where(c == 1, j, j + N)
                Fr(i).wait_recv()
                return 0
            lax.fori_loop(0, N, body, 0)
        def barrier():
            b = pltpu.get_barrier_semaphore()
            for d in plane(c, z, q) + [zp]:
                pl.semaphore_signal(b, inc=1, device_id=d, device_id_type=MESH)
            @pl.when(inner)
            def _():
                pl.semaphore_signal(b, inc=1, device_id=far, device_id_type=MESH)
                pl.semaphore_wait(b, 9)
            @pl.when(outer)
            def _(): pl.semaphore_wait(b, 8)
        self.D = D
        self.barrier, self.step, self.recv_final, self.iters = barrier, step, recv_final, 2*N + self.gap + len(stages) - 1


class NoRing:
    def __init__(self, N, U, M):
        self.N, self.U, self.M, self.D = N, U, M, None
        self.out_units = (2 * N - M) * U
    def scratch(self): return []
    def bind(self, *refs): pass
    def barrier(self): greet(plane(lax.axis_index("section"), lax.axis_index("dp"), lax.axis_index("seq")))
    def step(self, t): pass


def plane(c, z, q):
    out = []
    for i in range(1, 8):
        n = lax.rem(c * 4 + q + i, 8)
        out.append((lax.div(n, 4), z, lax.rem(n, 4)))
    return out


def greet(ids):
    barrier = pltpu.get_barrier_semaphore()
    for d in ids:
        pl.semaphore_signal(barrier, inc=1, device_id=d, device_id_type=MESH)
    pl.semaphore_wait(barrier, len(ids))


def remote(src, dst, ss, rs, dev):
    return pltpu.make_async_remote_copy(src_ref=src, dst_ref=dst, send_sem=ss, recv_sem=rs, device_id=dev, device_id_type=MESH)


def both_ways(cond, here, there):
    @pl.when(cond)
    def _():
        here()

    @pl.when(jnp.logical_not(cond))
    def _():
        there()


class Spread:
    def __init__(self, c, z, q, ss, rs, ls):
        self.c, self.z, self.q, self.ss, self.rs, self.ls = c, z, q, ss, rs, ls

    def go(self, a, src, dst, m, start):
        c, z, q = self.c, self.z, self.q
        for h in range(2):
            s, d, j = src.at[m, :, h], dst(q), 2 * m + h
            far = remote(s, d, self.ss.at[a, j], self.rs.at[a, q], (jnp.int32(h), z, 2 * c + m))
            near = pltpu.make_async_copy(s, d, self.ls.at[a])
            both_ways(jnp.logical_and(h == c, 2 * c + m == q), near.start if start else near.wait, far.start if start else far.wait_send)

    def arrive(self, a, src, dst):
        c, z, q = self.c, self.z, self.q
        fc = lax.div(q, 2)
        for p in range(4):
            @pl.when(jnp.logical_not(jnp.logical_and(c == fc, p == q)))
            def _():
                remote(src.at[0, :, 0], dst(p), self.ss.at[a, 0], self.rs.at[a, p], (fc, z, jnp.int32(p))).wait_recv()

    def back(self, a, src, dst, p, start):
        c, z, q = self.c, self.z, self.q
        tc, slot = lax.div(q, 2), lax.rem(q, 2)
        s, d = src.at[pl.ds(2 * p, 2)], dst.at[slot, :, c]
        far = remote(s, d, self.ss.at[a, p], self.rs.at[a, 2 * slot + c], (tc, z, jnp.int32(p)))
        near = pltpu.make_async_copy(s, d, self.ls.at[a])
        both_ways(jnp.logical_and(tc == c, p == q), near.start if start else near.wait, far.start if start else far.wait_send)

    def back_arrive(self, a, src, dst, m):
        c, z, q = self.c, self.z, self.q
        for h in range(2):
            @pl.when(jnp.logical_not(jnp.logical_and(h == c, 2 * c + m == q)))
            def _():
                remote(src.at[pl.ds(0, 2)], dst.at[m, :, h], self.ss.at[a, 0], self.rs.at[a, 2 * m + h], (jnp.int32(h), z, 2 * c + m)).wait_recv()


def edges(ref, m, seg, ss, rs, z, q, c):
    before = remote(ref.at[m, pl.ds(HALO, HALO)], ref.at[m, pl.ds(HALO + seg, HALO)], ss.at[0, m], rs.at[0, m], (c, z, q - 1))
    after = remote(ref.at[m, pl.ds(seg, HALO)], ref.at[m, pl.ds(0, HALO)], ss.at[1, m], rs.at[1, m], (c, z, q + 1))
    return ((q > 0, q < 3, before), (q < 3, q > 0, after))


def front(lengths, inputs, cot_all, params, w_in, conv_w, w_out,
          xe_o, out1_o, first1_o, hidden1_o, sec1_o, mixed1_o, third1_o, first2_o, hidden2_o, w_in_o, conv1_o, w_out_o, pr_o, g_o,
          third2, dsec2, dgb,
          WI, WC, WO, PR, xe, cot, out1, first1, hidden1, sec1, mixed1, third1, first2, hidden2, sec2, dth2, sp, dthr, thirdr, dpad, dsecr,
          G, fe, he, me, mx, hold,
          ws, wr, wl, xs, xr, xl, ss, rs, ls, os_):
    c, z, q = lax.axis_index("section"), lax.axis_index("dp"), lax.axis_index("seq")
    peer = (1 - c, z, q)
    seg, D = cot.shape[1:]
    H = mixed1.shape[2]
    nd, nh = D // 128, H // 128
    rows = seg + 2 * HALO
    base = q * seg
    own = [pltpu.make_async_copy(inputs.at[2 * c + m, 0], xe.at[m, pl.ds(HALO, seg)], xl.at[m]) for m in range(2)]
    own += [pltpu.make_async_copy(cot_all.at[2 * c + m, 0], cot.at[m], xl.at[2 + m]) for m in range(2)]
    mats = [(params, PR.at[c]), (w_in.at[0], WI.at[c])] + [(conv_w.at[0, k], WC.at[c, k]) for k in range(5)] + [(w_out.at[0], WO.at[c])]
    loads = [pltpu.make_async_copy(s, d, wl.at[i]) for i, (s, d) in enumerate(mats)]
    for cp in own[:2] + loads + own[2:]:
        cp.start()
    greet(plane(c, z, q))
    sends = [remote(s, d, ws.at[i], wr.at[i], peer) for i, (s, d) in enumerate(mats)]
    halos = []
    for m in range(2):
        x = inputs.at[2 * c + m, 0]
        halos.append((q > 0, q < 3, remote(x.at[pl.ds(0, HALO)], xe.at[m, pl.ds(HALO + seg, HALO)], xs.at[0, m], xr.at[0, m], (c, z, q - 1))))
        halos.append((q < 3, q > 0, remote(x.at[pl.ds(seg - HALO, HALO)], xe.at[m, pl.ds(0, HALO)], xs.at[1, m], xr.at[1, m], (c, z, q + 1))))
    for cond, _, cp in halos:
        pl.when(cond)(cp.start)
    for cp in sends:
        cp.start()

    @pl.when(q == 0)
    def _():
        xe[:, pl.ds(0, HALO)] = jnp.zeros((2, HALO, D), BF)

    @pl.when(q == 3)
    def _():
        xe[:, pl.ds(HALO + seg, HALO)] = jnp.zeros((2, HALO, D), BF)

    def have(i):
        loads[i].wait()
        sends[i].wait_recv()

    dgb[...] = jnp.zeros_like(dgb)
    zero = jnp.zeros((2, 64, H), BF)
    for ref in (sp, dpad):
        ref[pl.ds(0, 2)] = zero
        ref[pl.ds(10, 2)] = zero
    sec1[:, pl.ds(0, 8)] = jnp.zeros((2, 8, H), F32)
    sec1[:, pl.ds(rows + 8, 8)] = jnp.zeros((2, 8, H), F32)
    spread = Spread(c, z, q, ss, rs, ls)
    sp_at = lambda p: sp.at[pl.ds(2 + 2 * p, 2)]
    dthr_at = lambda p: dthr.at[pl.ds(2 * p, 2)]
    gi, bi = lambda l: row(PR.at[l], 0), lambda l: row(PR.at[l], 1)
    gm = lambda l, k: (lambda j: PR[l, pl.ds(2, 1), cols(k * nh + j)])
    bm = lambda l, k: (lambda j: PR[l, pl.ds(3, 1), cols(k * nh + j)])
    out_sem = [0]

    def out_copy(src, dst):
        cp = pltpu.make_async_copy(src, dst, os_.at[out_sem[0]])
        out_sem[0] += 1
        return cp

    have(0)
    for m in range(2):
        own[m].wait()
    for _, cond, cp in halos:
        pl.when(cond)(cp.wait_recv)
    have(1)

    def forward(m, _):
        length = lengths[2 * c + m]

        def a(i, size):
            r = pl.ds(i, size)
            norm_gelu(view(xe, m, r), nd, gi(0), bi(0), put(fe, r))

        chunks(rows, a)
        first1[m] = fe[pl.ds(HALO, seg)]
        he[...] = dot(fe[...], WI[0])
        hidden1[m] = he[pl.ds(HALO, seg)]

        def b(i, size):
            pos = positions(base - HALO, i, size)
            keep = jnp.logical_and(pos >= 0, pos < length)

            def store(j, v):
                sec1[m, pl.ds(i + 8, size), cols(j)] = jnp.where(keep, v, 0.0).astype(BF).astype(F32)

            norm_gelu(view(he, pl.ds(i, size)), nh, gm(0, 0), bm(0, 0), store)

        chunks(rows, b)

        @pl.when(m == 0)
        def _():
            for k in range(5):
                have(2 + k)

        acc = None
        for k in range(5):
            term = dot(sec1[m, pl.ds(8 + DIL * (k - 2), rows)].astype(BF), WC[0, k])
            acc = term if acc is None else acc + term
        mixed1[m] = acc

        def e(i, size):
            norm_gelu(view(mixed1, m, pl.ds(i + HALO, size)), nh, gm(0, 1), bm(0, 1), put(third1, m, pl.ds(i, size)))

        chunks(seg, e)

        @pl.when(m == 0)
        def _():
            have(7)

        he[pl.ds(0, seg)] = dot(third1[m], WO[0, :, :H])
        me[...] = dot(third1[m], WO[0, :, H:])

        def d(i, size):
            r = pl.ds(i, size)
            for j in range(nd):
                br = he[r, cols(j)] if j < nh else me[r, cols(j - nh)]
                out1[m, r, cols(j)] = (xe[m, pl.ds(i + HALO, size), cols(j)].astype(F32) + br).astype(BF)
            norm_gelu(view(out1, m, r), nd, gi(1), bi(1), put(first2, m, r))

        chunks(seg, d)
        hidden2[m] = dot(first2[m], WI[1])

        def f(jj, _):
            i = pl.multiple_of(jj * 64, 64)
            pos = positions(base, i, 64)

            def store(j, v):
                sec2[m, lax.div(jj, 2), lax.rem(jj, 2), :, cols(j)] = jnp.where(pos < length, v, 0.0).astype(BF)

            norm_gelu(view(hidden2, m, pl.ds(i, 64)), nh, gm(1, 0), bm(1, 0), store)
            return 0

        lax.fori_loop(0, seg // 64, f, 0)
        spread.go(0, sec2, sp_at, m, True)
        return 0

    lax.fori_loop(0, 2, forward, 0)
    for m in range(2):
        own[2 + m].wait()

    def third_grad(m, _):
        dth2[m] = dot_nt(cot[m], WO[1]).astype(BF).reshape(2, 2, 64, H)
        spread.go(1, dth2, dthr_at, m, True)
        return 0

    lax.fori_loop(0, 2, third_grad, 0)
    saves = [out_copy(s, d) for s, d in ((xe, xe_o), (first1, first1_o), (hidden1, hidden1_o), (sec1, sec1_o), (mixed1, mixed1_o),
                                         (third1, third1_o), (WI, w_in_o), (WC.at[0], conv1_o), (WO, w_out_o), (PR, pr_o),
                                         (out1, out1_o), (first2, first2_o), (hidden2, hidden2_o))]
    for cp in saves:
        cp.start()

    for m in range(2):
        spread.go(0, sec2, sp_at, m, False)
    spread.arrive(0, sec2, sp_at)

    def conv(r, _):
        acc = None
        for k in range(5):
            term = dot(sp[pl.ds(4 * r + k, 4)].reshape(256, H), WC[1, k])
            acc = term if acc is None else acc + term
        mx[pl.ds(4 * r, 4)] = acc.reshape(4, 64, H)
        return 0

    lax.fori_loop(0, 2, conv, 0)
    for m in range(2):
        spread.go(1, dth2, dthr_at, m, False)
    spread.arrive(1, dth2, dthr_at)

    def mid(i, _):
        every = pl.ds(0, 64)
        norm_gelu(view(mx, i, every), nh, gm(1, 1), bm(1, 1), put(thirdr, i, every))
        norm_gelu_back(view(mx, i, every), view(dthr, i, every), nh, gm(1, 1), bm(1, 1), dgb.at[0], dgb.at[1], hold, put(dpad, i + 2, every))
        return 0

    lax.fori_loop(0, 8, mid, 0)
    for p in range(4):
        spread.back(2, thirdr, third2, p, True)

    def conv_back(r, _):
        acc = None
        for k in range(5):
            term = dot_nt(dpad[pl.ds(4 * r + 4 - k, 4)].reshape(256, H), WC[1, k])
            acc = term if acc is None else acc + term
        dsecr[pl.ds(4 * r, 4)] = acc.astype(BF).reshape(4, 64, H)
        return 0

    lax.fori_loop(0, 2, conv_back, 0)
    for p in range(4):
        spread.back(3, dsecr, dsec2, p, True)
    dm = dpad[pl.ds(2, 8)].reshape(512, H)

    def conv_grads(k, _):
        put_grad(G, k * 100, dot_tn(sp[pl.ds(k, 8)].reshape(512, H), dm))
        return 0

    lax.fori_loop(0, 5, conv_grads, 0)
    g_conv = out_copy(G, g_o)
    g_conv.start()
    for p in range(4):
        spread.back(2, thirdr, third2, p, False)
        spread.back(3, dsecr, dsec2, p, False)
    for m in range(2):
        spread.back_arrive(2, thirdr, third2, m)
        spread.back_arrive(3, dsecr, dsec2, m)
    for cp in saves + [g_conv]:
        cp.wait()
    for cp in sends:
        cp.wait_send()
    for cond, _, cp in halos:
        pl.when(cond)(cp.wait_send)


def run_front(lengths, inputs, cot, params, w_in, conv_w, w_out):
    seg, D, H = inputs.shape[2], inputs.shape[3], w_in.shape[2]
    rows = seg + 2 * HALO
    any_, vm, sm = (pl.BlockSpec(memory_space=s) for s in (pl.ANY, pltpu.VMEM, pltpu.SMEM))
    sh = jax.ShapeDtypeStruct
    dma = lambda *s: pltpu.SemaphoreType.DMA(s)
    part = (2, 2, 2, 64, H)
    saved = [((2, rows, D), BF), ((2, seg, D), BF), ((2, seg, D), BF), ((2, seg, H), F32), ((2, rows + 16, H), F32),
             ((2, rows, H), F32), ((2, seg, H), BF), ((2, seg, D), BF), ((2, seg, H), F32), ((2, D, H), BF), ((5, H, H), BF), ((2, H, D), BF),
             ((2, 8, D), F32), ((2, 500, 16, 128), BF), (part, BF), (part, BF)]
    scratch = [((2, D, H), BF), ((2, 5, H, H), BF), ((2, H, D), BF), ((2, 8, D), F32), ((2, rows, D), BF), ((2, seg, D), BF),
               ((2, seg, D), BF), ((2, seg, D), BF), ((2, seg, H), F32), ((2, rows + 16, H), F32), ((2, rows, H), F32), ((2, seg, H), BF),
               ((2, seg, D), BF), ((2, seg, H), F32), (part, BF), (part, BF), ((12, 64, H), BF), ((8, 64, H), BF), ((8, 64, H), BF),
               ((12, 64, H), BF), ((8, 64, H), BF), ((2, 500, 16, 128), BF),
               ((rows, D), BF), ((rows, H), F32), ((seg, H), F32), ((8, 64, H), F32), ((2, 64, D), F32)]
    return pl.pallas_call(
        front,
        out_shape=[sh(s, d) for s, d in saved] + [sh((2, 8, H), F32)],
        in_specs=[sm] + [any_] * 6,
        out_specs=[any_] * len(saved) + [vm],
        scratch_shapes=[pltpu.VMEM(s, d) for s, d in scratch]
        + [dma(8), dma(8), dma(8), dma(2, 2), dma(2, 2), dma(4), dma(4, 4), dma(4, 4), dma(4), dma(20)],
        compiler_params=pltpu.CompilerParams(collective_id=1, has_side_effects=True, vmem_limit_bytes=62 * 2**20),
    )(lengths, inputs, cot, params, w_in, conv_w, w_out)


def back(lengths, cot_all, dec, mask, types, dgb, conv, xe_h, out1_h, first1_h, hidden1_h, sec1_h, mixed1_h, third1_h, first2_h, hidden2_h,
         third2_h, dsec2_h, w_in_h, conv1_h, w_out_h, pr_h,
         act, igr, total, cnt,
         WI, WO2, WO1, WC, PR, xo, ge, cot, og, first, hidden, third, dsec, dh, sec1, mixed1, he, me, dme, swin, hold, dgbi, dgbm, counts, GV,
         ls, gs, gr, ps, pr, *ring_refs, ring):
    c, z, q = lax.axis_index("section"), lax.axis_index("dp"), lax.axis_index("seq")
    peer = (1 - c, z, q)
    seg, D = cot.shape[1:]
    H = hidden.shape[2]
    nd, nh = D // 128, H // 128
    rows = seg + 2 * HALO
    base = q * seg
    N, U, M = ring.N, ring.U, ring.M
    low = N * U - M * U
    head = low - CONV0
    ring.first = head
    ring.bind(conv, GV, total, *ring_refs)
    count = [0]

    def load(src, dst):
        cp = pltpu.make_async_copy(src, dst, ls.at[count[0]])
        count[0] += 1
        return cp

    out1, xe = xo.at[:, pl.ds(0, seg)], xo
    l_ring = [] if ring.D is None else [load(conv.at[c, pl.ds(head + i * U, U)], ring.D.at[i]) for i in range(M)]
    l_two = [load(s, d) for s, d in ((pr_h, PR), (third2_h, third), (w_out_h.at[1], WO2), (out1_h, out1), (dsec2_h, dsec), (hidden2_h, hidden),
                                     (w_in_h.at[1], WI))]
    l_two += [load(cot_all.at[2 * c + m, 0], cot.at[m]) for m in range(2)]
    l_grad = [load(first2_h, first), load(conv.at[:, pl.ds(0, head)], GV.at[:, pl.ds(CONV0, head)])]
    l_one = [load(s, d) for s, d in ((w_out_h.at[0], WO1), (conv1_h, WC), (mixed1_h, mixed1), (sec1_h, sec1))]
    for cp in l_ring + l_two + l_grad + l_one:
        cp.start()
    ring.barrier()
    ring.step(0)

    @pl.when(q == 0)
    def _():
        ge[:, pl.ds(0, HALO)] = jnp.zeros((2, HALO, D), BF)

    @pl.when(q == 3)
    def _():
        ge[:, pl.ds(HALO + seg, HALO)] = jnp.zeros((2, HALO, D), BF)

    for ref in (dgbi, dgbm, counts):
        ref[...] = jnp.zeros_like(ref)
    gi, bi = lambda l: row(PR.at[l], 0), lambda l: row(PR.at[l], 1)
    gm = lambda l, k: (lambda j: PR[l, pl.ds(2, 1), cols(k * nh + j)])
    bm = lambda l, k: (lambda j: PR[l, pl.ds(3, 1), cols(k * nh + j)])
    for cp in l_two + l_ring:
        cp.wait()
    labels = lax.broadcasted_iota(jnp.int32, (1, 128), 1)

    def two(m, _):
        length = lengths[2 * c + m]
        he[pl.ds(0, seg)] = dot(third[m], WO2[:, :H])
        me[...] = dot(third[m], WO2[:, H:])

        def a(i, size):
            r = pl.ds(i, size)
            for j in range(nd):
                br = he[r, cols(j)] if j < nh else me[r, cols(j - nh)]
                og[m, r, cols(j)] = (out1[m, r, cols(j)].astype(F32) + br).astype(BF)

        chunks(seg, a)
        logits = jnp.where(labels < 30, dot(og[m], dec[...]), -1e30)
        ex = jnp.exp(logits - jnp.max(logits, axis=-1, keepdims=True))
        probs = ex / jnp.sum(ex, axis=-1, keepdims=True)
        weight = jnp.where(positions(base, 0, seg) < length, mask[2 * c + m].astype(F32), 0.0)
        counts[...] += fold(jnp.where(types[2 * c + m] == labels, probs * weight, 0.0))

        def b(i, size):
            r = pl.ds(i, size)
            pos = positions(base, i, size)
            ds = lambda j: jnp.where(pos < length, dsec[m, r, cols(j)].astype(F32), 0.0)
            norm_gelu_back(view(hidden, m, r), ds, nh, gm(1, 0), bm(1, 0), dgbm.at[0], dgbm.at[1], hold, put(dh, m, r))

        chunks(seg, b)
        he[pl.ds(0, seg)] = dot_nt(dh[m], WI[:H])
        me[...] = dot_nt(dh[m], WI[H:])

        def e(i, size):
            r = pl.ds(i, size)
            df = lambda j: he[r, cols(j)] if j < nh else me[r, cols(j - nh)]

            def store(j, v):
                ge[m, pl.ds(i + HALO, size), cols(j)] = (cot[m, r, cols(j)].astype(F32) + v).astype(BF)

            norm_gelu_back(view(out1, m, r), df, nd, gi(1), bi(1), dgbi.at[0], dgbi.at[1], hold, store)

        chunks(seg, e)
        for cond, _, cp in edges(ge, m, seg, gs, gr, z, q, c):
            pl.when(cond)(cp.start)
        ring.step(1 + m)
        return 0

    lax.fori_loop(0, 2, two, 0)

    def place(i, src, dst, layer):
        here = load(src, dst.at[pl.ds(2 * c, 2)])
        there = remote(src, dst.at[pl.ds(2 * c, 2)], ps.at[i], pr.at[i // 2], peer)
        both_ways(c == layer, here.start, there.start)
        return lambda: both_ways(c == layer, here.wait, there.wait_send)

    inside = ge.at[:, pl.ds(HALO, seg)]
    placed = [place(0, out1, act, 0), place(1, og, act, 1), place(2, inside, igr, 1)]
    flat = lambda v: v.reshape(2 * seg, v.shape[-1])
    for cp in l_grad:
        cp.wait()
    t2 = flat(third[...])
    for j in range(2):
        put_grad(GV, OUT0, dot_tn(t2, flat(cot[:, :, pl.ds(j * H, H)])), nh * j)
    put_grad(GV, IN0, dot_tn(flat(first[...]), flat(dh[...])))

    def extra(first_unit, third_norm, with_counts):
        flat_rows = [dgbi[k, :, cols(j)] for k in range(2) for j in range(nd)]
        flat_rows += [dgbm[k, :, cols(j)] for k in range(2) for j in range(nh)]
        flat_rows += [third_norm(k, j) for k in range(2) for j in range(nh)]
        small = [jnp.sum(v, axis=0, keepdims=True) for v in flat_rows]
        small.append(jnp.sum(counts[...], axis=0, keepdims=True) if with_counts else jnp.zeros((1, 128), F32))
        small.append(jnp.zeros((192 - len(small), 128), F32))
        block = jnp.concatenate(small, axis=0).astype(BF).reshape(12, 16, 128)
        for h in range(2):
            GV[h, pl.ds(first_unit, 12)] = block

    extra(0, lambda k, j: dgb[k, :, cols(j)], True)
    l_late = [load(s, d) for s, d in ((third1_h, third), (hidden1_h, hidden), (w_in_h.at[0], WI), (first1_h, first))]
    for cp in l_late:
        cp.start()
    ring.step(3)
    for ref in (dgbi, dgbm):
        ref[...] = jnp.zeros_like(ref)
    for m in range(2):
        for s_cond, r_cond, cp in edges(ge, m, seg, gs, gr, z, q, c):
            pl.when(s_cond)(cp.wait_send)
            pl.when(r_cond)(cp.wait_recv)
    for cp in l_one + l_late[1:3]:
        cp.wait()
    for done in placed[:2]:
        done()
    l_x = load(xe_h, xe)
    l_x.start()
    ring.step(4)

    def one(m, _):
        length = lengths[2 * c + m]
        he[...] = dot_nt(ge[m], WO1[...])

        def a(i, size):
            r = pl.ds(i + HALO, size)

            def store(j, v):
                v = v.astype(BF)
                dme[r, cols(j)] = v.astype(F32)
                dsec[m, pl.ds(i, size), cols(j)] = v

            norm_gelu_back(view(mixed1, m, r), view(he, r), nh, gm(0, 1), bm(0, 1), dgbm.at[2], dgbm.at[3], hold, store)

        chunks(seg, a)
        for edge in (0, rows - HALO):
            r = pl.ds(edge, HALO)
            pos = positions(base - HALO, edge, HALO)
            within = jnp.logical_and(pos >= 0, pos < 4 * seg)

            def store(j, v):
                dme[r, cols(j)] = jnp.where(within, v, 0.0).astype(BF).astype(F32)

            norm_gelu_back(view(mixed1, m, r), view(he, r), nh, gm(0, 1), bm(0, 1), None, None, hold.at[:, pl.ds(0, HALO)], store)
        ring.step(5 + 2 * m)
        acc = None
        for k in range(5):
            term = dot_nt(dme[pl.ds(HALO - DIL * (k - 2), seg)].astype(BF), WC[k])
            acc = term if acc is None else acc + term
        he[pl.ds(0, seg)] = acc

        def b(i, size):
            r = pl.ds(i, size)
            pos = positions(base, i, size)
            ds = lambda j: jnp.where(pos < length, he[r, cols(j)], 0.0)
            norm_gelu_back(view(hidden, m, r), ds, nh, gm(0, 0), bm(0, 0), dgbm.at[0], dgbm.at[1], hold, put(dh, m, r))

        chunks(seg, b)
        he[pl.ds(0, seg)] = dot_nt(dh[m], WI[:H])
        me[...] = dot_nt(dh[m], WI[H:])

        @pl.when(m == 0)
        def _():
            l_x.wait()

        def e(i, size):
            r, x = pl.ds(i, size), pl.ds(i + HALO, size)
            df = lambda j: he[r, cols(j)] if j < nh else me[r, cols(j - nh)]

            def store(j, v):
                og[m, r, cols(j)] = (ge[m, x, cols(j)].astype(F32) + v).astype(BF)

            norm_gelu_back(view(xe, m, x), df, nd, gi(0), bi(0), dgbi.at[0], dgbi.at[1], hold, store)

        chunks(seg, e)
        ring.step(6 + 2 * m)
        return 0

    lax.fori_loop(0, 2, one, 0)
    placed.append(place(3, og, igr, 0))
    for cp in (l_late[0], l_late[3]):
        cp.wait()
    t1 = flat(third[...])
    for j in range(2):
        put_grad(GV, low + OUT0, dot_tn(t1, flat(ge[:, pl.ds(HALO, seg), pl.ds(j * H, H)])), nh * j)
    put_grad(GV, low + IN0, dot_tn(flat(first[...]), flat(dh[...])))
    extra(low, lambda k, j: dgbm[2 + k, :, cols(j)], False)
    d1 = flat(dsec[...])
    for k in range(5):
        for m in range(2):
            swin[pl.ds(m * seg, seg)] = sec1[m, pl.ds(8 + HALO + DIL * (k - 2), seg)].astype(BF)
        put_grad(GV, low + CONV0 + k * 100, dot_tn(swin[...], d1))

    def rest(t, _):
        ring.step(t)
        return 0

    if ring.D is None:
        l_all = load(GV, total)
        l_all.start()
        l_all.wait()
        cnt[...] = jnp.zeros_like(cnt)
    else:
        lax.fori_loop(9, ring.iters, rest, 0)
        ring.recv_final()
        cnt[...] = ring.D[M, pl.ds(EXTRA0, 12)]
    for done in placed[2:]:
        done()
    for i, dst in ((0, act), (1, igr)):
        remote(og, dst.at[pl.ds(2 * (1 - c), 2)], ps.at[0], pr.at[i], peer).wait_recv()


def run_back(ring, lengths, cot, dec, mask, types, dgb, conv, saved):
    seg, D, H = cot.shape[2], cot.shape[3], saved[3].shape[-1]
    rows = seg + 2 * HALO
    N, M, U = ring.N, ring.M, ring.U
    any_, vm, sm = (pl.BlockSpec(memory_space=s) for s in (pl.ANY, pltpu.VMEM, pltpu.SMEM))
    sh = jax.ShapeDtypeStruct
    dma = lambda *s: pltpu.SemaphoreType.DMA(s)
    scratch = [((D, H), BF), ((H, D), BF), ((H, D), BF), ((5, H, H), BF), ((2, 8, D), F32), ((2, rows, D), BF), ((2, rows, D), BF),
               ((2, seg, D), BF), ((2, seg, D), BF), ((2, seg, D), BF), ((2, seg, H), F32), ((2, seg, H), BF), ((2, seg, H), BF),
               ((2, seg, H), BF), ((2, rows + 16, H), F32), ((2, rows, H), F32), ((rows, H), F32), ((seg, H), F32), ((rows, H), F32),
               ((2 * seg, H), BF), ((2, 64, D), F32), ((2, 8, D), F32), ((4, 8, H), F32), ((8, 128), F32),
               ((2, (2 * N - M) * U, 16, 128), BF)]
    return pl.pallas_call(
        functools.partial(back, ring=ring),
        out_shape=[sh((4, seg, D), BF), sh((4, seg, D), BF), sh((2, ring.out_units, 16, 128), BF), sh((12, 16, 128), BF)],
        in_specs=[sm, any_, vm, vm, vm, vm] + [any_] * (1 + len(saved)),
        out_specs=[any_, any_, any_, vm],
        scratch_shapes=[pltpu.VMEM(s, d) for s, d in scratch] + [dma(32), dma(2, 2), dma(2, 2), dma(4), dma(2)] + ring.scratch(),
        compiler_params=pltpu.CompilerParams(collective_id=2, has_side_effects=True, vmem_limit_bytes=63 * 2**20),
    )(lengths, cot, dec, mask, types, dgb, conv, *saved)


def unpack_kernel(conv, w_out, w_in, extra, cnt, s_conv, s_out, s_in, gi, bi, gm, bm, counts):
    H = s_conv.shape[-1]
    for j in range(5):
        for h in range(2):
            s_conv[0, 0, pl.ds(h * 320, 320), cols(j)] = conv[h, pl.ds(j * 20, 20)].reshape(320, 128).astype(F32)
    for j in range(2):
        for h in range(2):
            s_out[0, pl.ds(h * 320, 320), cols(j)] = w_out[h, pl.ds(j * 20, 20)].reshape(320, 128).astype(F32)
    for h in range(2):
        s_in[0, pl.ds(h * 640, 640)] = w_in[h].reshape(640, 128).astype(F32)

    @pl.when(pl.program_id(0) == 0)
    def _():
        small = extra[0].reshape(192, 128).astype(F32)
        for j in range(10):
            gi[:, cols(j)] = small[j : j + 1]
            bi[:, cols(j)] = small[10 + j : 11 + j]
        for k in range(2):
            for j in range(5):
                gm[0, pl.ds(k, 1), cols(j)] = small[20 + 10 * k + j : 21 + 10 * k + j]
                bm[0, pl.ds(k, 1), cols(j)] = small[25 + 10 * k + j : 26 + 10 * k + j]
        counts[...] = cnt[...].reshape(192, 128)[40:41].astype(F32)


def unpack(total, cnt, D, H):
    def spec(units, first):
        return pl.BlockSpec(tuple(pl.Element(n) for n in (2, units, 16, 128)), lambda k: (0, first + units * k, 0, 0))

    def full(*s):
        return pl.BlockSpec(s, lambda k: (0,) * len(s))

    sh = lambda *s: jax.ShapeDtypeStruct(s, F32)
    return pl.pallas_call(
        unpack_kernel,
        grid=(5,),
        out_shape=[sh(1, 5, H, H), sh(1, H, D), sh(1, D, H), sh(1, D), sh(1, D), sh(1, 2, H), sh(1, 2, H), sh(1, 128)],
        in_specs=[spec(100, CONV0), spec(40, OUT0), spec(40, IN0), pl.BlockSpec((2, 12, 16, 128), lambda k: (0, 0, 0, 0)), full(12, 16, 128)],
        out_specs=[pl.BlockSpec((1, 1, H, H), lambda k: (0, k, 0, 0)), pl.BlockSpec((1, H, 256), lambda k: (0, 0, k)),
                   pl.BlockSpec((1, D, 128), lambda k: (0, 0, k)), full(1, D), full(1, D), full(1, 2, H), full(1, 2, H), full(1, 128)],
        compiler_params=pltpu.CompilerParams(vmem_limit_bytes=60 * 2**20),
    )(total, total, total, total, cnt)


def body(inputs, lengths, mlm_mask, true_types, gain_in, bias_in, gain_mid, bias_mid, w_in, conv_w, w_out, decoder, cotangent, fast):
    seg, D, H = inputs.shape[2], inputs.shape[3], w_in.shape[2]
    params = jnp.concatenate([gain_in, bias_in, gain_mid.reshape(1, D), bias_mid.reshape(1, D), jnp.zeros((4, D), BF)]).astype(F32)
    dec = jnp.pad(decoder, ((0, 0), (0, 128 - decoder.shape[1])))
    line = lengths[:, 0]
    (xe, out1, first1, hidden1, sec1, mixed1, third1, first2, hidden2, w_in_b, conv1, w_out_b, pr, g_conv, third2, dsec2, dgb) = run_front(
        line, inputs, cotangent, params, w_in, conv_w, w_out)
    rows_of = lambda v: v.reshape(2, seg, H)
    act, igr, total, cnt = run_back(
        Ring(6, 88, 64, 3, 3) if fast else NoRing(6, 152, 3),
        line, cotangent, dec, mlm_mask[:, 0][..., None], true_types[:, 0][..., None], dgb, g_conv,
        (xe, out1, first1, hidden1, sec1, mixed1, third1, first2, hidden2, rows_of(third2), rows_of(dsec2), w_in_b, conv1, w_out_b, pr))
    if not fast:
        c = lax.axis_index("section")
        g_one, g_two = total[:, 456:], jnp.concatenate([total[:, :456], g_conv[:, 44:]], 1)
        own, other = jnp.where(c == 0, g_one, g_two), jnp.where(c == 0, g_two, g_one)
        got = lax.ppermute(other, "section", [(0, 1), (1, 0)])
        total = lax.psum(own.astype(F32) + got.astype(F32), ("dp", "seq")).astype(BF)
        cnt = lax.psum(g_two[0, :12].astype(F32), ("section", "dp", "seq")).astype(BF)
    s_conv, s_out, s_in, s_gi, s_bi, s_gm, s_bm, s_cnt = unpack(total, cnt, D, H)
    return (act[None, :, None], igr[None, :, None], s_gi, s_bi, s_gm, s_bm, s_in, s_conv, s_out, s_cnt[0, : decoder.shape[1]])


def solution(mesh):
    fast = mesh.shape["dp"] == 4 and mesh.shape["seq"] == 4
    return jax.shard_map(
        functools.partial(body, fast=fast),
        mesh=mesh,
        in_specs=(P(None, "dp", "seq", None), P(None, "dp"), P(None, "dp", "seq"), P(None, "dp", "seq"), P("section", None),
                  P("section", None), P("section", None, None), P("section", None, None), P("section", None, None),
                  P("section", None, None, None), P("section", None, None), P(), P(None, "dp", "seq", None)),
        out_specs=(P("section", None, "dp", "seq", None), P("section", None, "dp", "seq", None), P("section", None), P("section", None),
                   P("section", None, None), P("section", None, None), P("section", None, None), P("section", None, None, None),
                   P("section", None, None), P()),
        check_vma=False,
    )
```

```python
import functools

import jax
import jax.numpy as jnp
from jax import lax
from jax.experimental import pallas as pl
from jax.experimental.pallas import tpu as pltpu
from jax.sharding import PartitionSpec as P


EPS = 1e-05
BF, F32 = jnp.bfloat16, jnp.float32
MESH = pl.DeviceIdType.MESH
G0 = 0.7978845608028654
G1 = 0.044715
DIL = 2
HALO = 16
OUT0, CONV0, IN0, EXTRA0, UNITS = 0, 200, 700, 900, 936
PIECES, PLANE_UNITS, Z_UNITS, SLOTS = 13, 48, 24, 8


def dot(a, b):
    return lax.dot_general(a, b, (((1,), (0,)), ((), ())), preferred_element_type=F32)


def dot_nt(a, b):
    return lax.dot_general(a, b, (((1,), (1,)), ((), ())), preferred_element_type=F32)


def dot_tn(a, b):
    return lax.dot_general(a, b, (((0,), (0,)), ((), ())), preferred_element_type=F32)


def chunks(rows, fn, size=None):
    size = size or (96 if rows % 96 == 0 else 64)

    def one(i, _):
        fn(pl.multiple_of(i * size, size), size)
        return 0

    lax.fori_loop(0, rows // size, one, 0)


def cols(j):
    return pl.ds(j * 128, 128)


def stats(load, n):
    total = load(0)
    for j in range(1, n):
        total = total + load(j)
    mean = jnp.sum(total, axis=-1, keepdims=True) * (1.0 / (128 * n))
    square = None
    for j in range(n):
        d = load(j) - mean
        square = d * d if square is None else square + d * d
    var = jnp.sum(square, axis=-1, keepdims=True) * (1.0 / (128 * n))
    return mean, lax.rsqrt(var + EPS)


def norm_gelu(load, n, gain, shift, store):
    mean, rstd = stats(load, n)
    for j in range(n):
        u = (load(j) - mean) * rstd * gain(j) + shift(j)
        t = jnp.tanh(u * (G0 + (G0 * G1) * (u * u)))
        h = 0.5 * u
        store(j, h + h * t)


def fold(v):
    rows, width = v.shape
    return jnp.sum(v.reshape(rows // 8, 8, width), axis=0)


def norm_gelu_back(load, dy, n, gain, shift, dgain, dshift, hold, store):
    mean, rstd = stats(load, n)
    s1 = s2 = None
    for j in range(n):
        g = gain(j)
        hat = (load(j) - mean) * rstd
        u = hat * g + shift(j)
        w = u * u
        t = jnp.tanh(u * (G0 + (G0 * G1) * w))
        slope = 0.5 + 0.5 * t + u * (1.0 - t * t) * (0.5 * G0 + (1.5 * G0 * G1) * w)
        du = dy(j) * slope
        if dgain is not None:
            dgain[:, cols(j)] += fold(du * hat)
            dshift[:, cols(j)] += fold(du)
        dh = du * g
        hold[0, :, cols(j)] = hat
        hold[1, :, cols(j)] = dh
        p = dh * hat
        s1 = dh if s1 is None else s1 + dh
        s2 = p if s2 is None else s2 + p
    m1 = jnp.sum(s1, axis=-1, keepdims=True) * (1.0 / (128 * n))
    m2 = jnp.sum(s2, axis=-1, keepdims=True) * (1.0 / (128 * n))
    for j in range(n):
        store(j, rstd * (hold[1, :, cols(j)] - m1 - hold[0, :, cols(j)] * m2))


def norm_gelu_both(load, dy, n, gain, shift, dgain, dshift, hold, store, store_back):
    mean, rstd = stats(load, n)
    s1 = s2 = None
    for j in range(n):
        g = gain(j)
        hat = (load(j) - mean) * rstd
        u = hat * g + shift(j)
        w = u * u
        t = jnp.tanh(u * (G0 + (G0 * G1) * w))
        half = 0.5 + 0.5 * t
        store(j, u * half)
        slope = half + u * (1.0 - t * t) * (0.5 * G0 + (1.5 * G0 * G1) * w)
        du = dy(j) * slope
        dgain[:, cols(j)] += fold(du * hat)
        dshift[:, cols(j)] += fold(du)
        dh = du * g
        hold[0, :, cols(j)] = hat
        hold[1, :, cols(j)] = dh
        p = dh * hat
        s1 = dh if s1 is None else s1 + dh
        s2 = p if s2 is None else s2 + p
    m1 = jnp.sum(s1, axis=-1, keepdims=True) * (1.0 / (128 * n))
    m2 = jnp.sum(s2, axis=-1, keepdims=True) * (1.0 / (128 * n))
    for j in range(n):
        store_back(j, rstd * (hold[1, :, cols(j)] - m1 - hold[0, :, cols(j)] * m2))


def row(ref, k):
    return lambda j: ref[pl.ds(k, 1), cols(j)]


def view(ref, *at):
    return lambda j: ref[(*at, cols(j))].astype(F32)


def put_grad(DG, c, unit, value, col0=0):
    m, n = value.shape
    per = m // 32
    value = value.astype(BF)
    for j in range(n // 128):
        block = value[:, j * 128 : (j + 1) * 128].reshape(m // 16, 16, 128)
        for h in range(2):
            DG[lax.rem(h + c, 2), pl.ds(unit + (col0 + j) * per, per)] = block[h * per : (h + 1) * per]


def put(ref, *at):
    def store(j, v):
        ref[(*at, cols(j))] = v.astype(ref.dtype)

    return store


def positions(first, i, size):
    return first + i + lax.broadcasted_iota(jnp.int32, (size, 1), 0)


class Ring:
    KINDS = ("D", "P1", "P2", "PZ1", "PZ2", "PT1", "PT2", "PT3", "G1", "G2", "Q1", "Q2", "X1", "X2", "X3", "X4", "QT1", "QT2", "QT3", "F")

    def __init__(self, N, PU, QU):
        self.N, self.PU, self.QU, self.U = N, PU, QU, PU + QU
        self.out_units, self.live = N * self.U, True

    def scratch(self):
        PU, QU, U = self.PU, self.QU, self.U
        b = lambda u, n=SLOTS: pltpu.VMEM((n, u, 16, 128), BF)
        sems = pltpu.SemaphoreType.DMA((len(self.KINDS), 2 * self.N))
        return [b(U, 4), b(PU // 2), b(PU // 4), b(PU // 4), b(PU // 8), b(QU), b(QU // 2), b(QU // 4), b(QU // 8), b(PU // 4), b(QU // 8),
                sems, sems]

    def bind(self, DG, out, RD, RP1, RP2, RZ1, RZ2, RQ1, RQ2, RX1, RX2, TQ, TX, ss, rs):
        N, PU, QU, U, ds = self.N, self.PU, self.QU, self.U, pl.ds
        c, z, q = lax.axis_index("section"), lax.axis_index("dp"), lax.axis_index("seq")
        xb, yb = lax.rem(q, 2), lax.div(q, 2)
        f, s = jnp.where(c == 0, xb, yb), jnp.where(c == 0, yb, xb)
        qx, qy = yb * 2 + 1 - xb, (1 - yb) * 2 + xb
        n1 = (c, z, jnp.where(c == 0, qx, qy))
        n2 = (c, z, jnp.where(c == 0, qy, qx))
        side = lax.div(z, 2)
        near, farc = side, 1 - side
        zp = (c, side * 2 + 1 - lax.rem(z, 2), q)
        far = (c, 3 - z, q)
        peer = (1 - c, z, q)
        inner = jnp.logical_or(z == 1, z == 2)
        outer = jnp.logical_not(inner)
        order = {k: i for i, k in enumerate(self.KINDS)}

        def cp(k, i, src, dst, dev):
            return remote(src, dst, ss.at[order[k], i], rs.at[order[k], i], dev)

        def add(dst, *terms):
            acc = terms[0][...].astype(F32)
            for t in terms[1:]:
                acc = acc + t[...].astype(F32)
            dst[...] = acc.astype(BF)

        def phys(i):
            return jnp.where(i < 6, i + 3, jnp.where(i < 9, i - 6, i))

        def part(i, start=0, size=U):
            return DG.at[0, ds(phys(i) * U + start, size)]

        H, Q4, E8 = PU // 2, PU // 4, PU // 8
        h, h2, h4 = QU // 2, QU // 4, QU // 8
        pq = lambda a, b: ((2 * a + b) * Q4, Q4)
        pch = lambda k: ((2 * f + s) * Q4 + k * E8, E8)
        tch = lambda k: ds(k * E8, E8)
        qn = lambda k: (PU + k * h, h)
        qhalf = lambda k, a: (PU + k * h + a * h2, h2)
        qquart = lambda k, a, b: (PU + k * h + (2 * a + b) * h4, h4)
        k8 = lambda i: lax.rem(i, SLOTS)
        rd = lambda i: RD.at[lax.rem(i, 4)]
        same = lambda k, at, dev: (lambda i: cp(k, i, part(i, *at), part(i, *at), dev))
        C = dict(
            D=lambda i: cp("D", i, DG.at[1, ds(phys(i) * U, U)], rd(i), peer),
            P1=lambda i: cp("P1", i, part(i, (1 - f) * H, H), RP1.at[k8(i)], n1),
            P2=lambda i: cp("P2", i, part(i, *pq(f, 1 - s)), RP2.at[k8(i)], n2),
            PZ1=lambda i: cp("PZ1", i, part(i, *pq(f, s)), RZ1.at[k8(i)], zp),
            PZ2=lambda i: cp("PZ2", i, part(i, *pch(farc)), RZ2.at[k8(i)], far),
            PT1=lambda i: cp("PT1", i, TQ.at[k8(i), tch(near)], TQ.at[k8(i), tch(near)], far),
            PT2=lambda i: cp("PT2", i, TQ.at[k8(i), tch(near)], TQ.at[k8(i), tch(near)], zp),
            PT3=lambda i: cp("PT3", i, TQ.at[k8(i), tch(farc)], TQ.at[k8(i), tch(farc)], zp),
            G1=same("G1", pq(f, s), n2),
            G2=same("G2", (f * H, H), n1),
            Q1=lambda i: cp("Q1", i, part(i, PU, QU), RQ1.at[k8(i)], zp),
            Q2=lambda i: cp("Q2", i, part(i, *qn(farc)), RQ2.at[k8(i)], far),
            X1=lambda i: cp("X1", i, part(i, *qhalf(near, 1 - f)), RX1.at[k8(i)], n1),
            X2=lambda i: cp("X2", i, part(i, *qquart(near, f, 1 - s)), RX2.at[k8(i)], n2),
            X3=lambda i: cp("X3", i, part(i, *qquart(near, f, s)), TX.at[k8(i)], n2),
            X4=same("X4", qhalf(near, f), n1),
            QT1=same("QT1", qn(near), far),
            QT2=same("QT2", qn(near), zp),
            QT3=same("QT3", qn(farc), zp),
        )

        def final(i, start):
            to = out.at[c, ds(phys(i) * U - jnp.where(i < N, 0, N * U), U)]
            there, here = cp("F", i, part(i), to, peer), pltpu.make_async_copy(part(i), to, ss.at[order["F"], i])
            both_ways(jnp.where(i < N, 1, 0) == c, here.start if start else here.wait, there.start if start else there.wait_send)

        def on_inner(fn):
            pl.when(inner)(fn)

        def on_outer(fn):
            pl.when(outer)(fn)

        def s0(i):
            C["D"](i).start()

        def s1(i):
            C["D"](i).wait()
            add(part(i), part(i), rd(i))
            C["P1"](i).start()
            on_outer(lambda: C["Q1"](i).start())

        def s2(i):
            @on_inner
            def _():
                C["Q1"](i).wait_recv()
                add(part(i, *qn(farc)), part(i, *qn(farc)), RQ1.at[k8(i), ds(farc * h, h)])
                C["Q2"](i).start()

            C["P1"](i).wait()
            add(part(i, f * H, H), part(i, f * H, H), RP1.at[k8(i)])
            C["P2"](i).start()
            on_outer(lambda: C["Q1"](i).wait_send())

        def s3(i):
            C["P2"](i).wait()
            add(part(i, *pq(f, s)), part(i, *pq(f, s)), RP2.at[k8(i)])
            on_outer(lambda: C["PZ1"](i).start())

            @on_inner
            def _():
                C["Q2"](i).wait()
                add(part(i, *qn(near)), part(i, *qn(near)), RQ1.at[k8(i), ds(near * h, h)], RQ2.at[k8(i)])
                C["X1"](i).start()

        def s4(i):
            @on_inner
            def _():
                C["PZ1"](i).wait_recv()
                add(part(i, *pch(farc)), part(i, *pch(farc)), RZ1.at[k8(i), tch(farc)])
                C["PZ2"](i).start()
                C["X1"](i).wait()
                add(part(i, *qhalf(near, f)), part(i, *qhalf(near, f)), RX1.at[k8(i)])
                C["X2"](i).start()

            on_outer(lambda: C["PZ1"](i).wait_send())

        def s5(i):
            @on_inner
            def _():
                C["PZ2"](i).wait()
                add(TQ.at[k8(i), tch(near)], part(i, *pch(near)), RZ1.at[k8(i), tch(near)], RZ2.at[k8(i)])
                C["PT1"](i).start()
                C["PT2"](i).start()
                C["X2"](i).wait()
                add(part(i, *qquart(near, f, s)), part(i, *qquart(near, f, s)), RX2.at[k8(i)])
                C["X3"](i).start()

        def s6(i):
            @on_inner
            def _():
                C["PT1"](i).wait()
                C["PT3"](i).start()
                C["X3"](i).wait()
                part(i, *qquart(near, f, 1 - s))[...] = TX[k8(i)]
                C["X4"](i).start()

        def s7(i):
            @on_outer
            def _():
                C["PT2"](i).wait_recv()
                C["PT3"](i).wait_recv()

            @on_inner
            def _():
                C["PT2"](i).wait_send()
                C["PT3"](i).wait_send()

            part(i, *pq(f, s))[...] = TQ[k8(i)]
            C["G1"](i).start()

            @on_inner
            def _():
                C["X4"](i).wait()
                C["QT1"](i).start()
                C["QT2"](i).start()

        def s8(i):
            C["G1"](i).wait()
            C["G2"](i).start()

            @on_inner
            def _():
                C["QT1"](i).wait()
                C["QT3"](i).start()

        def s9(i):
            C["G2"](i).wait()

            @on_outer
            def _():
                C["QT2"](i).wait_recv()
                C["QT3"](i).wait_recv()

            @on_inner
            def _():
                C["QT2"](i).wait_send()
                C["QT3"](i).wait_send()

            final(i, True)

        def s10(i):
            final(i, False)

        stages = (s0, s1, s2, s3, s4, s5, s6, s7, s8, s9, s10)

        def step(t):
            for k, stage in enumerate(stages):
                i = t - k
                pl.when(jnp.logical_and(i >= 0, i < 2 * N))(functools.partial(stage, i))

        def finish():
            def one(j, _):
                i = jnp.where(c == 1, j, j + N)
                cp("F", i, part(i), out.at[c, ds(0, U)], peer).wait_recv()
                return 0

            lax.fori_loop(0, N, one, 0)

        def barrier():
            b = pltpu.get_barrier_semaphore()
            for d in plane(c, z, q) + [zp]:
                pl.semaphore_signal(b, inc=1, device_id=d, device_id_type=MESH)

            @on_inner
            def _():
                pl.semaphore_signal(b, inc=1, device_id=far, device_id_type=MESH)
                pl.semaphore_wait(b, 9)

            on_outer(lambda: pl.semaphore_wait(b, 8))

        self.step, self.finish, self.barrier, self.iters = step, finish, barrier, 2 * N + len(stages) - 1


class NoRing:
    def __init__(self, N, U):
        self.N, self.U, self.live, self.out_units = N, U, False, 2 * N * U

    def scratch(self):
        return []

    def bind(self, *refs):
        pass

    def barrier(self):
        greet(plane(lax.axis_index("section"), lax.axis_index("dp"), lax.axis_index("seq")))

    def step(self, t):
        pass


def plane(c, z, q):
    out = []
    for i in range(1, 8):
        n = lax.rem(c * 4 + q + i, 8)
        out.append((lax.div(n, 4), z, lax.rem(n, 4)))
    return out


def greet(ids):
    barrier = pltpu.get_barrier_semaphore()
    for d in ids:
        pl.semaphore_signal(barrier, inc=1, device_id=d, device_id_type=MESH)
    pl.semaphore_wait(barrier, len(ids))


def remote(src, dst, ss, rs, dev):
    return pltpu.make_async_remote_copy(src_ref=src, dst_ref=dst, send_sem=ss, recv_sem=rs, device_id=dev, device_id_type=MESH)


def both_ways(cond, here, there):
    @pl.when(cond)
    def _():
        here()

    @pl.when(jnp.logical_not(cond))
    def _():
        there()


class Spread:
    def __init__(self, c, z, q, ss, rs, ls):
        self.c, self.z, self.q, self.ss, self.rs, self.ls = c, z, q, ss, rs, ls

    def go(self, a, src, dst, m, start):
        c, z, q = self.c, self.z, self.q
        for h in range(2):
            s, d, j = src.at[m, :, h], dst(q), 2 * m + h
            far = remote(s, d, self.ss.at[a, j], self.rs.at[a, q], (jnp.int32(h), z, 2 * c + m))
            near = pltpu.make_async_copy(s, d, self.ls.at[a])
            both_ways(jnp.logical_and(h == c, 2 * c + m == q), near.start if start else near.wait, far.start if start else far.wait_send)

    def arrive(self, a, src, dst):
        c, z, q = self.c, self.z, self.q
        fc = lax.div(q, 2)
        for p in range(4):
            @pl.when(jnp.logical_not(jnp.logical_and(c == fc, p == q)))
            def _():
                remote(src.at[0, :, 0], dst(p), self.ss.at[a, 0], self.rs.at[a, p], (fc, z, jnp.int32(p))).wait_recv()

    def back(self, a, src, dst, p, start):
        c, z, q = self.c, self.z, self.q
        tc, slot = lax.div(q, 2), lax.rem(q, 2)
        s, d = src.at[pl.ds(2 * p, 2)], dst.at[slot, :, c]
        far = remote(s, d, self.ss.at[a, p], self.rs.at[a, 2 * slot + c], (tc, z, jnp.int32(p)))
        near = pltpu.make_async_copy(s, d, self.ls.at[a])
        both_ways(jnp.logical_and(tc == c, p == q), near.start if start else near.wait, far.start if start else far.wait_send)

    def back_arrive(self, a, src, dst, m):
        c, z, q = self.c, self.z, self.q
        for h in range(2):
            @pl.when(jnp.logical_not(jnp.logical_and(h == c, 2 * c + m == q)))
            def _():
                remote(src.at[pl.ds(0, 2)], dst.at[m, :, h], self.ss.at[a, 0], self.rs.at[a, 2 * m + h], (jnp.int32(h), z, 2 * c + m)).wait_recv()


def edges(ref, m, seg, ss, rs, z, q, c):
    before = remote(ref.at[m, pl.ds(HALO, HALO)], ref.at[m, pl.ds(HALO + seg, HALO)], ss.at[0, m], rs.at[0, m], (c, z, q - 1))
    after = remote(ref.at[m, pl.ds(seg, HALO)], ref.at[m, pl.ds(0, HALO)], ss.at[1, m], rs.at[1, m], (c, z, q + 1))
    return ((q > 0, q < 3, before), (q < 3, q > 0, after))


def whole(lengths, inputs, cot_all, params, w_in, conv_w, w_out, dec, code, act, igr, total, cnt,
          WI, WC, WO, PR, xe, cot, out1, first1, hidden1, sec1, mixed1, third1, first2, hidden2, sec2, dth2, sp, dthr, thirdr, dpad,
          third2, dsec2, og, ge, hd, me, hold, dgbi, dgbm, counts, DG,
          ws, wr, wl, xs, xr, xl, ss, rs, ls, gs, gr, ps, pr, pw, *ring_refs, ring):
    c, z, q = lax.axis_index("section"), lax.axis_index("dp"), lax.axis_index("seq")
    peer = (1 - c, z, q)
    seg, D = cot.shape[1:]
    H = mixed1.shape[2]
    nd, nh = D // 128, H // 128
    rows = seg + 2 * HALO
    base = q * seg
    he, dme = hd.at[pl.ds(0, rows)], hd.at[pl.ds(rows, rows)]
    ring.bind(DG, total, *ring_refs)
    own = [pltpu.make_async_copy(inputs.at[2 * c + m, 0], xe.at[m, pl.ds(HALO, seg)], xl.at[m]) for m in range(2)]
    own += [pltpu.make_async_copy(cot_all.at[2 * c + m, 0], cot.at[m], xl.at[2 + m]) for m in range(2)]
    mats = [(params, PR.at[c]), (w_in.at[0], WI.at[c])] + [(conv_w.at[0, k], WC.at[c, k]) for k in range(5)] + [(w_out.at[0], WO.at[c])]
    loads = [pltpu.make_async_copy(s, d, wl.at[i]) for i, (s, d) in enumerate(mats)]
    for cp in own[:2] + loads + own[2:]:
        cp.start()
    ring.barrier()
    sends = [remote(s, d, ws.at[i], wr.at[i], peer) for i, (s, d) in enumerate(mats)]
    halos = []
    for m in range(2):
        x = inputs.at[2 * c + m, 0]
        halos.append((q > 0, q < 3, remote(x.at[pl.ds(0, HALO)], xe.at[m, pl.ds(HALO + seg, HALO)], xs.at[0, m], xr.at[0, m], (c, z, q - 1))))
        halos.append((q < 3, q > 0, remote(x.at[pl.ds(seg - HALO, HALO)], xe.at[m, pl.ds(0, HALO)], xs.at[1, m], xr.at[1, m], (c, z, q + 1))))
    for cond, _, cp in halos:
        pl.when(cond)(cp.start)
    for cp in sends:
        cp.start()

    @pl.when(q == 0)
    def _():
        xe[:, pl.ds(0, HALO)] = jnp.zeros((2, HALO, D), BF)
        ge[:, pl.ds(0, HALO)] = jnp.zeros((2, HALO, D), BF)

    @pl.when(q == 3)
    def _():
        xe[:, pl.ds(HALO + seg, HALO)] = jnp.zeros((2, HALO, D), BF)
        ge[:, pl.ds(HALO + seg, HALO)] = jnp.zeros((2, HALO, D), BF)

    def have(i):
        loads[i].wait()
        sends[i].wait_recv()

    for ref in (dgbi, dgbm, counts):
        ref[...] = jnp.zeros_like(ref)
    zero = jnp.zeros((2, 64, H), BF)
    for ref in (sp, dpad):
        ref[pl.ds(0, 2)] = zero
        ref[pl.ds(10, 2)] = zero
    sec1[:, pl.ds(0, 8)] = jnp.zeros((2, 8, H), F32)
    sec1[:, pl.ds(rows + 8, 8)] = jnp.zeros((2, 8, H), F32)
    spread = Spread(c, z, q, ss, rs, ls)
    sp_at = lambda p: sp.at[pl.ds(2 + 2 * p, 2)]
    dthr_at = lambda p: dthr.at[pl.ds(2 * p, 2)]
    gi, bi = lambda l: row(PR.at[l], 0), lambda l: row(PR.at[l], 1)
    gm = lambda l, k: (lambda j: PR[l, pl.ds(2, 1), cols(k * nh + j)])
    bm = lambda l, k: (lambda j: PR[l, pl.ds(3, 1), cols(k * nh + j)])

    have(0)
    for m in range(2):
        own[m].wait()
    for _, cond, cp in halos:
        pl.when(cond)(cp.wait_recv)

    def first_norm(m, _):
        def a(i, size):
            r = pl.ds(i, size)
            norm_gelu(view(xe, m, r), nd, gi(0), bi(0), put(first1, m, r))

        chunks(rows, a)
        return 0

    lax.fori_loop(0, 2, first_norm, 0)
    have(1)

    def forward(m, _):
        length = lengths[2 * c + m]
        he[...] = dot(first1[m], WI[0])
        hidden1[m] = he[pl.ds(HALO, seg)]

        def b(i, size):
            pos = positions(base - HALO, i, size)
            keep = jnp.logical_and(pos >= 0, pos < length)

            def store(j, v):
                sec1[m, pl.ds(i + 8, size), cols(j)] = jnp.where(keep, v, 0.0).astype(BF).astype(F32)

            norm_gelu(view(he, pl.ds(i, size)), nh, gm(0, 0), bm(0, 0), store)

        chunks(rows, b)

        @pl.when(m == 0)
        def _():
            for k in range(5):
                have(2 + k)

        acc = None
        for k in range(5):
            term = dot(sec1[m, pl.ds(8 + DIL * (k - 2), rows)].astype(BF), WC[0, k])
            acc = term if acc is None else acc + term
        mixed1[m] = acc

        def e(i, size):
            norm_gelu(view(mixed1, m, pl.ds(i + HALO, size)), nh, gm(0, 1), bm(0, 1), put(third1, m, pl.ds(i, size)))

        chunks(seg, e)

        @pl.when(m == 0)
        def _():
            have(7)

        he[pl.ds(0, seg)] = dot(third1[m], WO[0, :, :H])
        me[...] = dot(third1[m], WO[0, :, H:])

        def d(i, size):
            r = pl.ds(i, size)
            for j in range(nd):
                br = he[r, cols(j)] if j < nh else me[r, cols(j - nh)]
                out1[m, r, cols(j)] = (xe[m, pl.ds(i + HALO, size), cols(j)].astype(F32) + br).astype(BF)
            norm_gelu(view(out1, m, r), nd, gi(1), bi(1), put(first2, m, r))

        chunks(seg, d)
        hidden2[m] = dot(first2[m], WI[1])

        def f(jj, _):
            i = pl.multiple_of(jj * 64, 64)
            pos = positions(base, i, 64)

            def store(j, v):
                sec2[m, lax.div(jj, 2), lax.rem(jj, 2), :, cols(j)] = jnp.where(pos < length, v, 0.0).astype(BF)

            norm_gelu(view(hidden2, m, pl.ds(i, 64)), nh, gm(1, 0), bm(1, 0), store)
            return 0

        lax.fori_loop(0, seg // 64, f, 0)
        spread.go(0, sec2, sp_at, m, True)
        return 0

    lax.fori_loop(0, 2, forward, 0)
    for m in range(2):
        own[2 + m].wait()

    def third_grad(m, _):
        dth2[m] = dot_nt(cot[m], WO[1]).astype(BF).reshape(2, 2, 64, H)
        spread.go(1, dth2, dthr_at, m, True)
        return 0

    lax.fori_loop(0, 2, third_grad, 0)

    def place(i, src, dst, layer):
        to = dst.at[pl.ds(2 * c, 2)]
        here, there = pltpu.make_async_copy(src, to, pw.at[i]), remote(src, to, ps.at[i], pr.at[i // 2], peer)
        both_ways(c == layer, here.start, there.start)
        return lambda: both_ways(c == layer, here.wait, there.wait_send)

    placed = [place(0, out1, act, 0)]
    for m in range(2):
        spread.go(0, sec2, sp_at, m, False)
    spread.arrive(0, sec2, sp_at)

    def conv(r, _):
        acc = None
        for k in range(5):
            term = dot(sp[pl.ds(4 * r + k, 4)].reshape(256, H), WC[1, k])
            acc = term if acc is None else acc + term
        hd[pl.ds(256 * r, 256)] = acc
        return 0

    lax.fori_loop(0, 2, conv, 0)
    for m in range(2):
        spread.go(1, dth2, dthr_at, m, False)
    spread.arrive(1, dth2, dthr_at)

    def mid(i, _):
        every = pl.ds(0, 64)
        norm_gelu_both(view(hd, pl.ds(pl.multiple_of(64 * i, 64), 64)), view(dthr, i, every), nh, gm(1, 1), bm(1, 1), dgbm.at[2], dgbm.at[3], hold,
                       put(thirdr, i, every), put(dpad, i + 2, every))
        return 0

    lax.fori_loop(0, 8, mid, 0)
    for p in range(4):
        spread.back(2, thirdr, third2, p, True)
    dm2 = dpad[pl.ds(2, 8)].reshape(512, H)

    def conv_grads(k, _):
        put_grad(DG, c, CONV0 + k * 100, dot_tn(sp[pl.ds(k, 8)].reshape(512, H), dm2))
        return 0

    lax.fori_loop(0, 5, conv_grads, 0)
    ring.step(0)

    def conv_back(r, _):
        acc = None
        for k in range(5):
            term = dot_nt(dpad[pl.ds(4 * r + 4 - k, 4)].reshape(256, H), WC[1, k])
            acc = term if acc is None else acc + term
        dthr[pl.ds(4 * r, 4)] = acc.astype(BF).reshape(4, 64, H)
        return 0

    lax.fori_loop(0, 2, conv_back, 0)
    for p in range(4):
        spread.back(3, dthr, dsec2, p, True)
    ring.step(1)
    for p in range(4):
        spread.back(2, thirdr, third2, p, False)
    for m in range(2):
        spread.back_arrive(2, thirdr, third2, m)
    labels = lax.broadcasted_iota(jnp.int32, (1, 128), 1)

    def two_out(m, _):
        t = third2[m].reshape(seg, H)
        he[pl.ds(0, seg)] = dot(t, WO[1, :, :H])
        me[...] = dot(t, WO[1, :, H:])

        def a(i, size):
            r = pl.ds(i, size)
            for j in range(nd):
                br = he[r, cols(j)] if j < nh else me[r, cols(j - nh)]
                og[m, r, cols(j)] = (out1[m, r, cols(j)].astype(F32) + br).astype(BF)

        chunks(seg, a)
        logits = jnp.where(labels < 30, dot(og[m], dec[...]), -1e30)
        ex = jnp.exp(logits - jnp.max(logits, axis=-1, keepdims=True))
        probs = ex / jnp.sum(ex, axis=-1, keepdims=True)
        kept = positions(base, 0, seg) < lengths[2 * c + m]
        counts[...] += fold(jnp.where(jnp.logical_and(code[2 * c + m] == labels, kept), probs, 0.0))
        return 0

    lax.fori_loop(0, 2, two_out, 0)
    placed.append(place(1, og, act, 1))
    ring.step(2)
    for p in range(4):
        spread.back(3, dthr, dsec2, p, False)
    for m in range(2):
        spread.back_arrive(3, dthr, dsec2, m)
    dh = lambda m: dpad.at[pl.ds(4 * m, 4)]

    def two(m, _):
        def b(i, _):
            pos = positions(base, i * 64, 64)
            u, h = lax.div(i, 2), lax.rem(i, 2)
            ds = lambda j: jnp.where(pos < lengths[2 * c + m], dsec2[m, u, h, :, cols(j)].astype(F32), 0.0)
            norm_gelu_back(view(hidden2, m, pl.ds(pl.multiple_of(i * 64, 64), 64)), ds, nh, gm(1, 0), bm(1, 0), dgbm.at[0], dgbm.at[1], hold,
                           put(dpad, 4 * m + i, pl.ds(0, 64)))
            return 0

        lax.fori_loop(0, seg // 64, b, 0)
        dhm = dh(m)[...].reshape(seg, H)
        he[pl.ds(0, seg)] = dot_nt(dhm, WI[1, :H])
        me[...] = dot_nt(dhm, WI[1, H:])

        def e(i, size):
            r = pl.ds(i, size)
            df = lambda j: he[r, cols(j)] if j < nh else me[r, cols(j - nh)]

            def store(j, v):
                ge[m, pl.ds(i + HALO, size), cols(j)] = (cot[m, r, cols(j)].astype(F32) + v).astype(BF)

            norm_gelu_back(view(out1, m, r), df, nd, gi(1), bi(1), dgbi.at[0], dgbi.at[1], hold, store)

        chunks(seg, e)
        for cond, _, cp in edges(ge, m, seg, gs, gr, z, q, c):
            pl.when(cond)(cp.start)
        ring.step(3 + m)
        return 0

    lax.fori_loop(0, 2, two, 0)
    placed.append(place(2, ge.at[:, pl.ds(HALO, seg)], igr, 1))
    flat = lambda v: v.reshape(2 * seg, v.shape[-1])
    t2 = flat(third2[...])
    for j in range(2):
        put_grad(DG, c, OUT0, dot_tn(t2, flat(cot[:, :, pl.ds(j * H, H)])), nh * j)
    ring.step(5)
    put_grad(DG, c, IN0, dot_tn(flat(first2[...]), dpad[pl.ds(0, 8)].reshape(2 * seg, H)))

    def extra(first_unit, with_counts):
        flat_rows = [dgbi[k, :, cols(j)] for k in range(2) for j in range(nd)]
        flat_rows += [dgbm[k, :, cols(j)] for k in range(4) for j in range(nh)]
        small = [jnp.sum(v, axis=0, keepdims=True) for v in flat_rows]
        if with_counts:
            small.append(jnp.sum(counts[...], axis=0, keepdims=True))
        size = UNITS - EXTRA0
        small.append(jnp.zeros((48 - len(small), 128), F32))
        block = jnp.concatenate(small, axis=0).astype(BF).reshape(3, 16, 128)
        for h in range(2):
            DG[h, pl.ds(first_unit, 3)] = block
            DG[h, pl.ds(first_unit + 3, size - 3)] = jnp.zeros((size - 3, 16, 128), BF)

    extra(EXTRA0, True)
    ring.step(6)
    for ref in (dgbi, dgbm):
        ref[...] = jnp.zeros_like(ref)
    for m in range(2):
        for s_cond, r_cond, cp in edges(ge, m, seg, gs, gr, z, q, c):
            pl.when(s_cond)(cp.wait_send)
            pl.when(r_cond)(cp.wait_recv)
    for done in placed[:2]:
        done()
    dm = lambda m: dsec2.at[m]

    def one(m, _):
        he[...] = dot_nt(ge[m], WO[0])

        def a(i, _):
            r = pl.ds(pl.multiple_of(i * 64 + HALO, 16), 64)
            u, h = lax.div(i, 2), lax.rem(i, 2)

            def store(j, v):
                v = v.astype(BF)
                dme[r, cols(j)] = v.astype(F32)
                dsec2[m, u, h, :, cols(j)] = v

            norm_gelu_back(view(mixed1, m, r), view(he, r), nh, gm(0, 1), bm(0, 1), dgbm.at[2], dgbm.at[3], hold, store)
            return 0

        lax.fori_loop(0, seg // 64, a, 0)
        for edge in (0, rows - HALO):
            r = pl.ds(edge, HALO)
            pos = positions(base - HALO, edge, HALO)
            within = jnp.logical_and(pos >= 0, pos < 4 * seg)

            def store(j, v):
                dme[r, cols(j)] = jnp.where(within, v, 0.0).astype(BF).astype(F32)

            norm_gelu_back(view(mixed1, m, r), view(he, r), nh, gm(0, 1), bm(0, 1), None, None, hold.at[:, pl.ds(0, HALO)], store)
        ring.step(7 + 3 * m)
        acc = None
        for k in range(5):
            term = dot_nt(dme[pl.ds(HALO - DIL * (k - 2), seg)].astype(BF), WC[0, k])
            acc = term if acc is None else acc + term
        he[pl.ds(0, seg)] = acc

        def b(i, _):
            r = pl.ds(pl.multiple_of(i * 64, 64), 64)
            pos = positions(base, i * 64, 64)
            ds = lambda j: jnp.where(pos < lengths[2 * c + m], he[r, cols(j)], 0.0)
            norm_gelu_back(view(hidden1, m, r), ds, nh, gm(0, 0), bm(0, 0), dgbm.at[0], dgbm.at[1], hold, put(dpad, 4 * m + i, pl.ds(0, 64)))
            return 0

        lax.fori_loop(0, seg // 64, b, 0)
        ring.step(8 + 3 * m)
        dhm = dh(m)[...].reshape(seg, H)
        he[pl.ds(0, seg)] = dot_nt(dhm, WI[0, :H])
        me[...] = dot_nt(dhm, WI[0, H:])

        def e(i, size):
            r, x = pl.ds(i, size), pl.ds(i + HALO, size)
            df = lambda j: he[r, cols(j)] if j < nh else me[r, cols(j - nh)]

            def store(j, v):
                og[m, r, cols(j)] = (ge[m, x, cols(j)].astype(F32) + v).astype(BF)

            norm_gelu_back(view(xe, m, x), df, nd, gi(0), bi(0), dgbi.at[0], dgbi.at[1], hold, store)

        chunks(seg, e)
        ring.step(9 + 3 * m)
        return 0

    lax.fori_loop(0, 2, one, 0)
    placed.append(place(3, og, igr, 0))
    low = UNITS
    t1 = flat(third1[...])
    for j in range(2):
        put_grad(DG, c, low + OUT0, dot_tn(t1, flat(ge[:, pl.ds(HALO, seg), pl.ds(j * H, H)])), nh * j)
    ring.step(13)
    d1 = flat(dsec2[...])
    for k in range(5):
        for m in range(2):
            third2[m] = sec1[m, pl.ds(8 + HALO + DIL * (k - 2), seg)].astype(BF).reshape(2, 2, 64, H)
        put_grad(DG, c, low + CONV0 + k * 100, dot_tn(flat(third2[...]), d1))
        if k in (1, 3):
            ring.step(14 + k // 2)
    put_grad(DG, c, low + IN0, dot_tn(flat(first1[:, pl.ds(HALO, seg)]), dpad[pl.ds(0, 8)].reshape(2 * seg, H)))
    extra(low + EXTRA0, False)

    def rest(t, _):
        ring.step(t)
        return 0

    if ring.live:
        lax.fori_loop(16, ring.iters, rest, 0)
        ring.finish()
        cnt[...] = DG[0, pl.ds(EXTRA0, 3)]
    else:
        everything = pltpu.make_async_copy(DG, total, pw.at[0])
        everything.start()
        everything.wait()
        cnt[...] = jnp.zeros_like(cnt)
    for done in placed[2:]:
        done()
    for i, dst in ((0, act), (1, igr)):
        remote(og, dst.at[pl.ds(2 * (1 - c), 2)], ps.at[0], pr.at[i], peer).wait_recv()
    for cp in sends:
        cp.wait_send()
    for cond, _, cp in halos:
        pl.when(cond)(cp.wait_send)


def run(ring, lengths, inputs, cot, params, w_in, conv_w, w_out, dec, code):
    seg, D, H = inputs.shape[2], inputs.shape[3], w_in.shape[2]
    rows = seg + 2 * HALO
    any_, vm, sm = (pl.BlockSpec(memory_space=s) for s in (pl.ANY, pltpu.VMEM, pltpu.SMEM))
    sh = jax.ShapeDtypeStruct
    dma = lambda *s: pltpu.SemaphoreType.DMA(s)
    part = (2, 2, 2, 64, H)
    scratch = [((2, D, H), BF), ((2, 5, H, H), BF), ((2, H, D), BF), ((2, 8, D), F32), ((2, rows, D), BF), ((2, seg, D), BF),
               ((2, seg, D), BF), ((2, rows, D), BF), ((2, seg, H), F32), ((2, rows + 16, H), F32), ((2, rows, H), F32), ((2, seg, H), BF),
               ((2, seg, D), BF), ((2, seg, H), F32), (part, BF), (part, BF), ((12, 64, H), BF), ((8, 64, H), BF), ((8, 64, H), BF),
               ((12, 64, H), BF), (part, BF), (part, BF), ((2, seg, D), BF), ((2, rows, D), BF), ((2 * rows, H), F32), ((seg, H), F32),
               ((2, 64, D), F32), ((2, 8, D), F32), ((4, 8, H), F32), ((8, 128), F32), ((2, 2 * UNITS, 16, 128), BF)]
    return pl.pallas_call(
        functools.partial(whole, ring=ring),
        out_shape=[sh((4, seg, D), BF), sh((4, seg, D), BF), sh((2, ring.out_units, 16, 128), BF), sh((3, 16, 128), BF)],
        in_specs=[sm] + [any_] * 6 + [vm, vm],
        out_specs=[any_, any_, any_, vm],
        scratch_shapes=[pltpu.VMEM(s, d) for s, d in scratch]
        + [dma(8), dma(8), dma(8), dma(2, 2), dma(2, 2), dma(4), dma(4, 4), dma(4, 4), dma(4), dma(2, 2), dma(2, 2), dma(4), dma(2), dma(4)]
        + ring.scratch(),
        compiler_params=pltpu.CompilerParams(collective_id=1, has_side_effects=True, vmem_limit_bytes=63 * 2**20 + 2**19),
    )(lengths, inputs, cot, params, w_in, conv_w, w_out, dec, code)


def unpack_kernel(conv, w_out, w_in, extra, cnt, s_conv, s_out, s_in, gi, bi, gm, bm, counts):
    H = s_conv.shape[-1]
    for j in range(5):
        for h in range(2):
            s_conv[0, 0, pl.ds(h * 320, 320), cols(j)] = conv[h, pl.ds(j * 20, 20)].reshape(320, 128).astype(F32)
    for j in range(2):
        for h in range(2):
            s_out[0, pl.ds(h * 320, 320), cols(j)] = w_out[h, pl.ds(j * 20, 20)].reshape(320, 128).astype(F32)
    for h in range(2):
        s_in[0, pl.ds(h * 640, 640)] = w_in[h].reshape(640, 128).astype(F32)

    @pl.when(pl.program_id(0) == 0)
    def _():
        small = extra[0, pl.ds(0, 3)].reshape(48, 128).astype(F32)
        for j in range(10):
            gi[:, cols(j)] = small[j : j + 1]
            bi[:, cols(j)] = small[10 + j : 11 + j]
        for k in range(2):
            for j in range(5):
                gm[0, pl.ds(k, 1), cols(j)] = small[20 + 10 * k + j : 21 + 10 * k + j]
                bm[0, pl.ds(k, 1), cols(j)] = small[25 + 10 * k + j : 26 + 10 * k + j]
        counts[...] = cnt[...].reshape(48, 128)[40:41].astype(F32)


def unpack(total, cnt, D, H):
    def spec(units, first, moves=1):
        return pl.BlockSpec(tuple(pl.Element(n) for n in (2, units, 16, 128)), lambda k: (0, first + units * k * moves, 0, 0))

    def full(*s):
        return pl.BlockSpec(s, lambda k: (0,) * len(s))

    sh = lambda *s: jax.ShapeDtypeStruct(s, F32)
    return pl.pallas_call(
        unpack_kernel,
        grid=(5,),
        out_shape=[sh(1, 5, H, H), sh(1, H, D), sh(1, D, H), sh(1, D), sh(1, D), sh(1, 2, H), sh(1, 2, H), sh(1, 128)],
        in_specs=[spec(100, CONV0), spec(40, OUT0), spec(40, IN0), spec(36, EXTRA0, 0), full(3, 16, 128)],
        out_specs=[pl.BlockSpec((1, 1, H, H), lambda k: (0, k, 0, 0)), pl.BlockSpec((1, H, 256), lambda k: (0, 0, k)),
                   pl.BlockSpec((1, D, 128), lambda k: (0, 0, k)), full(1, D), full(1, D), full(1, 2, H), full(1, 2, H), full(1, 128)],
        compiler_params=pltpu.CompilerParams(vmem_limit_bytes=60 * 2**20),
    )(total, total, total, total, cnt)


def body(inputs, lengths, mlm_mask, true_types, gain_in, bias_in, gain_mid, bias_mid, w_in, conv_w, w_out, decoder, cotangent, fast):
    D, H = inputs.shape[3], w_in.shape[2]
    params = jnp.concatenate([gain_in, bias_in, gain_mid.reshape(1, D), bias_mid.reshape(1, D), jnp.zeros((4, D), BF)]).astype(F32)
    dec = jnp.pad(decoder, ((0, 0), (0, 128 - decoder.shape[1])))
    code = jnp.where(mlm_mask[:, 0] == 1, true_types[:, 0], -1)[..., None]
    ring = Ring(PIECES, PLANE_UNITS, Z_UNITS) if fast else NoRing(PIECES, PLANE_UNITS + Z_UNITS)
    act, igr, total, cnt = run(ring, lengths[:, 0], inputs, cotangent, params, w_in, conv_w, w_out, dec, code)
    if not fast:
        c = lax.axis_index("section")
        halves = jnp.where(c == 0, total, total[::-1])
        g_two, g_one = halves[:, :UNITS], halves[:, UNITS:]
        own, other = jnp.where(c == 0, g_one, g_two), jnp.where(c == 0, g_two, g_one)
        got = lax.ppermute(other, "section", [(0, 1), (1, 0)])
        total = lax.psum(own.astype(F32) + got.astype(F32), ("dp", "seq")).astype(BF)
        cnt = lax.psum(g_two[0, EXTRA0 : EXTRA0 + 3].astype(F32), ("section", "dp", "seq")).astype(BF)
    s_conv, s_out, s_in, s_gi, s_bi, s_gm, s_bm, s_cnt = unpack(total, cnt, D, H)
    return (act[None, :, None], igr[None, :, None], s_gi, s_bi, s_gm, s_bm, s_in, s_conv, s_out, s_cnt[0, : decoder.shape[1]])


def solution(mesh):
    fast = mesh.shape["dp"] == 4 and mesh.shape["seq"] == 4
    return jax.shard_map(
        functools.partial(body, fast=fast),
        mesh=mesh,
        in_specs=(P(None, "dp", "seq", None), P(None, "dp"), P(None, "dp", "seq"), P(None, "dp", "seq"), P("section", None),
                  P("section", None), P("section", None, None), P("section", None, None), P("section", None, None),
                  P("section", None, None, None), P("section", None, None), P(), P(None, "dp", "seq", None)),
        out_specs=(P("section", None, "dp", "seq", None), P("section", None, "dp", "seq", None), P("section", None), P("section", None),
                   P("section", None, None), P("section", None, None), P("section", None, None), P("section", None, None, None),
                   P("section", None, None), P()),
        check_vma=False,
    )
```

```python
import functools

import jax
import jax.numpy as jnp
from jax import lax
from jax.experimental import pallas as pl
from jax.experimental.pallas import tpu as pltpu
from jax.sharding import PartitionSpec as P


EPS = 1e-05
BF, F32 = jnp.bfloat16, jnp.float32
MESH = pl.DeviceIdType.MESH
G0 = 0.7978845608028654
G1 = 0.044715
DIL = 2
HALO = 16
OUT0, CONV0, IN0, EXTRA0, UNITS = 0, 200, 700, 900, 936
PIECES, PLANE_UNITS, Z_UNITS, SLOTS = 9, 80, 24, 7


def dot(a, b):
    return lax.dot_general(a, b, (((1,), (0,)), ((), ())), preferred_element_type=F32)


def dot_nt(a, b):
    return lax.dot_general(a, b, (((1,), (1,)), ((), ())), preferred_element_type=F32)


def dot_tn(a, b):
    return lax.dot_general(a, b, (((0,), (0,)), ((), ())), preferred_element_type=F32)


def chunks(rows, fn, size=None):
    size = size or (96 if rows % 96 == 0 else 64)

    def one(i, _):
        fn(pl.multiple_of(i * size, size), size)
        return 0

    lax.fori_loop(0, rows // size, one, 0)


def cols(j):
    return pl.ds(j * 128, 128)


def stats(load, n):
    total = load(0)
    for j in range(1, n):
        total = total + load(j)
    mean = jnp.sum(total, axis=-1, keepdims=True) * (1.0 / (128 * n))
    square = None
    for j in range(n):
        d = load(j) - mean
        square = d * d if square is None else square + d * d
    var = jnp.sum(square, axis=-1, keepdims=True) * (1.0 / (128 * n))
    return mean, lax.rsqrt(var + EPS)


def norm_gelu(load, n, gain, shift, store):
    mean, rstd = stats(load, n)
    for j in range(n):
        u = (load(j) - mean) * rstd * gain(j) + shift(j)
        t = jnp.tanh(u * (G0 + (G0 * G1) * (u * u)))
        h = 0.5 * u
        store(j, h + h * t)


def fold(v):
    rows, width = v.shape
    return jnp.sum(v.reshape(rows // 8, 8, width), axis=0)


def norm_gelu_back(load, dy, n, gain, shift, dgain, dshift, hold, store):
    mean, rstd = stats(load, n)
    s1 = s2 = None
    for j in range(n):
        g = gain(j)
        hat = (load(j) - mean) * rstd
        u = hat * g + shift(j)
        w = u * u
        t = jnp.tanh(u * (G0 + (G0 * G1) * w))
        slope = 0.5 + 0.5 * t + u * (1.0 - t * t) * (0.5 * G0 + (1.5 * G0 * G1) * w)
        du = dy(j) * slope
        if dgain is not None:
            dgain[:, cols(j)] += fold(du * hat)
            dshift[:, cols(j)] += fold(du)
        dh = du * g
        hold[0, :, cols(j)] = hat
        hold[1, :, cols(j)] = dh
        p = dh * hat
        s1 = dh if s1 is None else s1 + dh
        s2 = p if s2 is None else s2 + p
    m1 = jnp.sum(s1, axis=-1, keepdims=True) * (1.0 / (128 * n))
    m2 = jnp.sum(s2, axis=-1, keepdims=True) * (1.0 / (128 * n))
    for j in range(n):
        store(j, rstd * (hold[1, :, cols(j)] - m1 - hold[0, :, cols(j)] * m2))


def norm_gelu_both(load, dy, n, gain, shift, dgain, dshift, hold, store, store_back):
    mean, rstd = stats(load, n)
    s1 = s2 = None
    for j in range(n):
        g = gain(j)
        hat = (load(j) - mean) * rstd
        u = hat * g + shift(j)
        w = u * u
        t = jnp.tanh(u * (G0 + (G0 * G1) * w))
        half = 0.5 + 0.5 * t
        store(j, u * half)
        slope = half + u * (1.0 - t * t) * (0.5 * G0 + (1.5 * G0 * G1) * w)
        du = dy(j) * slope
        dgain[:, cols(j)] += fold(du * hat)
        dshift[:, cols(j)] += fold(du)
        dh = du * g
        hold[0, :, cols(j)] = hat
        hold[1, :, cols(j)] = dh
        p = dh * hat
        s1 = dh if s1 is None else s1 + dh
        s2 = p if s2 is None else s2 + p
    m1 = jnp.sum(s1, axis=-1, keepdims=True) * (1.0 / (128 * n))
    m2 = jnp.sum(s2, axis=-1, keepdims=True) * (1.0 / (128 * n))
    for j in range(n):
        store_back(j, rstd * (hold[1, :, cols(j)] - m1 - hold[0, :, cols(j)] * m2))


def row(ref, k):
    return lambda j: ref[pl.ds(k, 1), cols(j)]


def view(ref, *at):
    return lambda j: ref[(*at, cols(j))].astype(F32)


def put_grad(DG, c, unit, value, col0=0):
    m, n = value.shape
    per = m // 32
    value = value.astype(BF)
    for j in range(n // 128):
        block = value[:, j * 128 : (j + 1) * 128].reshape(m // 16, 16, 128)
        for h in range(2):
            DG[lax.rem(h + c, 2), pl.ds(unit + (col0 + j) * per, per)] = block[h * per : (h + 1) * per]


def put(ref, *at):
    def store(j, v):
        ref[(*at, cols(j))] = v.astype(ref.dtype)

    return store


def positions(first, i, size):
    return first + i + lax.broadcasted_iota(jnp.int32, (size, 1), 0)


class Ring:
    KINDS = ("D", "P1", "P2", "PZ1", "PZ2", "PT1", "PT2", "PT3", "G1", "G2", "Q1", "Q2", "X1", "X2", "X3", "X4", "QT1", "QT2", "QT3", "F")

    def __init__(self, N, PU, QU):
        self.N, self.PU, self.QU, self.U = N, PU, QU, PU + QU
        self.out_units, self.live = N * self.U, True

    def scratch(self):
        PU, QU, U = self.PU, self.QU, self.U
        b = lambda u, n=SLOTS - 1: pltpu.VMEM((n, u, 16, 128), BF)
        sems = pltpu.SemaphoreType.DMA((len(self.KINDS), 2 * self.N))
        return [b(U, 4), b(PU // 2), b(PU // 4), b(PU // 4, SLOTS), b(PU // 8), b(QU, SLOTS), b(QU // 2, SLOTS), b(QU // 4), b(QU // 8), b(PU // 4), b(QU // 8),
                sems, sems]

    def bind(self, DG, out, RD, RP1, RP2, RZ1, RZ2, RQ1, RQ2, RX1, RX2, TQ, TX, ss, rs):
        N, PU, QU, U, ds = self.N, self.PU, self.QU, self.U, pl.ds
        c, z, q = lax.axis_index("section"), lax.axis_index("dp"), lax.axis_index("seq")
        xb, yb = lax.rem(q, 2), lax.div(q, 2)
        f, s = jnp.where(c == 0, xb, yb), jnp.where(c == 0, yb, xb)
        qx, qy = yb * 2 + 1 - xb, (1 - yb) * 2 + xb
        n1 = (c, z, jnp.where(c == 0, qx, qy))
        n2 = (c, z, jnp.where(c == 0, qy, qx))
        side = lax.div(z, 2)
        near, farc = side, 1 - side
        zp = (c, side * 2 + 1 - lax.rem(z, 2), q)
        far = (c, 3 - z, q)
        peer = (1 - c, z, q)
        inner = jnp.logical_or(z == 1, z == 2)
        outer = jnp.logical_not(inner)
        order = {k: i for i, k in enumerate(self.KINDS)}

        def cp(k, i, src, dst, dev):
            return remote(src, dst, ss.at[order[k], i], rs.at[order[k], i], dev)

        def add(dst, *terms):
            acc = terms[0][...].astype(F32)
            for t in terms[1:]:
                acc = acc + t[...].astype(F32)
            dst[...] = acc.astype(BF)

        def phys(i):
            return jnp.where(i < 4, i + 2, jnp.where(i < 6, i - 4, i))

        def part(i, start=0, size=U):
            return DG.at[0, ds(phys(i) * U + start, size)]

        H, Q4, E8 = PU // 2, PU // 4, PU // 8
        h, h2, h4 = QU // 2, QU // 4, QU // 8
        pq = lambda a, b: ((2 * a + b) * Q4, Q4)
        pch = lambda k: ((2 * f + s) * Q4 + k * E8, E8)
        tch = lambda k: ds(k * E8, E8)
        qn = lambda k: (PU + k * h, h)
        qhalf = lambda k, a: (PU + k * h + a * h2, h2)
        qquart = lambda k, a, b: (PU + k * h + (2 * a + b) * h4, h4)
        k8 = lambda i: lax.rem(i, SLOTS)
        k7 = lambda i: lax.rem(i, SLOTS - 1)
        rd = lambda i: RD.at[lax.rem(i, 4)]
        same = lambda k, at, dev: (lambda i: cp(k, i, part(i, *at), part(i, *at), dev))
        C = dict(
            D=lambda i: cp("D", i, DG.at[1, ds(phys(i) * U, U)], rd(i), peer),
            P1=lambda i: cp("P1", i, part(i, (1 - f) * H, H), RP1.at[k7(i)], n1),
            P2=lambda i: cp("P2", i, part(i, *pq(f, 1 - s)), RP2.at[k7(i)], n2),
            PZ1=lambda i: cp("PZ1", i, part(i, *pq(f, s)), RZ1.at[k8(i)], zp),
            PZ2=lambda i: cp("PZ2", i, part(i, *pch(farc)), RZ2.at[k7(i)], far),
            PT1=lambda i: cp("PT1", i, TQ.at[k7(i), tch(near)], TQ.at[k7(i), tch(near)], far),
            PT2=lambda i: cp("PT2", i, TQ.at[k7(i), tch(near)], TQ.at[k7(i), tch(near)], zp),
            PT3=lambda i: cp("PT3", i, TQ.at[k7(i), tch(farc)], TQ.at[k7(i), tch(farc)], zp),
            G1=same("G1", pq(f, s), n2),
            G2=same("G2", (f * H, H), n1),
            Q1=lambda i: cp("Q1", i, part(i, PU, QU), RQ1.at[k8(i)], zp),
            Q2=lambda i: cp("Q2", i, part(i, *qn(farc)), RQ2.at[k8(i)], far),
            X1=lambda i: cp("X1", i, part(i, *qhalf(near, 1 - f)), RX1.at[k7(i)], n1),
            X2=lambda i: cp("X2", i, part(i, *qquart(near, f, 1 - s)), RX2.at[k7(i)], n2),
            X3=lambda i: cp("X3", i, part(i, *qquart(near, f, s)), TX.at[k7(i)], n2),
            X4=same("X4", qhalf(near, f), n1),
            QT1=same("QT1", qn(near), far),
            QT2=same("QT2", qn(near), zp),
            QT3=same("QT3", qn(farc), zp),
        )

        def final(i, start):
            to = out.at[c, ds(phys(i) * U - jnp.where(i < N, 0, N * U), U)]
            there, here = cp("F", i, part(i), to, peer), pltpu.make_async_copy(part(i), to, ss.at[order["F"], i])
            both_ways(jnp.where(i < N, 1, 0) == c, here.start if start else here.wait, there.start if start else there.wait_send)

        def on_inner(fn):
            pl.when(inner)(fn)

        def on_outer(fn):
            pl.when(outer)(fn)

        def s0(i):
            C["D"](i).start()

        def s1(i):
            C["D"](i).wait()
            add(part(i), part(i), rd(i))
            C["P1"](i).start()
            on_outer(lambda: C["Q1"](i).start())

        def s2(i):
            @on_inner
            def _():
                C["Q1"](i).wait_recv()
                add(part(i, *qn(farc)), part(i, *qn(farc)), RQ1.at[k8(i), ds(farc * h, h)])
                C["Q2"](i).start()

            C["P1"](i).wait()
            add(part(i, f * H, H), part(i, f * H, H), RP1.at[k7(i)])
            C["P2"](i).start()
            on_outer(lambda: C["Q1"](i).wait_send())

        def s3(i):
            C["P2"](i).wait()
            add(part(i, *pq(f, s)), part(i, *pq(f, s)), RP2.at[k7(i)])
            on_outer(lambda: C["PZ1"](i).start())

            @on_inner
            def _():
                C["Q2"](i).wait()
                add(part(i, *qn(near)), part(i, *qn(near)), RQ1.at[k8(i), ds(near * h, h)], RQ2.at[k8(i)])
                C["X1"](i).start()

        def s4(i):
            @on_inner
            def _():
                C["PZ1"](i).wait_recv()
                add(part(i, *pch(farc)), part(i, *pch(farc)), RZ1.at[k8(i), tch(farc)])
                C["PZ2"](i).start()
                C["X1"](i).wait()
                add(part(i, *qhalf(near, f)), part(i, *qhalf(near, f)), RX1.at[k7(i)])
                C["X2"](i).start()

            on_outer(lambda: C["PZ1"](i).wait_send())

        def s5(i):
            @on_inner
            def _():
                C["PZ2"](i).wait()
                add(TQ.at[k7(i), tch(near)], part(i, *pch(near)), RZ1.at[k8(i), tch(near)], RZ2.at[k7(i)])
                C["PT1"](i).start()
                C["PT2"](i).start()
                C["X2"](i).wait()
                add(part(i, *qquart(near, f, s)), part(i, *qquart(near, f, s)), RX2.at[k7(i)])
                C["X3"](i).start()

        def s6(i):
            @on_inner
            def _():
                C["PT1"](i).wait()
                C["PT3"](i).start()
                C["X3"](i).wait()
                part(i, *qquart(near, f, 1 - s))[...] = TX[k7(i)]
                C["X4"](i).start()

        def s7(i):
            @on_outer
            def _():
                C["PT2"](i).wait_recv()
                C["PT3"](i).wait_recv()

            @on_inner
            def _():
                C["PT2"](i).wait_send()
                C["PT3"](i).wait_send()

            part(i, *pq(f, s))[...] = TQ[k7(i)]
            C["G1"](i).start()

            @on_inner
            def _():
                C["X4"](i).wait()
                C["QT1"](i).start()
                C["QT2"](i).start()

        def s8(i):
            C["G1"](i).wait()
            C["G2"](i).start()

            @on_inner
            def _():
                C["QT1"](i).wait()
                C["QT3"](i).start()

        def s9(i):
            C["G2"](i).wait()

            @on_outer
            def _():
                C["QT2"](i).wait_recv()
                C["QT3"](i).wait_recv()

            @on_inner
            def _():
                C["QT2"](i).wait_send()
                C["QT3"](i).wait_send()

            final(i, True)

        def s10(i):
            final(i, False)

        stages = (s0, s1, s2, s3, s4, s5, s6, s7, s8, s9, s10)

        def step(t):
            for k, stage in enumerate(stages):
                i = t - k
                pl.when(jnp.logical_and(i >= 0, i < 2 * N))(functools.partial(stage, i))

        def finish():
            def one(j, _):
                i = jnp.where(c == 1, j, j + N)
                cp("F", i, part(i), out.at[c, ds(0, U)], peer).wait_recv()
                return 0

            lax.fori_loop(0, N, one, 0)

        def barrier():
            b = pltpu.get_barrier_semaphore()
            for d in plane(c, z, q) + [zp]:
                pl.semaphore_signal(b, inc=1, device_id=d, device_id_type=MESH)

            @on_inner
            def _():
                pl.semaphore_signal(b, inc=1, device_id=far, device_id_type=MESH)
                pl.semaphore_wait(b, 9)

            on_outer(lambda: pl.semaphore_wait(b, 8))

        self.step, self.finish, self.barrier, self.iters = step, finish, barrier, 2 * N + len(stages) - 1


class NoRing:
    def __init__(self, N, U):
        self.N, self.U, self.live, self.out_units = N, U, False, 2 * N * U

    def scratch(self):
        return []

    def bind(self, *refs):
        pass

    def barrier(self):
        greet(plane(lax.axis_index("section"), lax.axis_index("dp"), lax.axis_index("seq")))

    def step(self, t):
        pass


def plane(c, z, q):
    out = []
    for i in range(1, 8):
        n = lax.rem(c * 4 + q + i, 8)
        out.append((lax.div(n, 4), z, lax.rem(n, 4)))
    return out


def greet(ids):
    barrier = pltpu.get_barrier_semaphore()
    for d in ids:
        pl.semaphore_signal(barrier, inc=1, device_id=d, device_id_type=MESH)
    pl.semaphore_wait(barrier, len(ids))


def remote(src, dst, ss, rs, dev):
    return pltpu.make_async_remote_copy(src_ref=src, dst_ref=dst, send_sem=ss, recv_sem=rs, device_id=dev, device_id_type=MESH)


def both_ways(cond, here, there):
    @pl.when(cond)
    def _():
        here()

    @pl.when(jnp.logical_not(cond))
    def _():
        there()


class Spread:
    def __init__(self, c, z, q, ss, rs, ls):
        self.c, self.z, self.q, self.ss, self.rs, self.ls = c, z, q, ss, rs, ls

    def go(self, a, src, dst, m, start):
        c, z, q = self.c, self.z, self.q
        for h in range(2):
            s, d, j = src.at[m, :, h], dst(q), 2 * m + h
            far = remote(s, d, self.ss.at[a, j], self.rs.at[a, q], (jnp.int32(h), z, 2 * c + m))
            near = pltpu.make_async_copy(s, d, self.ls.at[a])
            both_ways(jnp.logical_and(h == c, 2 * c + m == q), near.start if start else near.wait, far.start if start else far.wait_send)

    def arrive(self, a, src, dst):
        c, z, q = self.c, self.z, self.q
        fc = lax.div(q, 2)
        for p in range(4):
            @pl.when(jnp.logical_not(jnp.logical_and(c == fc, p == q)))
            def _():
                remote(src.at[0, :, 0], dst(p), self.ss.at[a, 0], self.rs.at[a, p], (fc, z, jnp.int32(p))).wait_recv()

    def back(self, a, src, dst, p, start):
        c, z, q = self.c, self.z, self.q
        tc, slot = lax.div(q, 2), lax.rem(q, 2)
        s, d = src, dst.at[slot, :, c]
        far = remote(s, d, self.ss.at[a, p], self.rs.at[a, 2 * slot + c], (tc, z, jnp.int32(p)))
        near = pltpu.make_async_copy(s, d, self.ls.at[a])
        both_ways(jnp.logical_and(tc == c, p == q), near.start if start else near.wait, far.start if start else far.wait_send)

    def back_arrive(self, a, src, dst, m):
        c, z, q = self.c, self.z, self.q
        for h in range(2):
            @pl.when(jnp.logical_not(jnp.logical_and(h == c, 2 * c + m == q)))
            def _():
                remote(src.at[pl.ds(0, 2)], dst.at[m, :, h], self.ss.at[a, 0], self.rs.at[a, 2 * m + h], (jnp.int32(h), z, 2 * c + m)).wait_recv()


def edges(ref, m, seg, ss, rs, z, q, c):
    before = remote(ref.at[m, pl.ds(HALO, HALO)], ref.at[m, pl.ds(HALO + seg, HALO)], ss.at[0, m], rs.at[0, m], (c, z, q - 1))
    after = remote(ref.at[m, pl.ds(seg, HALO)], ref.at[m, pl.ds(0, HALO)], ss.at[1, m], rs.at[1, m], (c, z, q + 1))
    return ((q > 0, q < 3, before), (q < 3, q > 0, after))


def whole(lengths, inputs, cot_all, w_in, conv_w, w_out, gain_in, bias_in, gain_mid, bias_mid, dec, mask, types, act, igr, total, cnt,
          WI, WC, WO, PR, xe, cot, out1, first1, hidden1, sec1, mixed1, third1, first2, hidden2, sec2, dth2, sp, dthr, dpad,
          third2, dsec2, og, ge, hd, hold, dgbi, dgbm, counts, DG,
          ws, wr, wl, xs, xr, xl, ss, rs, ls, gs, gr, ps, pr, pw, *ring_refs, ring):
    c, z, q = lax.axis_index("section"), lax.axis_index("dp"), lax.axis_index("seq")
    peer = (1 - c, z, q)
    seg, D = cot.shape[1:]
    H = mixed1.shape[2]
    nd, nh = D // 128, H // 128
    rows = seg + 2 * HALO
    base = q * seg
    he, dme, me = hd.at[pl.ds(0, rows)], hd.at[pl.ds(rows, rows)], hd.at[pl.ds(rows, seg)]
    ring.bind(DG, total, *ring_refs)
    own = [pltpu.make_async_copy(inputs.at[2 * c + m, 0], xe.at[m, pl.ds(HALO, seg)], xl.at[m]) for m in range(2)]
    own += [pltpu.make_async_copy(cot_all.at[2 * c + m, 0], cot.at[m], xl.at[2 + m]) for m in range(2)]
    mats = [(PR.at[c], PR.at[c]), (w_in.at[0], WI.at[c])] + [(conv_w.at[0, k], WC.at[c, k]) for k in range(5)] + [(w_out.at[0], WO.at[c])]
    loads = [pltpu.make_async_copy(s, d, wl.at[i]) for i, (s, d) in enumerate(mats) if i > 0]
    for cp in own[:2] + loads + own[2:]:
        cp.start()
    PR[c, pl.ds(4, 4)] = jnp.zeros((4, D), F32)
    PR[c, pl.ds(0, 1)] = gain_in[...].astype(F32)
    PR[c, pl.ds(1, 1)] = bias_in[...].astype(F32)
    for k in range(2):
        PR[c, pl.ds(2, 1), pl.ds(k * H, H)] = gain_mid[0, pl.ds(k, 1)].astype(F32)
        PR[c, pl.ds(3, 1), pl.ds(k * H, H)] = bias_mid[0, pl.ds(k, 1)].astype(F32)
    ring.barrier()
    sends = [remote(s, d, ws.at[i], wr.at[i], peer) for i, (s, d) in enumerate(mats)]
    halos = []
    for m in range(2):
        x = inputs.at[2 * c + m, 0]
        halos.append((q > 0, q < 3, remote(x.at[pl.ds(0, HALO)], xe.at[m, pl.ds(HALO + seg, HALO)], xs.at[0, m], xr.at[0, m], (c, z, q - 1))))
        halos.append((q < 3, q > 0, remote(x.at[pl.ds(seg - HALO, HALO)], xe.at[m, pl.ds(0, HALO)], xs.at[1, m], xr.at[1, m], (c, z, q + 1))))
    for cond, _, cp in halos:
        pl.when(cond)(cp.start)
    sends[0].start()

    @pl.when(c == 0)
    def _():
        for cp in sends[1:]:
            cp.start()

    @pl.when(c == 1)
    def _():
        for cp in sends[7:] + sends[1:7]:
            cp.start()

    @pl.when(q == 0)
    def _():
        xe[:, pl.ds(0, HALO)] = jnp.zeros((2, HALO, D), BF)
        ge[:, pl.ds(0, HALO)] = jnp.zeros((2, HALO, D), BF)

    @pl.when(q == 3)
    def _():
        xe[:, pl.ds(HALO + seg, HALO)] = jnp.zeros((2, HALO, D), BF)
        ge[:, pl.ds(HALO + seg, HALO)] = jnp.zeros((2, HALO, D), BF)

    def have(i, layer):
        both_ways(c == layer, loads[i - 1].wait, sends[i].wait_recv)

    for ref in (dgbi, dgbm, counts):
        ref[...] = jnp.zeros_like(ref)
    zero = jnp.zeros((2, 64, H), BF)
    for ref in (sp, dpad):
        ref[pl.ds(0, 2)] = zero
        ref[pl.ds(10, 2)] = zero
    sec1[:, pl.ds(0, 8)] = jnp.zeros((2, 8, H), F32)
    sec1[:, pl.ds(rows + 8, 8)] = jnp.zeros((2, 8, H), F32)
    spread = Spread(c, z, q, ss, rs, ls)
    sp_at = lambda p: sp.at[pl.ds(2 + 2 * p, 2)]
    dthr_at = lambda p: dthr.at[pl.ds(2 * p, 2)]
    gi, bi = lambda l: row(PR.at[l], 0), lambda l: row(PR.at[l], 1)
    gm = lambda l, k: (lambda j: PR[l, pl.ds(2, 1), cols(k * nh + j)])
    bm = lambda l, k: (lambda j: PR[l, pl.ds(3, 1), cols(k * nh + j)])

    sends[0].wait_recv()
    for m in range(2):
        own[m].wait()
    for _, cond, cp in halos:
        pl.when(cond)(cp.wait_recv)

    def first_norm(m, _):
        def a(i, size):
            r = pl.ds(i, size)
            norm_gelu(view(xe, m, r), nd, gi(0), bi(0), put(first1, m, r))

        chunks(rows, a)
        return 0

    lax.fori_loop(0, 2, first_norm, 0)
    for m in range(2):
        own[2 + m].wait()
    have(7, 1)

    def third_grad(m, _):
        dth2[m] = dot_nt(cot[m], WO[1]).astype(BF).reshape(2, 2, 64, H)
        spread.go(1, dth2, dthr_at, m, True)
        return 0

    lax.fori_loop(0, 2, third_grad, 0)
    have(1, 0)

    def second_norm(m, _):
        he[...] = dot(first1[m], WI[0])
        hidden1[m] = he[pl.ds(HALO, seg)]

        def b(i, size):
            pos = positions(base - HALO, i, size)
            keep = jnp.logical_and(pos >= 0, pos < lengths[2 * c + m])

            def store(j, v):
                sec1[m, pl.ds(i + 8, size), cols(j)] = jnp.where(keep, v, 0.0).astype(BF).astype(F32)

            norm_gelu(view(he, pl.ds(i, size)), nh, gm(0, 0), bm(0, 0), store)

        chunks(rows, b)
        return 0

    lax.fori_loop(0, 2, second_norm, 0)
    for k in range(5):
        have(2 + k, 0)

    def forward(m, _):
        acc = None
        for k in range(5):
            term = dot(sec1[m, pl.ds(8 + DIL * (k - 2), rows)].astype(BF), WC[0, k])
            acc = term if acc is None else acc + term
        mixed1[m] = acc

        def e(i, size):
            norm_gelu(view(mixed1, m, pl.ds(i + HALO, size)), nh, gm(0, 1), bm(0, 1), put(third1, m, pl.ds(i, size)))

        chunks(seg, e)

        @pl.when(m == 0)
        def _():
            have(7, 0)

        he[pl.ds(0, seg)] = dot(third1[m], WO[0, :, :H])
        me[...] = dot(third1[m], WO[0, :, H:])

        def d(i, size):
            r = pl.ds(i, size)
            for j in range(nd):
                br = he[r, cols(j)] if j < nh else me[r, cols(j - nh)]
                out1[m, r, cols(j)] = (xe[m, pl.ds(i + HALO, size), cols(j)].astype(F32) + br).astype(BF)
            norm_gelu(view(out1, m, r), nd, gi(1), bi(1), put(first2, m, r))

        chunks(seg, d)

        @pl.when(m == 0)
        def _():
            have(1, 1)

        hidden2[m] = dot(first2[m], WI[1])

        def f(jj, _):
            i = pl.multiple_of(jj * 64, 64)
            pos = positions(base, i, 64)

            def store(j, v):
                sec2[m, lax.div(jj, 2), lax.rem(jj, 2), :, cols(j)] = jnp.where(pos < lengths[2 * c + m], v, 0.0).astype(BF)

            norm_gelu(view(hidden2, m, pl.ds(i, 64)), nh, gm(1, 0), bm(1, 0), store)
            return 0

        lax.fori_loop(0, seg // 64, f, 0)
        spread.go(0, sec2, sp_at, m, True)
        return 0

    lax.fori_loop(0, 2, forward, 0)
    for k in range(5):
        have(2 + k, 1)

    def place(i, src, dst, layer):
        to = dst.at[pl.ds(2 * c, 2)]
        here, there = pltpu.make_async_copy(src, to, pw.at[i]), remote(src, to, ps.at[i], pr.at[i // 2], peer)
        both_ways(c == layer, here.start, there.start)
        return lambda: both_ways(c == layer, here.wait, there.wait_send)

    placed = [place(0, out1, act, 0)]
    for m in range(2):
        spread.go(0, sec2, sp_at, m, False)
    spread.arrive(0, sec2, sp_at)

    def conv(r, _):
        acc = None
        for k in range(5):
            term = dot(sp[pl.ds(4 * r + k, 4)].reshape(256, H), WC[1, k])
            acc = term if acc is None else acc + term
        hd[pl.ds(256 * r, 256)] = acc
        return 0

    lax.fori_loop(0, 2, conv, 0)
    for m in range(2):
        spread.go(1, dth2, dthr_at, m, False)
    spread.arrive(1, dth2, dthr_at)

    def mid(i, _):
        every = pl.ds(0, 64)
        norm_gelu_both(view(hd, pl.ds(pl.multiple_of(64 * i, 64), 64)), view(dthr, i, every), nh, gm(1, 1), bm(1, 1), dgbm.at[2], dgbm.at[3], hold,
                       put(dth2, lax.div(i, 4), lax.rem(lax.div(i, 2), 2), lax.rem(i, 2), every), put(dpad, i + 2, every))
        return 0

    lax.fori_loop(0, 8, mid, 0)
    for p in range(4):
        spread.back(2, dth2.at[p // 2, p % 2], third2, p, True)
    dm2 = dpad[pl.ds(2, 8)].reshape(512, H)

    def conv_grads(k, _):
        put_grad(DG, c, CONV0 + k * 100, dot_tn(sp[pl.ds(k, 8)].reshape(512, H), dm2))

        @pl.when(k % 2 == 1)
        def _():
            ring.step(lax.div(k, 2))

        return 0

    lax.fori_loop(0, 5, conv_grads, 0)

    def conv_back(r, _):
        acc = None
        for k in range(5):
            term = dot_nt(dpad[pl.ds(4 * r + 4 - k, 4)].reshape(256, H), WC[1, k])
            acc = term if acc is None else acc + term
        dthr[pl.ds(4 * r, 4)] = acc.astype(BF).reshape(4, 64, H)
        return 0

    lax.fori_loop(0, 2, conv_back, 0)
    for p in range(4):
        spread.back(3, dthr.at[pl.ds(2 * p, 2)], dsec2, p, True)
    ring.step(2)
    for p in range(4):
        spread.back(2, dth2.at[p // 2, p % 2], third2, p, False)
    for m in range(2):
        spread.back_arrive(2, dthr, third2, m)
    flat = lambda v: v.reshape(2 * seg, v.shape[-1])
    t2 = flat(third2[...])
    for j in range(2):
        put_grad(DG, c, OUT0, dot_tn(t2, flat(cot[:, :, pl.ds(j * H, H)])), nh * j)
    ring.step(3)
    for p in range(4):
        spread.back(3, dthr.at[pl.ds(2 * p, 2)], dsec2, p, False)
    for m in range(2):
        spread.back_arrive(3, dthr, dsec2, m)
    dh = lambda m: dpad.at[pl.ds(4 * m, 4)]

    def two(m, _):
        def b(i, _):
            pos = positions(base, i * 64, 64)
            u, h = lax.div(i, 2), lax.rem(i, 2)
            ds = lambda j: jnp.where(pos < lengths[2 * c + m], dsec2[m, u, h, :, cols(j)].astype(F32), 0.0)
            norm_gelu_back(view(hidden2, m, pl.ds(pl.multiple_of(i * 64, 64), 64)), ds, nh, gm(1, 0), bm(1, 0), dgbm.at[0], dgbm.at[1], hold,
                           put(dpad, 4 * m + i, pl.ds(0, 64)))
            return 0

        lax.fori_loop(0, seg // 64, b, 0)
        dhm = dh(m)[...].reshape(seg, H)
        he[pl.ds(0, seg)] = dot_nt(dhm, WI[1, :H])
        me[...] = dot_nt(dhm, WI[1, H:])

        def e(i, size):
            r = pl.ds(i, size)
            df = lambda j: he[r, cols(j)] if j < nh else me[r, cols(j - nh)]

            def store(j, v):
                ge[m, pl.ds(i + HALO, size), cols(j)] = (cot[m, r, cols(j)].astype(F32) + v).astype(BF)

            norm_gelu_back(view(out1, m, r), df, nd, gi(1), bi(1), dgbi.at[0], dgbi.at[1], hold, store)

        chunks(seg, e)
        for cond, _, cp in edges(ge, m, seg, gs, gr, z, q, c):
            pl.when(cond)(cp.start)
        ring.step(4 + m)
        return 0

    lax.fori_loop(0, 2, two, 0)
    placed.append(place(2, ge.at[:, pl.ds(HALO, seg)], igr, 1))
    put_grad(DG, c, IN0, dot_tn(flat(first2[...]), dpad[pl.ds(0, 8)].reshape(2 * seg, H)))

    def extra(first_unit, with_counts):
        flat_rows = [dgbi[k, :, cols(j)] for k in range(2) for j in range(nd)]
        flat_rows += [dgbm[k, :, cols(j)] for k in range(4) for j in range(nh)]
        small = [jnp.sum(v, axis=0, keepdims=True) for v in flat_rows]
        if with_counts:
            small.append(jnp.pad(jnp.sum(counts[...], axis=0, keepdims=True), ((0, 0), (0, 128 - classes))))
        size = UNITS - EXTRA0
        small.append(jnp.zeros((48 - len(small), 128), F32))
        block = jnp.concatenate(small, axis=0).astype(BF).reshape(3, 16, 128)
        for h in range(2):
            DG[h, pl.ds(first_unit, 3)] = block
            DG[h, pl.ds(first_unit + 3, size - 3)] = jnp.zeros((size - 3, 16, 128), BF)

    extra(EXTRA0, False)
    ring.step(6)
    for ref in (dgbi, dgbm):
        ref[...] = jnp.zeros_like(ref)
    for m in range(2):
        for s_cond, r_cond, cp in edges(ge, m, seg, gs, gr, z, q, c):
            pl.when(s_cond)(cp.wait_send)
            pl.when(r_cond)(cp.wait_recv)
    dm = lambda m: dsec2.at[m]

    def one(m, _):
        he[...] = dot_nt(ge[m], WO[0])

        def a(i, _):
            r = pl.ds(pl.multiple_of(i * 64 + HALO, 16), 64)
            u, h = lax.div(i, 2), lax.rem(i, 2)

            def store(j, v):
                v = v.astype(BF)
                dme[r, cols(j)] = v.astype(F32)
                dsec2[m, u, h, :, cols(j)] = v

            norm_gelu_back(view(mixed1, m, r), view(he, r), nh, gm(0, 1), bm(0, 1), dgbm.at[2], dgbm.at[3], hold, store)
            return 0

        lax.fori_loop(0, seg // 64, a, 0)
        for edge in (0, rows - HALO):
            r = pl.ds(edge, HALO)
            pos = positions(base - HALO, edge, HALO)
            within = jnp.logical_and(pos >= 0, pos < 4 * seg)

            def store(j, v):
                dme[r, cols(j)] = jnp.where(within, v, 0.0).astype(BF).astype(F32)

            norm_gelu_back(view(mixed1, m, r), view(he, r), nh, gm(0, 1), bm(0, 1), None, None, hold.at[:, pl.ds(0, HALO)], store)
        acc = None
        for k in range(5):
            term = dot_nt(dme[pl.ds(HALO - DIL * (k - 2), seg)].astype(BF), WC[0, k])
            acc = term if acc is None else acc + term
        he[pl.ds(0, seg)] = acc

        def b(i, _):
            r = pl.ds(pl.multiple_of(i * 64, 64), 64)
            pos = positions(base, i * 64, 64)
            ds = lambda j: jnp.where(pos < lengths[2 * c + m], he[r, cols(j)], 0.0)
            norm_gelu_back(view(hidden1, m, r), ds, nh, gm(0, 0), bm(0, 0), dgbm.at[0], dgbm.at[1], hold, put(dpad, 4 * m + i, pl.ds(0, 64)))
            return 0

        lax.fori_loop(0, seg // 64, b, 0)
        ring.step(7 + m)
        return 0

    lax.fori_loop(0, 2, one, 0)
    low = UNITS
    t1 = flat(third1[...])
    for j in range(2):
        put_grad(DG, c, low + OUT0, dot_tn(t1, flat(ge[:, pl.ds(HALO, seg), pl.ds(j * H, H)])), nh * j)
    ring.step(9)
    d1 = flat(dsec2[...])
    for k in range(5):
        for m in range(2):
            sec2[m] = sec1[m, pl.ds(8 + HALO + DIL * (k - 2), seg)].astype(BF).reshape(2, 2, 64, H)
        put_grad(DG, c, low + CONV0 + k * 100, dot_tn(flat(sec2[...]), d1))
        if k in (1, 3):
            ring.step(10 + k // 2)
    put_grad(DG, c, low + IN0, dot_tn(flat(first1[:, pl.ds(HALO, seg)]), dpad[pl.ds(0, 8)].reshape(2 * seg, H)))
    ring.step(12)
    classes = dec.shape[0]
    labels = lax.broadcasted_iota(jnp.int32, (1, classes), 1).astype(F32)

    def two_out(m, _):
        t = third2[m].reshape(seg, H)
        he[pl.ds(0, seg)] = dot(t, WO[1, :, :H])
        me[...] = dot(t, WO[1, :, H:])

        def a(i, size):
            r = pl.ds(i, size)
            for j in range(nd):
                br = he[r, cols(j)] if j < nh else me[r, cols(j - nh)]
                og[m, r, cols(j)] = (out1[m, r, cols(j)].astype(F32) + br).astype(BF)

        chunks(seg, a)
        logits = dot_nt(og[m], dec[...])
        ex = jnp.exp(logits - jnp.max(logits, axis=-1, keepdims=True))
        probs = ex / jnp.sum(ex, axis=-1, keepdims=True)
        pos = base + lax.broadcasted_iota(jnp.int32, (1, seg), 1)
        live = jnp.logical_and(mask[2 * c + m] == 1, pos < lengths[2 * c + m])
        code = jnp.where(live, types[2 * c + m], -1).astype(F32)
        code = jnp.broadcast_to(code, (128, seg)).T[:, :classes]
        counts[...] += fold(jnp.where(code == labels, probs, 0.0))
        ring.step(13 + m)
        return 0

    lax.fori_loop(0, 2, two_out, 0)
    placed.append(place(1, og, act, 1))
    placed[-1]()

    def one_in(m, _):
        dhm = dh(m)[...].reshape(seg, H)
        he[pl.ds(0, seg)] = dot_nt(dhm, WI[0, :H])
        me[...] = dot_nt(dhm, WI[0, H:])
        ring.step(15 + m)

        def e(i, _):
            r, x = pl.ds(pl.multiple_of(i * 64, 64), 64), pl.ds(pl.multiple_of(i * 64 + HALO, 16), 64)
            df = lambda j: he[r, cols(j)] if j < nh else me[r, cols(j - nh)]

            def store(j, v):
                og[m, r, cols(j)] = (ge[m, x, cols(j)].astype(F32) + v).astype(BF)

            norm_gelu_back(view(xe, m, x), df, nd, gi(0), bi(0), dgbi.at[0], dgbi.at[1], hold, store)

            return 0

        lax.fori_loop(0, seg // 64, e, 0)
        return 0

    lax.fori_loop(0, 2, one_in, 0)
    placed.append(place(3, og, igr, 0))
    extra(low + EXTRA0, True)

    def rest(t, _):
        ring.step(t)
        return 0

    if ring.live:
        lax.fori_loop(17, ring.iters, rest, 0)
        ring.finish()
        cnt[...] = DG[0, pl.ds(UNITS + EXTRA0, 3)]
    else:
        everything = pltpu.make_async_copy(DG, total, pw.at[0])
        everything.start()
        everything.wait()
        cnt[...] = jnp.zeros_like(cnt)
    for i in (0, 1, 3):
        placed[i]()
    for i, dst in ((0, act), (1, igr)):
        remote(og, dst.at[pl.ds(2 * (1 - c), 2)], ps.at[0], pr.at[i], peer).wait_recv()
    for cp in sends:
        cp.wait_send()
    for cond, _, cp in halos:
        pl.when(cond)(cp.wait_send)


def run(ring, lengths, inputs, cot, w_in, conv_w, w_out, gain_in, bias_in, gain_mid, bias_mid, dec, mask, types):
    seg, D, H = inputs.shape[2], inputs.shape[3], w_in.shape[2]
    rows = seg + 2 * HALO
    any_, vm, sm = (pl.BlockSpec(memory_space=s) for s in (pl.ANY, pltpu.VMEM, pltpu.SMEM))
    sh = jax.ShapeDtypeStruct
    dma = lambda *s: pltpu.SemaphoreType.DMA(s)
    part = (2, 2, 2, 64, H)
    scratch = [((2, D, H), BF), ((2, 5, H, H), BF), ((2, H, D), BF), ((2, 8, D), F32), ((2, rows, D), BF), ((2, seg, D), BF),
               ((2, seg, D), BF), ((2, rows, D), BF), ((2, seg, H), F32), ((2, rows + 16, H), F32), ((2, rows, H), F32), ((2, seg, H), BF),
               ((2, seg, D), BF), ((2, seg, H), F32), (part, BF), (part, BF), ((12, 64, H), BF), ((8, 64, H), BF),
               ((12, 64, H), BF), (part, BF), (part, BF), ((2, seg, D), BF), ((2, rows, D), BF), ((2 * rows, H), F32),
               ((2, 64, D), F32), ((2, 8, D), F32), ((4, 8, H), F32), ((8, dec.shape[0]), F32), ((2, 2 * UNITS, 16, 128), BF)]
    return pl.pallas_call(
        functools.partial(whole, ring=ring),
        out_shape=[sh((4, seg, D), BF), sh((4, seg, D), BF), sh((2, ring.out_units, 16, 128), BF), sh((3, 16, 128), BF)],
        in_specs=[sm] + [any_] * 5 + [vm] * 7,
        out_specs=[any_, any_, any_, vm],
        scratch_shapes=[pltpu.VMEM(s, d) for s, d in scratch]
        + [dma(8), dma(8), dma(8), dma(2, 2), dma(2, 2), dma(4), dma(4, 4), dma(4, 4), dma(4), dma(2, 2), dma(2, 2), dma(4), dma(2), dma(4)]
        + ring.scratch(),
        compiler_params=pltpu.CompilerParams(collective_id=1, has_side_effects=True, vmem_limit_bytes=63 * 2**20 + 2**19),
    )(lengths, inputs, cot, w_in, conv_w, w_out, gain_in, bias_in, gain_mid, bias_mid, dec, mask, types)


def unpack_kernel(conv, w_out, w_in, extra, cnt, s_conv, s_out, s_in, gi, bi, gm, bm, counts):
    H = s_conv.shape[-1]
    for j in range(5):
        for h in range(2):
            s_conv[0, 0, pl.ds(h * 320, 320), cols(j)] = conv[h, pl.ds(j * 20, 20)].reshape(320, 128).astype(F32)
    for j in range(2):
        for h in range(2):
            s_out[0, pl.ds(h * 320, 320), cols(j)] = w_out[h, pl.ds(j * 20, 20)].reshape(320, 128).astype(F32)
    for h in range(2):
        s_in[0, pl.ds(h * 640, 640)] = w_in[h].reshape(640, 128).astype(F32)

    @pl.when(pl.program_id(0) == 0)
    def _():
        small = extra[0, pl.ds(0, 3)].reshape(48, 128).astype(F32)
        for j in range(10):
            gi[:, cols(j)] = small[j : j + 1]
            bi[:, cols(j)] = small[10 + j : 11 + j]
        for k in range(2):
            for j in range(5):
                gm[0, pl.ds(k, 1), cols(j)] = small[20 + 10 * k + j : 21 + 10 * k + j]
                bm[0, pl.ds(k, 1), cols(j)] = small[25 + 10 * k + j : 26 + 10 * k + j]
        counts[...] = cnt[...].reshape(48, 128)[40, : counts.shape[0]].astype(F32)


def unpack(total, cnt, D, H, classes):
    def spec(units, first, moves=1):
        return pl.BlockSpec(tuple(pl.Element(n) for n in (2, units, 16, 128)), lambda k: (0, first + units * k * moves, 0, 0))

    def full(*s):
        return pl.BlockSpec(s, lambda k: (0,) * len(s))

    sh = lambda *s: jax.ShapeDtypeStruct(s, F32)
    return pl.pallas_call(
        unpack_kernel,
        grid=(5,),
        out_shape=[sh(1, 5, H, H), sh(1, H, D), sh(1, D, H), sh(1, D), sh(1, D), sh(1, 2, H), sh(1, 2, H), sh(classes)],
        in_specs=[spec(100, CONV0), spec(40, OUT0), spec(40, IN0), spec(36, EXTRA0, 0), full(3, 16, 128)],
        out_specs=[pl.BlockSpec((1, 1, H, H), lambda k: (0, k, 0, 0)), pl.BlockSpec((1, H, 256), lambda k: (0, 0, k)),
                   pl.BlockSpec((1, D, 128), lambda k: (0, 0, k)), full(1, D), full(1, D), full(1, 2, H), full(1, 2, H), full(classes)],
        compiler_params=pltpu.CompilerParams(vmem_limit_bytes=60 * 2**20),
    )(total, total, total, total, cnt)


def body(inputs, lengths, mlm_mask, true_types, gain_in, bias_in, gain_mid, bias_mid, w_in, conv_w, w_out, decoder, cotangent, fast):
    D, H = inputs.shape[3], w_in.shape[2]
    ring = Ring(PIECES, PLANE_UNITS, Z_UNITS) if fast else NoRing(PIECES, PLANE_UNITS + Z_UNITS)
    act, igr, total, cnt = run(
        ring, lengths[:, 0], inputs, cotangent, w_in, conv_w, w_out, gain_in, bias_in, gain_mid, bias_mid, decoder.T, mlm_mask, true_types)
    if not fast:
        c = lax.axis_index("section")
        halves = jnp.where(c == 0, total, total[::-1])
        g_two, g_one = halves[:, :UNITS], halves[:, UNITS:]
        own, other = jnp.where(c == 0, g_one, g_two), jnp.where(c == 0, g_two, g_one)
        got = lax.ppermute(other, "section", [(0, 1), (1, 0)])
        total = lax.psum(own.astype(F32) + got.astype(F32), ("dp", "seq")).astype(BF)
        cnt = lax.psum(g_one[0, EXTRA0 : EXTRA0 + 3].astype(F32), ("section", "dp", "seq")).astype(BF)
    s_conv, s_out, s_in, s_gi, s_bi, s_gm, s_bm, s_cnt = unpack(total, cnt, D, H, decoder.shape[1])
    return (act[None, :, None], igr[None, :, None], s_gi, s_bi, s_gm, s_bm, s_in, s_conv, s_out, s_cnt)


def solution(mesh):
    fast = mesh.shape["dp"] == 4 and mesh.shape["seq"] == 4
    return jax.shard_map(
        functools.partial(body, fast=fast),
        mesh=mesh,
        in_specs=(P(None, "dp", "seq", None), P(None, "dp"), P(None, "dp", "seq"), P(None, "dp", "seq"), P("section", None),
                  P("section", None), P("section", None, None), P("section", None, None), P("section", None, None),
                  P("section", None, None, None), P("section", None, None), P(), P(None, "dp", "seq", None)),
        out_specs=(P("section", None, "dp", "seq", None), P("section", None, "dp", "seq", None), P("section", None), P("section", None),
                   P("section", None, None), P("section", None, None), P("section", None, None), P("section", None, None, None),
                   P("section", None, None), P()),
        check_vma=False,
    )
```

```python
import functools

import jax
import jax.numpy as jnp
from jax import lax
from jax.experimental import pallas as pl
from jax.experimental.pallas import tpu as pltpu
from jax.sharding import PartitionSpec as P


EPS = 1e-05
BF, F32 = jnp.bfloat16, jnp.float32
MESH = pl.DeviceIdType.MESH
G0 = 0.7978845608028654
G1 = 0.044715
DIL = 2
HALO = 16
OUT0, CONV0, IN0, EXTRA0, UNITS = 0, 200, 700, 900, 936
PIECES, PLANE_UNITS, Z_UNITS, SLOTS = 9, 80, 24, 7


def dot(a, b):
    return lax.dot_general(a, b, (((1,), (0,)), ((), ())), preferred_element_type=F32)


def dot_nt(a, b):
    return lax.dot_general(a, b, (((1,), (1,)), ((), ())), preferred_element_type=F32)


def dot_tn(a, b):
    return lax.dot_general(a, b, (((0,), (0,)), ((), ())), preferred_element_type=F32)


def chunks(rows, fn, size=None, unroll=1):
    size = size or (96 if rows % 96 == 0 else 64)

    def one(i, _):
        fn(pl.multiple_of(i * size, size), size)
        return 0

    lax.fori_loop(0, rows // size, one, 0, unroll=unroll)


def cols(j):
    return pl.ds(j * 128, 128)


def stats(load, n):
    total = load(0)
    for j in range(1, n):
        total = total + load(j)
    mean = jnp.sum(total, axis=-1, keepdims=True) * (1.0 / (128 * n))
    square = None
    for j in range(n):
        d = load(j) - mean
        square = d * d if square is None else square + d * d
    var = jnp.sum(square, axis=-1, keepdims=True) * (1.0 / (128 * n))
    return mean, lax.rsqrt(var + EPS)


def norm_gelu(load, n, gain, shift, store):
    mean, rstd = stats(load, n)
    for j in range(n):
        u = (load(j) - mean) * rstd * gain(j) + shift(j)
        t = jnp.tanh(u * (G0 + (G0 * G1) * (u * u)))
        h = 0.5 * u
        store(j, h + h * t)


def fold(v):
    rows, width = v.shape
    return jnp.sum(v.reshape(rows // 8, 8, width), axis=0)


def norm_gelu_back(load, dy, n, gain, shift, dgain, dshift, hold, store):
    mean, rstd = stats(load, n)
    s1 = s2 = None
    for j in range(n):
        g = gain(j)
        hat = (load(j) - mean) * rstd
        u = hat * g + shift(j)
        w = u * u
        t = jnp.tanh(u * (G0 + (G0 * G1) * w))
        slope = 0.5 + 0.5 * t + u * (1.0 - t * t) * (0.5 * G0 + (1.5 * G0 * G1) * w)
        du = dy(j) * slope
        if dgain is not None:
            dgain[:, cols(j)] += fold(du * hat)
            dshift[:, cols(j)] += fold(du)
        dh = du * g
        hold[0, :, cols(j)] = hat
        hold[1, :, cols(j)] = dh
        p = dh * hat
        s1 = dh if s1 is None else s1 + dh
        s2 = p if s2 is None else s2 + p
    m1 = jnp.sum(s1, axis=-1, keepdims=True) * (1.0 / (128 * n))
    m2 = jnp.sum(s2, axis=-1, keepdims=True) * (1.0 / (128 * n))
    for j in range(n):
        store(j, rstd * (hold[1, :, cols(j)] - m1 - hold[0, :, cols(j)] * m2))


def norm_gelu_both(load, dy, n, gain, shift, dgain, dshift, hold, store, store_back):
    mean, rstd = stats(load, n)
    s1 = s2 = None
    for j in range(n):
        g = gain(j)
        hat = (load(j) - mean) * rstd
        u = hat * g + shift(j)
        w = u * u
        t = jnp.tanh(u * (G0 + (G0 * G1) * w))
        half = 0.5 + 0.5 * t
        store(j, u * half)
        slope = half + u * (1.0 - t * t) * (0.5 * G0 + (1.5 * G0 * G1) * w)
        du = dy(j) * slope
        dgain[:, cols(j)] += fold(du * hat)
        dshift[:, cols(j)] += fold(du)
        dh = du * g
        hold[0, :, cols(j)] = hat
        hold[1, :, cols(j)] = dh
        p = dh * hat
        s1 = dh if s1 is None else s1 + dh
        s2 = p if s2 is None else s2 + p
    m1 = jnp.sum(s1, axis=-1, keepdims=True) * (1.0 / (128 * n))
    m2 = jnp.sum(s2, axis=-1, keepdims=True) * (1.0 / (128 * n))
    for j in range(n):
        store_back(j, rstd * (hold[1, :, cols(j)] - m1 - hold[0, :, cols(j)] * m2))


def row(ref, k):
    return lambda j: ref[pl.ds(k, 1), cols(j)]


def view(ref, *at):
    return lambda j: ref[(*at, cols(j))].astype(F32)


def put_grad(DG, c, unit, value, col0=0):
    m, n = value.shape
    per = m // 32
    value = value.astype(BF)
    for j in range(n // 128):
        block = value[:, j * 128 : (j + 1) * 128].reshape(m // 16, 16, 128)
        for h in range(2):
            DG[lax.rem(h + c, 2), pl.ds(unit + (col0 + j) * per, per)] = block[h * per : (h + 1) * per]


def put(ref, *at):
    def store(j, v):
        ref[(*at, cols(j))] = v.astype(ref.dtype)

    return store


def positions(first, i, size):
    return first + i + lax.broadcasted_iota(jnp.int32, (size, 1), 0)


class Ring:
    KINDS = ("D", "P1", "P2", "PZ1", "PZ2", "PT1", "PT2", "PT3", "G1", "G2", "Q1", "Q2", "X1", "X2", "X3", "X4", "QT1", "QT2", "QT3", "F")

    def __init__(self, N, PU, QU):
        self.N, self.PU, self.QU, self.U = N, PU, QU, PU + QU
        self.out_units, self.live = N * self.U, True

    def scratch(self):
        PU, QU, U = self.PU, self.QU, self.U
        b = lambda u, n=SLOTS - 1: pltpu.VMEM((n, u, 16, 128), BF)
        sems = pltpu.SemaphoreType.DMA((len(self.KINDS), 2 * self.N))
        return [b(U, 4), b(PU // 2), b(PU // 4), b(PU // 4, SLOTS), b(PU // 8), b(QU, SLOTS), b(QU // 2, SLOTS), b(QU // 4), b(QU // 8), b(PU // 4), b(QU // 8),
                sems, sems]

    def bind(self, DG, out, RD, RP1, RP2, RZ1, RZ2, RQ1, RQ2, RX1, RX2, TQ, TX, ss, rs):
        N, PU, QU, U, ds = self.N, self.PU, self.QU, self.U, pl.ds
        c, z, q = lax.axis_index("section"), lax.axis_index("dp"), lax.axis_index("seq")
        xb, yb = lax.rem(q, 2), lax.div(q, 2)
        f, s = jnp.where(c == 0, xb, yb), jnp.where(c == 0, yb, xb)
        qx, qy = yb * 2 + 1 - xb, (1 - yb) * 2 + xb
        n1 = (c, z, jnp.where(c == 0, qx, qy))
        n2 = (c, z, jnp.where(c == 0, qy, qx))
        side = lax.div(z, 2)
        near, farc = side, 1 - side
        zp = (c, side * 2 + 1 - lax.rem(z, 2), q)
        far = (c, 3 - z, q)
        peer = (1 - c, z, q)
        inner = jnp.logical_or(z == 1, z == 2)
        outer = jnp.logical_not(inner)
        order = {k: i for i, k in enumerate(self.KINDS)}

        def cp(k, i, src, dst, dev):
            return remote(src, dst, ss.at[order[k], i], rs.at[order[k], i], dev)

        def add(dst, *terms):
            acc = terms[0][...].astype(F32)
            for t in terms[1:]:
                acc = acc + t[...].astype(F32)
            dst[...] = acc.astype(BF)

        def phys(i):
            return jnp.where(i < 4, i + 2, jnp.where(i < 6, i - 4, i))

        def part(i, start=0, size=U):
            return DG.at[0, ds(phys(i) * U + start, size)]

        H, Q4, E8 = PU // 2, PU // 4, PU // 8
        h, h2, h4 = QU // 2, QU // 4, QU // 8
        pq = lambda a, b: ((2 * a + b) * Q4, Q4)
        pch = lambda k: ((2 * f + s) * Q4 + k * E8, E8)
        tch = lambda k: ds(k * E8, E8)
        qn = lambda k: (PU + k * h, h)
        qhalf = lambda k, a: (PU + k * h + a * h2, h2)
        qquart = lambda k, a, b: (PU + k * h + (2 * a + b) * h4, h4)
        k8 = lambda i: lax.rem(i, SLOTS)
        k7 = lambda i: lax.rem(i, SLOTS - 1)
        rd = lambda i: RD.at[lax.rem(i, 4)]
        same = lambda k, at, dev: (lambda i: cp(k, i, part(i, *at), part(i, *at), dev))
        C = dict(
            D=lambda i: cp("D", i, DG.at[1, ds(phys(i) * U, U)], rd(i), peer),
            P1=lambda i: cp("P1", i, part(i, (1 - f) * H, H), RP1.at[k7(i)], n1),
            P2=lambda i: cp("P2", i, part(i, *pq(f, 1 - s)), RP2.at[k7(i)], n2),
            PZ1=lambda i: cp("PZ1", i, part(i, *pq(f, s)), RZ1.at[k8(i)], zp),
            PZ2=lambda i: cp("PZ2", i, part(i, *pch(farc)), RZ2.at[k7(i)], far),
            PT1=lambda i: cp("PT1", i, TQ.at[k7(i), tch(near)], TQ.at[k7(i), tch(near)], far),
            PT2=lambda i: cp("PT2", i, TQ.at[k7(i), tch(near)], TQ.at[k7(i), tch(near)], zp),
            PT3=lambda i: cp("PT3", i, TQ.at[k7(i), tch(farc)], TQ.at[k7(i), tch(farc)], zp),
            G1=same("G1", pq(f, s), n2),
            G2=same("G2", (f * H, H), n1),
            Q1=lambda i: cp("Q1", i, part(i, PU, QU), RQ1.at[k8(i)], zp),
            Q2=lambda i: cp("Q2", i, part(i, *qn(farc)), RQ2.at[k8(i)], far),
            X1=lambda i: cp("X1", i, part(i, *qhalf(near, 1 - f)), RX1.at[k7(i)], n1),
            X2=lambda i: cp("X2", i, part(i, *qquart(near, f, 1 - s)), RX2.at[k7(i)], n2),
            X3=lambda i: cp("X3", i, part(i, *qquart(near, f, s)), TX.at[k7(i)], n2),
            X4=same("X4", qhalf(near, f), n1),
            QT1=same("QT1", qn(near), far),
            QT2=same("QT2", qn(near), zp),
            QT3=same("QT3", qn(farc), zp),
        )

        def final(i, start):
            to = out.at[c, ds(phys(i) * U - jnp.where(i < N, 0, N * U), U)]
            there, here = cp("F", i, part(i), to, peer), pltpu.make_async_copy(part(i), to, ss.at[order["F"], i])
            both_ways(jnp.where(i < N, 1, 0) == c, here.start if start else here.wait, there.start if start else there.wait_send)

        def on_inner(fn):
            pl.when(inner)(fn)

        def on_outer(fn):
            pl.when(outer)(fn)

        def s0(i):
            C["D"](i).start()

        def s1(i):
            C["D"](i).wait()
            add(part(i), part(i), rd(i))
            C["P1"](i).start()
            on_outer(lambda: C["Q1"](i).start())

        def s2(i):
            @on_inner
            def _():
                C["Q1"](i).wait_recv()
                add(part(i, *qn(farc)), part(i, *qn(farc)), RQ1.at[k8(i), ds(farc * h, h)])
                C["Q2"](i).start()

            C["P1"](i).wait()
            add(part(i, f * H, H), part(i, f * H, H), RP1.at[k7(i)])
            C["P2"](i).start()
            on_outer(lambda: C["Q1"](i).wait_send())

        def s3(i):
            C["P2"](i).wait()
            add(part(i, *pq(f, s)), part(i, *pq(f, s)), RP2.at[k7(i)])
            on_outer(lambda: C["PZ1"](i).start())

            @on_inner
            def _():
                C["Q2"](i).wait()
                add(part(i, *qn(near)), part(i, *qn(near)), RQ1.at[k8(i), ds(near * h, h)], RQ2.at[k8(i)])
                C["X1"](i).start()

        def s4(i):
            @on_inner
            def _():
                C["PZ1"](i).wait_recv()
                add(part(i, *pch(farc)), part(i, *pch(farc)), RZ1.at[k8(i), tch(farc)])
                C["PZ2"](i).start()
                C["X1"](i).wait()
                add(part(i, *qhalf(near, f)), part(i, *qhalf(near, f)), RX1.at[k7(i)])
                C["X2"](i).start()

            on_outer(lambda: C["PZ1"](i).wait_send())

        def s5(i):
            @on_inner
            def _():
                C["PZ2"](i).wait()
                add(TQ.at[k7(i), tch(near)], part(i, *pch(near)), RZ1.at[k8(i), tch(near)], RZ2.at[k7(i)])
                C["PT1"](i).start()
                C["PT2"](i).start()
                C["X2"](i).wait()
                add(part(i, *qquart(near, f, s)), part(i, *qquart(near, f, s)), RX2.at[k7(i)])
                C["X3"](i).start()

        def s6(i):
            @on_inner
            def _():
                C["PT1"](i).wait()
                C["PT3"](i).start()
                C["X3"](i).wait()
                part(i, *qquart(near, f, 1 - s))[...] = TX[k7(i)]
                C["X4"](i).start()

        def s7(i):
            @on_outer
            def _():
                C["PT2"](i).wait_recv()
                C["PT3"](i).wait_recv()

            @on_inner
            def _():
                C["PT2"](i).wait_send()
                C["PT3"](i).wait_send()

            part(i, *pq(f, s))[...] = TQ[k7(i)]
            C["G1"](i).start()

            @on_inner
            def _():
                C["X4"](i).wait()
                C["QT1"](i).start()
                C["QT2"](i).start()

        def s8(i):
            C["G1"](i).wait()
            C["G2"](i).start()

            @on_inner
            def _():
                C["QT1"](i).wait()
                C["QT3"](i).start()

        def s9(i):
            C["G2"](i).wait()

            @on_outer
            def _():
                C["QT2"](i).wait_recv()
                C["QT3"](i).wait_recv()

            @on_inner
            def _():
                C["QT2"](i).wait_send()
                C["QT3"](i).wait_send()

            final(i, True)

        def s10(i):
            final(i, False)

        stages = (s0, s1, s2, s3, s4, s5, s6, s7, s8, s9, s10)

        def step(t):
            for k, stage in enumerate(stages):
                i = t - k
                pl.when(jnp.logical_and(i >= 0, i < 2 * N))(functools.partial(stage, i))

        def finish():
            def one(j, _):
                i = jnp.where(c == 1, j, j + N)
                cp("F", i, part(i), out.at[c, ds(0, U)], peer).wait_recv()
                return 0

            lax.fori_loop(0, N, one, 0)

        def barrier():
            b = pltpu.get_barrier_semaphore()
            for d in plane(c, z, q) + [zp]:
                pl.semaphore_signal(b, inc=1, device_id=d, device_id_type=MESH)

            @on_inner
            def _():
                pl.semaphore_signal(b, inc=1, device_id=far, device_id_type=MESH)
                pl.semaphore_wait(b, 9)

            on_outer(lambda: pl.semaphore_wait(b, 8))

        self.step, self.finish, self.barrier, self.iters = step, finish, barrier, 2 * N + len(stages) - 1


class NoRing:
    def __init__(self, N, U):
        self.N, self.U, self.live, self.out_units = N, U, False, 2 * N * U

    def scratch(self):
        return []

    def bind(self, *refs):
        pass

    def barrier(self):
        greet(plane(lax.axis_index("section"), lax.axis_index("dp"), lax.axis_index("seq")))

    def step(self, t):
        pass


def plane(c, z, q):
    out = []
    for i in range(1, 8):
        n = lax.rem(c * 4 + q + i, 8)
        out.append((lax.div(n, 4), z, lax.rem(n, 4)))
    return out


def greet(ids):
    barrier = pltpu.get_barrier_semaphore()
    for d in ids:
        pl.semaphore_signal(barrier, inc=1, device_id=d, device_id_type=MESH)
    pl.semaphore_wait(barrier, len(ids))


def remote(src, dst, ss, rs, dev):
    return pltpu.make_async_remote_copy(src_ref=src, dst_ref=dst, send_sem=ss, recv_sem=rs, device_id=dev, device_id_type=MESH)


def both_ways(cond, here, there):
    @pl.when(cond)
    def _():
        here()

    @pl.when(jnp.logical_not(cond))
    def _():
        there()


class Spread:
    def __init__(self, c, z, q, ss, rs, ls):
        self.c, self.z, self.q, self.ss, self.rs, self.ls = c, z, q, ss, rs, ls

    def go(self, a, src, dst, m, start):
        c, z, q = self.c, self.z, self.q
        for h in range(2):
            s, d, j = src.at[m, :, h], dst(q), 2 * m + h
            far = remote(s, d, self.ss.at[a, j], self.rs.at[a, q], (jnp.int32(h), z, 2 * c + m))
            near = pltpu.make_async_copy(s, d, self.ls.at[a])
            both_ways(jnp.logical_and(h == c, 2 * c + m == q), near.start if start else near.wait, far.start if start else far.wait_send)

    def arrive(self, a, src, dst):
        c, z, q = self.c, self.z, self.q
        fc = lax.div(q, 2)
        for p in range(4):
            @pl.when(jnp.logical_not(jnp.logical_and(c == fc, p == q)))
            def _():
                remote(src.at[0, :, 0], dst(p), self.ss.at[a, 0], self.rs.at[a, p], (fc, z, jnp.int32(p))).wait_recv()

    def back(self, a, src, dst, p, start):
        c, z, q = self.c, self.z, self.q
        tc, slot = lax.div(q, 2), lax.rem(q, 2)
        s, d = src, dst.at[slot, :, c]
        far = remote(s, d, self.ss.at[a, p], self.rs.at[a, 2 * slot + c], (tc, z, jnp.int32(p)))
        near = pltpu.make_async_copy(s, d, self.ls.at[a])
        both_ways(jnp.logical_and(tc == c, p == q), near.start if start else near.wait, far.start if start else far.wait_send)

    def back_arrive(self, a, src, dst, m):
        c, z, q = self.c, self.z, self.q
        for h in range(2):
            @pl.when(jnp.logical_not(jnp.logical_and(h == c, 2 * c + m == q)))
            def _():
                remote(src.at[pl.ds(0, 2)], dst.at[m, :, h], self.ss.at[a, 0], self.rs.at[a, 2 * m + h], (jnp.int32(h), z, 2 * c + m)).wait_recv()


def edges(ref, m, seg, ss, rs, z, q, c):
    before = remote(ref.at[m, pl.ds(HALO, HALO)], ref.at[m, pl.ds(HALO + seg, HALO)], ss.at[0, m], rs.at[0, m], (c, z, q - 1))
    after = remote(ref.at[m, pl.ds(seg, HALO)], ref.at[m, pl.ds(0, HALO)], ss.at[1, m], rs.at[1, m], (c, z, q + 1))
    return ((q > 0, q < 3, before), (q < 3, q > 0, after))


def whole(lengths, inputs, cot_all, w_in, conv_w, w_out, gain_in, bias_in, gain_mid, bias_mid, dec, mask, types, act, igr, total, cnt,
          WI, WC, WO, PR, xe, cot, out1, first1, hidden1, sec1, mixed1, third1, first2, hidden2, sec2, dth2, sp, dthr, dpad,
          third2, dsec2, og, ge, hd, hold, dgbi, dgbm, counts, DG,
          ws, wr, wl, xs, xr, xl, ss, rs, ls, gs, gr, ps, pr, pw, *ring_refs, ring):
    c, z, q = lax.axis_index("section"), lax.axis_index("dp"), lax.axis_index("seq")
    peer = (1 - c, z, q)
    seg, D = cot.shape[1:]
    H = mixed1.shape[2]
    nd, nh = D // 128, H // 128
    rows = seg + 2 * HALO
    base = q * seg
    he, dme, me = hd.at[pl.ds(0, rows)], hd.at[pl.ds(rows, rows)], hd.at[pl.ds(rows, seg)]
    ring.bind(DG, total, *ring_refs)
    own = [pltpu.make_async_copy(inputs.at[2 * c + m, 0], xe.at[m, pl.ds(HALO, seg)], xl.at[m]) for m in range(2)]
    own += [pltpu.make_async_copy(cot_all.at[2 * c + m, 0], cot.at[m], xl.at[2 + m]) for m in range(2)]
    mats = [(PR.at[c], PR.at[c]), (w_in.at[0], WI.at[c])] + [(conv_w.at[0, k], WC.at[c, k]) for k in range(5)] + [(w_out.at[0], WO.at[c])]
    loads = [pltpu.make_async_copy(s, d, wl.at[i]) for i, (s, d) in enumerate(mats) if i > 0]
    for cp in own[:2] + loads + own[2:]:
        cp.start()
    PR[c, pl.ds(4, 4)] = jnp.zeros((4, D), F32)
    PR[c, pl.ds(0, 1)] = gain_in[...].astype(F32)
    PR[c, pl.ds(1, 1)] = bias_in[...].astype(F32)
    for k in range(2):
        PR[c, pl.ds(2, 1), pl.ds(k * H, H)] = gain_mid[0, pl.ds(k, 1)].astype(F32)
        PR[c, pl.ds(3, 1), pl.ds(k * H, H)] = bias_mid[0, pl.ds(k, 1)].astype(F32)
    ring.barrier()
    sends = [remote(s, d, ws.at[i], wr.at[i], peer) for i, (s, d) in enumerate(mats)]
    halos = []
    for m in range(2):
        x = inputs.at[2 * c + m, 0]
        halos.append((q > 0, q < 3, remote(x.at[pl.ds(0, HALO)], xe.at[m, pl.ds(HALO + seg, HALO)], xs.at[0, m], xr.at[0, m], (c, z, q - 1))))
        halos.append((q < 3, q > 0, remote(x.at[pl.ds(seg - HALO, HALO)], xe.at[m, pl.ds(0, HALO)], xs.at[1, m], xr.at[1, m], (c, z, q + 1))))
    for cond, _, cp in halos:
        pl.when(cond)(cp.start)
    sends[0].start()

    @pl.when(c == 0)
    def _():
        for cp in sends[1:]:
            cp.start()

    @pl.when(c == 1)
    def _():
        for cp in sends[7:] + sends[1:7]:
            cp.start()

    @pl.when(q == 0)
    def _():
        xe[:, pl.ds(0, HALO)] = jnp.zeros((2, HALO, D), BF)
        ge[:, pl.ds(0, HALO)] = jnp.zeros((2, HALO, D), BF)

    @pl.when(q == 3)
    def _():
        xe[:, pl.ds(HALO + seg, HALO)] = jnp.zeros((2, HALO, D), BF)
        ge[:, pl.ds(HALO + seg, HALO)] = jnp.zeros((2, HALO, D), BF)

    def have(i, layer):
        both_ways(c == layer, loads[i - 1].wait, sends[i].wait_recv)

    for ref in (dgbi, dgbm, counts):
        ref[...] = jnp.zeros_like(ref)
    zero = jnp.zeros((2, 64, H), BF)
    for ref in (sp, dpad):
        ref[pl.ds(0, 2)] = zero
        ref[pl.ds(10, 2)] = zero
    sec1[:, pl.ds(0, 8)] = jnp.zeros((2, 8, H), F32)
    sec1[:, pl.ds(rows + 8, 8)] = jnp.zeros((2, 8, H), F32)
    spread = Spread(c, z, q, ss, rs, ls)
    sp_at = lambda p: sp.at[pl.ds(2 + 2 * p, 2)]
    dthr_at = lambda p: dthr.at[pl.ds(2 * p, 2)]
    gi, bi = lambda l: row(PR.at[l], 0), lambda l: row(PR.at[l], 1)
    gm = lambda l, k: (lambda j: PR[l, pl.ds(2, 1), cols(k * nh + j)])
    bm = lambda l, k: (lambda j: PR[l, pl.ds(3, 1), cols(k * nh + j)])

    sends[0].wait_recv()
    for m in range(2):
        own[m].wait()
    for _, cond, cp in halos:
        pl.when(cond)(cp.wait_recv)

    def first_norm(m, _):
        def a(i, size):
            r = pl.ds(i, size)
            norm_gelu(view(xe, m, r), nd, gi(0), bi(0), put(first1, m, r))

        chunks(rows, a, unroll=3)
        return 0

    lax.fori_loop(0, 2, first_norm, 0)
    for m in range(2):
        own[2 + m].wait()
    have(7, 1)

    def third_grad(m, _):
        dth2[m] = dot_nt(cot[m], WO[1]).astype(BF).reshape(2, 2, 64, H)
        spread.go(1, dth2, dthr_at, m, True)
        return 0

    lax.fori_loop(0, 2, third_grad, 0)
    have(1, 0)

    def second_norm(m, _):
        he[...] = dot(first1[m], WI[0])
        hidden1[m] = he[pl.ds(HALO, seg)]

        def b(i, size):
            pos = positions(base - HALO, i, size)
            keep = jnp.logical_and(pos >= 0, pos < lengths[2 * c + m])

            def store(j, v):
                sec1[m, pl.ds(i + 8, size), cols(j)] = jnp.where(keep, v, 0.0).astype(BF).astype(F32)

            norm_gelu(view(he, pl.ds(i, size)), nh, gm(0, 0), bm(0, 0), store)

        chunks(rows, b, unroll=3)
        return 0

    lax.fori_loop(0, 2, second_norm, 0)
    for k in range(5):
        have(2 + k, 0)

    def forward(m, _):
        acc = None
        for k in range(5):
            term = dot(sec1[m, pl.ds(8 + DIL * (k - 2), rows)].astype(BF), WC[0, k])
            acc = term if acc is None else acc + term
        mixed1[m] = acc

        def e(i, size):
            norm_gelu(view(mixed1, m, pl.ds(i + HALO, size)), nh, gm(0, 1), bm(0, 1), put(third1, m, pl.ds(i, size)))

        chunks(seg, e, unroll=4)

        @pl.when(m == 0)
        def _():
            have(7, 0)

        he[pl.ds(0, seg)] = dot(third1[m], WO[0, :, :H])
        me[...] = dot(third1[m], WO[0, :, H:])

        def d(i, size):
            r = pl.ds(i, size)
            for j in range(nd):
                br = he[r, cols(j)] if j < nh else me[r, cols(j - nh)]
                out1[m, r, cols(j)] = (xe[m, pl.ds(i + HALO, size), cols(j)].astype(F32) + br).astype(BF)
            norm_gelu(view(out1, m, r), nd, gi(1), bi(1), put(first2, m, r))

        chunks(seg, d, unroll=4)

        @pl.when(m == 0)
        def _():
            have(1, 1)

        hidden2[m] = dot(first2[m], WI[1])

        def f(jj, _):
            i = pl.multiple_of(jj * 64, 64)
            pos = positions(base, i, 64)

            def store(j, v):
                sec2[m, lax.div(jj, 2), lax.rem(jj, 2), :, cols(j)] = jnp.where(pos < lengths[2 * c + m], v, 0.0).astype(BF)

            norm_gelu(view(hidden2, m, pl.ds(i, 64)), nh, gm(1, 0), bm(1, 0), store)
            return 0

        lax.fori_loop(0, seg // 64, f, 0, unroll=4)
        spread.go(0, sec2, sp_at, m, True)
        return 0

    lax.fori_loop(0, 2, forward, 0)
    for k in range(5):
        have(2 + k, 1)

    def place(i, src, dst, layer):
        to = dst.at[pl.ds(2 * c, 2)]
        here, there = pltpu.make_async_copy(src, to, pw.at[i]), remote(src, to, ps.at[i], pr.at[i // 2], peer)
        both_ways(c == layer, here.start, there.start)
        return lambda: both_ways(c == layer, here.wait, there.wait_send)

    placed = [place(0, out1, act, 0)]
    for m in range(2):
        spread.go(0, sec2, sp_at, m, False)
    spread.arrive(0, sec2, sp_at)

    def conv(r, _):
        acc = None
        for k in range(5):
            term = dot(sp[pl.ds(4 * r + k, 4)].reshape(256, H), WC[1, k])
            acc = term if acc is None else acc + term
        hd[pl.ds(256 * r, 256)] = acc
        return 0

    lax.fori_loop(0, 2, conv, 0)
    for m in range(2):
        spread.go(1, dth2, dthr_at, m, False)
    spread.arrive(1, dth2, dthr_at)

    def mid(i, _):
        every = pl.ds(0, 64)
        norm_gelu_both(view(hd, pl.ds(pl.multiple_of(64 * i, 64), 64)), view(dthr, i, every), nh, gm(1, 1), bm(1, 1), dgbm.at[2], dgbm.at[3], hold,
                       put(dth2, lax.div(i, 4), lax.rem(lax.div(i, 2), 2), lax.rem(i, 2), every), put(dpad, i + 2, every))
        return 0

    lax.fori_loop(0, 8, mid, 0, unroll=4)
    for p in range(4):
        spread.back(2, dth2.at[p // 2, p % 2], third2, p, True)
    dm2 = dpad[pl.ds(2, 8)].reshape(512, H)

    def conv_grads(k, _):
        put_grad(DG, c, CONV0 + k * 100, dot_tn(sp[pl.ds(k, 8)].reshape(512, H), dm2))

        @pl.when(k % 2 == 1)
        def _():
            ring.step(lax.div(k, 2))

        return 0

    lax.fori_loop(0, 5, conv_grads, 0)

    def conv_back(r, _):
        acc = None
        for k in range(5):
            term = dot_nt(dpad[pl.ds(4 * r + 4 - k, 4)].reshape(256, H), WC[1, k])
            acc = term if acc is None else acc + term
        dthr[pl.ds(4 * r, 4)] = acc.astype(BF).reshape(4, 64, H)
        return 0

    lax.fori_loop(0, 2, conv_back, 0)
    for p in range(4):
        spread.back(3, dthr.at[pl.ds(2 * p, 2)], dsec2, p, True)
    ring.step(2)
    for p in range(4):
        spread.back(2, dth2.at[p // 2, p % 2], third2, p, False)
    for m in range(2):
        spread.back_arrive(2, dthr, third2, m)
    flat = lambda v: v.reshape(2 * seg, v.shape[-1])
    t2 = flat(third2[...])
    for j in range(2):
        put_grad(DG, c, OUT0, dot_tn(t2, flat(cot[:, :, pl.ds(j * H, H)])), nh * j)
    ring.step(3)
    for p in range(4):
        spread.back(3, dthr.at[pl.ds(2 * p, 2)], dsec2, p, False)
    for m in range(2):
        spread.back_arrive(3, dthr, dsec2, m)
    dh = lambda m: dpad.at[pl.ds(4 * m, 4)]

    def two(m, _):
        def b(i, _):
            pos = positions(base, i * 64, 64)
            u, h = lax.div(i, 2), lax.rem(i, 2)
            ds = lambda j: jnp.where(pos < lengths[2 * c + m], dsec2[m, u, h, :, cols(j)].astype(F32), 0.0)
            norm_gelu_back(view(hidden2, m, pl.ds(pl.multiple_of(i * 64, 64), 64)), ds, nh, gm(1, 0), bm(1, 0), dgbm.at[0], dgbm.at[1], hold,
                           put(dpad, 4 * m + i, pl.ds(0, 64)))
            return 0

        lax.fori_loop(0, seg // 64, b, 0, unroll=2)
        dhm = dh(m)[...].reshape(seg, H)
        he[pl.ds(0, seg)] = dot_nt(dhm, WI[1, :H])
        me[...] = dot_nt(dhm, WI[1, H:])

        def e(i, size):
            r = pl.ds(i, size)
            df = lambda j: he[r, cols(j)] if j < nh else me[r, cols(j - nh)]

            def store(j, v):
                ge[m, pl.ds(i + HALO, size), cols(j)] = (cot[m, r, cols(j)].astype(F32) + v).astype(BF)

            norm_gelu_back(view(out1, m, r), df, nd, gi(1), bi(1), dgbi.at[0], dgbi.at[1], hold, store)

        chunks(seg, e, unroll=2)
        for cond, _, cp in edges(ge, m, seg, gs, gr, z, q, c):
            pl.when(cond)(cp.start)
        ring.step(4 + m)
        return 0

    lax.fori_loop(0, 2, two, 0)
    placed.append(place(2, ge.at[:, pl.ds(HALO, seg)], igr, 1))
    put_grad(DG, c, IN0, dot_tn(flat(first2[...]), dpad[pl.ds(0, 8)].reshape(2 * seg, H)))

    def extra(first_unit, with_counts):
        flat_rows = [dgbi[k, :, cols(j)] for k in range(2) for j in range(nd)]
        flat_rows += [dgbm[k, :, cols(j)] for k in range(4) for j in range(nh)]
        small = [jnp.sum(v, axis=0, keepdims=True) for v in flat_rows]
        if with_counts:
            small.append(jnp.pad(jnp.sum(counts[...], axis=0, keepdims=True), ((0, 0), (0, 128 - classes))))
        size = UNITS - EXTRA0
        small.append(jnp.zeros((48 - len(small), 128), F32))
        block = jnp.concatenate(small, axis=0).astype(BF).reshape(3, 16, 128)
        for h in range(2):
            DG[h, pl.ds(first_unit, 3)] = block
            DG[h, pl.ds(first_unit + 3, size - 3)] = jnp.zeros((size - 3, 16, 128), BF)

    extra(EXTRA0, False)
    ring.step(6)
    for ref in (dgbi, dgbm):
        ref[...] = jnp.zeros_like(ref)
    for m in range(2):
        for s_cond, r_cond, cp in edges(ge, m, seg, gs, gr, z, q, c):
            pl.when(s_cond)(cp.wait_send)
            pl.when(r_cond)(cp.wait_recv)
    dm = lambda m: dsec2.at[m]

    def one(m, _):
        he[...] = dot_nt(ge[m], WO[0])

        def a(i, _):
            r = pl.ds(pl.multiple_of(i * 64 + HALO, 16), 64)
            u, h = lax.div(i, 2), lax.rem(i, 2)

            def store(j, v):
                v = v.astype(BF)
                dme[r, cols(j)] = v.astype(F32)
                dsec2[m, u, h, :, cols(j)] = v

            norm_gelu_back(view(mixed1, m, r), view(he, r), nh, gm(0, 1), bm(0, 1), dgbm.at[2], dgbm.at[3], hold, store)
            return 0

        lax.fori_loop(0, seg // 64, a, 0, unroll=2)
        for edge in (0, rows - HALO):
            r = pl.ds(edge, HALO)
            pos = positions(base - HALO, edge, HALO)
            within = jnp.logical_and(pos >= 0, pos < 4 * seg)

            def store(j, v):
                dme[r, cols(j)] = jnp.where(within, v, 0.0).astype(BF).astype(F32)

            norm_gelu_back(view(mixed1, m, r), view(he, r), nh, gm(0, 1), bm(0, 1), None, None, hold.at[:, pl.ds(0, HALO)], store)
        acc = None
        for k in range(5):
            term = dot_nt(dme[pl.ds(HALO - DIL * (k - 2), seg)].astype(BF), WC[0, k])
            acc = term if acc is None else acc + term
        he[pl.ds(0, seg)] = acc

        def b(i, _):
            r = pl.ds(pl.multiple_of(i * 64, 64), 64)
            pos = positions(base, i * 64, 64)
            ds = lambda j: jnp.where(pos < lengths[2 * c + m], he[r, cols(j)], 0.0)
            norm_gelu_back(view(hidden1, m, r), ds, nh, gm(0, 0), bm(0, 0), dgbm.at[0], dgbm.at[1], hold, put(dpad, 4 * m + i, pl.ds(0, 64)))
            return 0

        lax.fori_loop(0, seg // 64, b, 0, unroll=2)
        ring.step(7 + m)
        return 0

    lax.fori_loop(0, 2, one, 0)
    low = UNITS
    t1 = flat(third1[...])
    for j in range(2):
        put_grad(DG, c, low + OUT0, dot_tn(t1, flat(ge[:, pl.ds(HALO, seg), pl.ds(j * H, H)])), nh * j)
    ring.step(9)
    d1 = flat(dsec2[...])
    for k in range(5):
        for m in range(2):
            sec2[m] = sec1[m, pl.ds(8 + HALO + DIL * (k - 2), seg)].astype(BF).reshape(2, 2, 64, H)
        put_grad(DG, c, low + CONV0 + k * 100, dot_tn(flat(sec2[...]), d1))
        if k in (1, 3):
            ring.step(10 + k // 2)
    put_grad(DG, c, low + IN0, dot_tn(flat(first1[:, pl.ds(HALO, seg)]), dpad[pl.ds(0, 8)].reshape(2 * seg, H)))
    ring.step(12)
    classes = dec.shape[0]
    labels = lax.broadcasted_iota(jnp.int32, (1, classes), 1).astype(F32)

    def two_out(m, _):
        t = third2[m].reshape(seg, H)
        he[pl.ds(0, seg)] = dot(t, WO[1, :, :H])
        me[...] = dot(t, WO[1, :, H:])

        def a(i, size):
            r = pl.ds(i, size)
            for j in range(nd):
                br = he[r, cols(j)] if j < nh else me[r, cols(j - nh)]
                og[m, r, cols(j)] = (out1[m, r, cols(j)].astype(F32) + br).astype(BF)

        chunks(seg, a)
        logits = dot_nt(og[m], dec[...])
        ex = jnp.exp(logits - jnp.max(logits, axis=-1, keepdims=True))
        probs = ex / jnp.sum(ex, axis=-1, keepdims=True)
        pos = base + lax.broadcasted_iota(jnp.int32, (1, seg), 1)
        live = jnp.logical_and(mask[2 * c + m] == 1, pos < lengths[2 * c + m])
        code = jnp.where(live, types[2 * c + m], -1).astype(F32)
        code = jnp.broadcast_to(code, (128, seg)).T[:, :classes]
        counts[...] += fold(jnp.where(code == labels, probs, 0.0))
        ring.step(13 + m)
        return 0

    lax.fori_loop(0, 2, two_out, 0)
    placed.append(place(1, og, act, 1))
    placed[-1]()

    def one_in(m, _):
        dhm = dh(m)[...].reshape(seg, H)
        he[pl.ds(0, seg)] = dot_nt(dhm, WI[0, :H])
        me[...] = dot_nt(dhm, WI[0, H:])
        ring.step(15 + m)

        def e(i, _):
            r, x = pl.ds(pl.multiple_of(i * 64, 64), 64), pl.ds(pl.multiple_of(i * 64 + HALO, 16), 64)
            df = lambda j: he[r, cols(j)] if j < nh else me[r, cols(j - nh)]

            def store(j, v):
                og[m, r, cols(j)] = (ge[m, x, cols(j)].astype(F32) + v).astype(BF)

            norm_gelu_back(view(xe, m, x), df, nd, gi(0), bi(0), dgbi.at[0], dgbi.at[1], hold, store)

            return 0

        lax.fori_loop(0, seg // 64, e, 0)
        return 0

    lax.fori_loop(0, 2, one_in, 0)
    placed.append(place(3, og, igr, 0))
    extra(low + EXTRA0, True)

    def rest(t, _):
        ring.step(t)
        return 0

    if ring.live:
        lax.fori_loop(17, ring.iters, rest, 0)
        ring.finish()
        cnt[...] = DG[0, pl.ds(UNITS + EXTRA0, 3)]
    else:
        everything = pltpu.make_async_copy(DG, total, pw.at[0])
        everything.start()
        everything.wait()
        cnt[...] = jnp.zeros_like(cnt)
    for i in (0, 1, 3):
        placed[i]()
    for i, dst in ((0, act), (1, igr)):
        remote(og, dst.at[pl.ds(2 * (1 - c), 2)], ps.at[0], pr.at[i], peer).wait_recv()
    for cp in sends:
        cp.wait_send()
    for cond, _, cp in halos:
        pl.when(cond)(cp.wait_send)


def run(ring, lengths, inputs, cot, w_in, conv_w, w_out, gain_in, bias_in, gain_mid, bias_mid, dec, mask, types):
    seg, D, H = inputs.shape[2], inputs.shape[3], w_in.shape[2]
    rows = seg + 2 * HALO
    any_, vm, sm = (pl.BlockSpec(memory_space=s) for s in (pl.ANY, pltpu.VMEM, pltpu.SMEM))
    sh = jax.ShapeDtypeStruct
    dma = lambda *s: pltpu.SemaphoreType.DMA(s)
    part = (2, 2, 2, 64, H)
    scratch = [((2, D, H), BF), ((2, 5, H, H), BF), ((2, H, D), BF), ((2, 8, D), F32), ((2, rows, D), BF), ((2, seg, D), BF),
               ((2, seg, D), BF), ((2, rows, D), BF), ((2, seg, H), F32), ((2, rows + 16, H), F32), ((2, rows, H), F32), ((2, seg, H), BF),
               ((2, seg, D), BF), ((2, seg, H), F32), (part, BF), (part, BF), ((12, 64, H), BF), ((8, 64, H), BF),
               ((12, 64, H), BF), (part, BF), (part, BF), ((2, seg, D), BF), ((2, rows, D), BF), ((2 * rows, H), F32),
               ((2, 64, D), F32), ((2, 8, D), F32), ((4, 8, H), F32), ((8, dec.shape[0]), F32), ((2, 2 * UNITS, 16, 128), BF)]
    return pl.pallas_call(
        functools.partial(whole, ring=ring),
        out_shape=[sh((4, seg, D), BF), sh((4, seg, D), BF), sh((2, ring.out_units, 16, 128), BF), sh((3, 16, 128), BF)],
        in_specs=[sm] + [any_] * 5 + [vm] * 7,
        out_specs=[any_, any_, any_, vm],
        scratch_shapes=[pltpu.VMEM(s, d) for s, d in scratch]
        + [dma(8), dma(8), dma(8), dma(2, 2), dma(2, 2), dma(4), dma(4, 4), dma(4, 4), dma(4), dma(2, 2), dma(2, 2), dma(4), dma(2), dma(4)]
        + ring.scratch(),
        compiler_params=pltpu.CompilerParams(collective_id=1, has_side_effects=True, vmem_limit_bytes=63 * 2**20 + 2**19),
    )(lengths, inputs, cot, w_in, conv_w, w_out, gain_in, bias_in, gain_mid, bias_mid, dec, mask, types)


def unpack_kernel(conv, w_out, w_in, extra, cnt, act, igr, s_conv, s_out, s_in, gi, bi, gm, bm, counts, act_o, igr_o):
    act_o[...] = act[...]
    igr_o[...] = igr[...]
    for j in range(5):
        for h in range(2):
            s_conv[0, 0, pl.ds(h * 320, 320), cols(j)] = conv[h, pl.ds(j * 20, 20)].reshape(320, 128).astype(F32)
    for j in range(2):
        for h in range(2):
            s_out[0, pl.ds(h * 320, 320), cols(j)] = w_out[h, pl.ds(j * 20, 20)].reshape(320, 128).astype(F32)
    for h in range(2):
        s_in[0, pl.ds(h * 640, 640)] = w_in[h].reshape(640, 128).astype(F32)

    @pl.when(pl.program_id(0) == 0)
    def _():
        small = extra[0, pl.ds(0, 3)].reshape(48, 128).astype(F32)
        for j in range(10):
            gi[:, cols(j)] = small[j : j + 1]
            bi[:, cols(j)] = small[10 + j : 11 + j]
        for k in range(2):
            for j in range(5):
                gm[0, pl.ds(k, 1), cols(j)] = small[20 + 10 * k + j : 21 + 10 * k + j]
                bm[0, pl.ds(k, 1), cols(j)] = small[25 + 10 * k + j : 26 + 10 * k + j]
        counts[...] = cnt[...].reshape(48, 128)[40, : counts.shape[0]].astype(F32)


def unpack(total, cnt, act, igr, D, H, classes):
    def spec(units, first, moves=1):
        return pl.BlockSpec(tuple(pl.Element(n) for n in (2, units, 16, 128)), lambda k: (0, first + units * k * moves, 0, 0))

    def full(*s):
        return pl.BlockSpec(s, lambda k: (0,) * len(s))

    block = pl.BlockSpec((1, *act.shape[1:]), lambda k: (jnp.minimum(k, act.shape[0] - 1), 0, 0))
    sh = lambda *s: jax.ShapeDtypeStruct(s, F32)
    return pl.pallas_call(
        unpack_kernel,
        grid=(5,),
        out_shape=[sh(1, 5, H, H), sh(1, H, D), sh(1, D, H), sh(1, D), sh(1, D), sh(1, 2, H), sh(1, 2, H), sh(classes),
                   jax.ShapeDtypeStruct(act.shape, BF), jax.ShapeDtypeStruct(igr.shape, BF)],
        in_specs=[spec(100, CONV0), spec(40, OUT0), spec(40, IN0), spec(36, EXTRA0, 0), full(3, 16, 128), block, block],
        out_specs=[pl.BlockSpec((1, 1, H, H), lambda k: (0, k, 0, 0)), pl.BlockSpec((1, H, 256), lambda k: (0, 0, k)),
                   pl.BlockSpec((1, D, 128), lambda k: (0, 0, k)), full(1, D), full(1, D), full(1, 2, H), full(1, 2, H), full(classes), block, block],
        compiler_params=pltpu.CompilerParams(vmem_limit_bytes=60 * 2**20),
    )(total, total, total, total, cnt, act, igr)


def body(inputs, lengths, mlm_mask, true_types, gain_in, bias_in, gain_mid, bias_mid, w_in, conv_w, w_out, decoder, cotangent, fast):
    D, H = inputs.shape[3], w_in.shape[2]
    ring = Ring(PIECES, PLANE_UNITS, Z_UNITS) if fast else NoRing(PIECES, PLANE_UNITS + Z_UNITS)
    act, igr, total, cnt = run(
        ring, lengths[:, 0], inputs, cotangent, w_in, conv_w, w_out, gain_in, bias_in, gain_mid, bias_mid, decoder.T, mlm_mask, true_types)
    if not fast:
        c = lax.axis_index("section")
        halves = jnp.where(c == 0, total, total[::-1])
        g_two, g_one = halves[:, :UNITS], halves[:, UNITS:]
        own, other = jnp.where(c == 0, g_one, g_two), jnp.where(c == 0, g_two, g_one)
        got = lax.ppermute(other, "section", [(0, 1), (1, 0)])
        total = lax.psum(own.astype(F32) + got.astype(F32), ("dp", "seq")).astype(BF)
        cnt = lax.psum(g_one[0, EXTRA0 : EXTRA0 + 3].astype(F32), ("section", "dp", "seq")).astype(BF)
    s_conv, s_out, s_in, s_gi, s_bi, s_gm, s_bm, s_cnt, act, igr = unpack(total, cnt, act, igr, D, H, decoder.shape[1])
    return (act[None, :, None], igr[None, :, None], s_gi, s_bi, s_gm, s_bm, s_in, s_conv, s_out, s_cnt)


def solution(mesh):
    fast = mesh.shape["dp"] == 4 and mesh.shape["seq"] == 4
    return jax.shard_map(
        functools.partial(body, fast=fast),
        mesh=mesh,
        in_specs=(P(None, "dp", "seq", None), P(None, "dp"), P(None, "dp", "seq"), P(None, "dp", "seq"), P("section", None),
                  P("section", None), P("section", None, None), P("section", None, None), P("section", None, None),
                  P("section", None, None, None), P("section", None, None), P(), P(None, "dp", "seq", None)),
        out_specs=(P("section", None, "dp", "seq", None), P("section", None, "dp", "seq", None), P("section", None), P("section", None),
                   P("section", None, None), P("section", None, None), P("section", None, None), P("section", None, None, None),
                   P("section", None, None), P()),
        check_vma=False,
    )
```

```python
import functools

import jax
import jax.numpy as jnp
from jax import lax
from jax.experimental import pallas as pl
from jax.experimental.pallas import tpu as pltpu
from jax.sharding import PartitionSpec as P


EPS = 1e-05
BF, F32 = jnp.bfloat16, jnp.float32
MESH = pl.DeviceIdType.MESH
G0 = 0.7978845608028654
G1 = 0.044715
DIL = 2
HALO = 16
OUT0, CONV0, IN0, EXTRA0, UNITS = 0, 200, 700, 900, 936
PIECES, PLANE_UNITS, Z_UNITS, SLOTS = 9, 80, 24, 7


def dot(a, b):
    return lax.dot_general(a, b, (((1,), (0,)), ((), ())), preferred_element_type=F32)


def dot_nt(a, b):
    return lax.dot_general(a, b, (((1,), (1,)), ((), ())), preferred_element_type=F32)


def dot_tn(a, b):
    return lax.dot_general(a, b, (((0,), (0,)), ((), ())), preferred_element_type=F32)


def chunks(rows, fn, size=None, unroll=1):
    size = size or (96 if rows % 96 == 0 else 64)

    def one(i, _):
        fn(pl.multiple_of(i * size, size), size)
        return 0

    lax.fori_loop(0, rows // size, one, 0, unroll=unroll)


def cols(j):
    return pl.ds(j * 128, 128)


def stats(load, n):
    total = load(0)
    for j in range(1, n):
        total = total + load(j)
    mean = jnp.sum(total, axis=-1, keepdims=True) * (1.0 / (128 * n))
    square = None
    for j in range(n):
        d = load(j) - mean
        square = d * d if square is None else square + d * d
    var = jnp.sum(square, axis=-1, keepdims=True) * (1.0 / (128 * n))
    return mean, lax.rsqrt(var + EPS)


def norm_gelu(load, n, gain, shift, store):
    mean, rstd = stats(load, n)
    for j in range(n):
        u = (load(j) - mean) * rstd * gain(j) + shift(j)
        t = jnp.tanh(u * (G0 + (G0 * G1) * (u * u)))
        h = 0.5 * u
        store(j, h + h * t)


def fold(v):
    rows, width = v.shape
    return jnp.sum(v.reshape(rows // 8, 8, width), axis=0)


def norm_gelu_back(load, dy, n, gain, shift, dgain, dshift, hold, store):
    mean, rstd = stats(load, n)
    s1 = s2 = None
    for j in range(n):
        g = gain(j)
        hat = (load(j) - mean) * rstd
        u = hat * g + shift(j)
        w = u * u
        t = jnp.tanh(u * (G0 + (G0 * G1) * w))
        slope = 0.5 + 0.5 * t + u * (1.0 - t * t) * (0.5 * G0 + (1.5 * G0 * G1) * w)
        du = dy(j) * slope
        if dgain is not None:
            dgain[:, cols(j)] += fold(du * hat)
            dshift[:, cols(j)] += fold(du)
        dh = du * g
        hold[0, :, cols(j)] = hat
        hold[1, :, cols(j)] = dh
        p = dh * hat
        s1 = dh if s1 is None else s1 + dh
        s2 = p if s2 is None else s2 + p
    m1 = jnp.sum(s1, axis=-1, keepdims=True) * (1.0 / (128 * n))
    m2 = jnp.sum(s2, axis=-1, keepdims=True) * (1.0 / (128 * n))
    for j in range(n):
        store(j, rstd * (hold[1, :, cols(j)] - m1 - hold[0, :, cols(j)] * m2))


def norm_gelu_both(load, dy, n, gain, shift, dgain, dshift, hold, store, store_back):
    mean, rstd = stats(load, n)
    s1 = s2 = None
    for j in range(n):
        g = gain(j)
        hat = (load(j) - mean) * rstd
        u = hat * g + shift(j)
        w = u * u
        t = jnp.tanh(u * (G0 + (G0 * G1) * w))
        half = 0.5 + 0.5 * t
        store(j, u * half)
        slope = half + u * (1.0 - t * t) * (0.5 * G0 + (1.5 * G0 * G1) * w)
        du = dy(j) * slope
        dgain[:, cols(j)] += fold(du * hat)
        dshift[:, cols(j)] += fold(du)
        dh = du * g
        hold[0, :, cols(j)] = hat
        hold[1, :, cols(j)] = dh
        p = dh * hat
        s1 = dh if s1 is None else s1 + dh
        s2 = p if s2 is None else s2 + p
    m1 = jnp.sum(s1, axis=-1, keepdims=True) * (1.0 / (128 * n))
    m2 = jnp.sum(s2, axis=-1, keepdims=True) * (1.0 / (128 * n))
    for j in range(n):
        store_back(j, rstd * (hold[1, :, cols(j)] - m1 - hold[0, :, cols(j)] * m2))


def row(ref, k):
    return lambda j: ref[pl.ds(k, 1), cols(j)]


def view(ref, *at):
    return lambda j: ref[(*at, cols(j))].astype(F32)


def put_grad(DG, c, unit, value, col0=0):
    m, n = value.shape
    per = m // 32
    value = value.astype(BF)
    for j in range(n // 128):
        block = value[:, j * 128 : (j + 1) * 128].reshape(m // 16, 16, 128)
        for h in range(2):
            DG[lax.rem(h + c, 2), pl.ds(unit + (col0 + j) * per, per)] = block[h * per : (h + 1) * per]


def put(ref, *at):
    def store(j, v):
        ref[(*at, cols(j))] = v.astype(ref.dtype)

    return store


def positions(first, i, size):
    return first + i + lax.broadcasted_iota(jnp.int32, (size, 1), 0)


class Ring:
    KINDS = ("D", "P1", "P2", "PZ1", "PZ2", "PT1", "PT2", "PT3", "G1", "G2", "Q1", "Q2", "X1", "X2", "X3", "X4", "QT1", "QT2", "QT3", "F")

    def __init__(self, N, PU, QU):
        self.N, self.PU, self.QU, self.U = N, PU, QU, PU + QU
        self.out_units, self.live = N * self.U, True

    def scratch(self):
        PU, QU, U = self.PU, self.QU, self.U
        b = lambda u, n=SLOTS - 1: pltpu.VMEM((n, u, 16, 128), BF)
        sems = pltpu.SemaphoreType.DMA((len(self.KINDS), 2 * self.N))
        return [b(U, 4), b(PU // 2), b(PU // 4), b(PU // 4, SLOTS), b(PU // 8), b(QU, SLOTS), b(QU // 2, SLOTS), b(QU // 4), b(QU // 8), b(PU // 4), b(QU // 8),
                sems, sems]

    def bind(self, DG, out, RD, RP1, RP2, RZ1, RZ2, RQ1, RQ2, RX1, RX2, TQ, TX, ss, rs):
        N, PU, QU, U, ds = self.N, self.PU, self.QU, self.U, pl.ds
        c, z, q = lax.axis_index("section"), lax.axis_index("dp"), lax.axis_index("seq")
        xb, yb = lax.rem(q, 2), lax.div(q, 2)
        f, s = jnp.where(c == 0, xb, yb), jnp.where(c == 0, yb, xb)
        qx, qy = yb * 2 + 1 - xb, (1 - yb) * 2 + xb
        n1 = (c, z, jnp.where(c == 0, qx, qy))
        n2 = (c, z, jnp.where(c == 0, qy, qx))
        side = lax.div(z, 2)
        near, farc = side, 1 - side
        zp = (c, side * 2 + 1 - lax.rem(z, 2), q)
        far = (c, 3 - z, q)
        peer = (1 - c, z, q)
        inner = jnp.logical_or(z == 1, z == 2)
        outer = jnp.logical_not(inner)
        order = {k: i for i, k in enumerate(self.KINDS)}

        def cp(k, i, src, dst, dev):
            return remote(src, dst, ss.at[order[k], i], rs.at[order[k], i], dev)

        def add(dst, *terms):
            acc = terms[0][...].astype(F32)
            for t in terms[1:]:
                acc = acc + t[...].astype(F32)
            dst[...] = acc.astype(BF)

        def phys(i):
            return jnp.where(i < 4, i + 2, jnp.where(i < 6, i - 4, i))

        def part(i, start=0, size=U):
            return DG.at[0, ds(phys(i) * U + start, size)]

        H, Q4, E8 = PU // 2, PU // 4, PU // 8
        h, h2, h4 = QU // 2, QU // 4, QU // 8
        pq = lambda a, b: ((2 * a + b) * Q4, Q4)
        pch = lambda k: ((2 * f + s) * Q4 + k * E8, E8)
        tch = lambda k: ds(k * E8, E8)
        qn = lambda k: (PU + k * h, h)
        qhalf = lambda k, a: (PU + k * h + a * h2, h2)
        qquart = lambda k, a, b: (PU + k * h + (2 * a + b) * h4, h4)
        k8 = lambda i: lax.rem(i, SLOTS)
        k7 = lambda i: lax.rem(i, SLOTS - 1)
        rd = lambda i: RD.at[lax.rem(i, 4)]
        same = lambda k, at, dev: (lambda i: cp(k, i, part(i, *at), part(i, *at), dev))
        C = dict(
            D=lambda i: cp("D", i, DG.at[1, ds(phys(i) * U, U)], rd(i), peer),
            P1=lambda i: cp("P1", i, part(i, (1 - f) * H, H), RP1.at[k7(i)], n1),
            P2=lambda i: cp("P2", i, part(i, *pq(f, 1 - s)), RP2.at[k7(i)], n2),
            PZ1=lambda i: cp("PZ1", i, part(i, *pq(f, s)), RZ1.at[k8(i)], zp),
            PZ2=lambda i: cp("PZ2", i, part(i, *pch(farc)), RZ2.at[k7(i)], far),
            PT1=lambda i: cp("PT1", i, TQ.at[k7(i), tch(near)], TQ.at[k7(i), tch(near)], far),
            PT2=lambda i: cp("PT2", i, TQ.at[k7(i), tch(near)], TQ.at[k7(i), tch(near)], zp),
            PT3=lambda i: cp("PT3", i, TQ.at[k7(i), tch(farc)], TQ.at[k7(i), tch(farc)], zp),
            G1=same("G1", pq(f, s), n2),
            G2=same("G2", (f * H, H), n1),
            Q1=lambda i: cp("Q1", i, part(i, PU, QU), RQ1.at[k8(i)], zp),
            Q2=lambda i: cp("Q2", i, part(i, *qn(farc)), RQ2.at[k8(i)], far),
            X1=lambda i: cp("X1", i, part(i, *qhalf(near, 1 - f)), RX1.at[k7(i)], n1),
            X2=lambda i: cp("X2", i, part(i, *qquart(near, f, 1 - s)), RX2.at[k7(i)], n2),
            X3=lambda i: cp("X3", i, part(i, *qquart(near, f, s)), TX.at[k7(i)], n2),
            X4=same("X4", qhalf(near, f), n1),
            QT1=same("QT1", qn(near), far),
            QT2=same("QT2", qn(near), zp),
            QT3=same("QT3", qn(farc), zp),
        )

        def final(i, start):
            to = out.at[c, ds(phys(i) * U - jnp.where(i < N, 0, N * U), U)]
            there, here = cp("F", i, part(i), to, peer), pltpu.make_async_copy(part(i), to, ss.at[order["F"], i])
            both_ways(jnp.where(i < N, 1, 0) == c, here.start if start else here.wait, there.start if start else there.wait_send)

        def on_inner(fn):
            pl.when(inner)(fn)

        def on_outer(fn):
            pl.when(outer)(fn)

        def s0(i):
            C["D"](i).start()

        def s1(i):
            C["D"](i).wait()
            add(part(i), part(i), rd(i))
            C["P1"](i).start()
            on_outer(lambda: C["Q1"](i).start())

        def s2(i):
            @on_inner
            def _():
                C["Q1"](i).wait_recv()
                add(part(i, *qn(farc)), part(i, *qn(farc)), RQ1.at[k8(i), ds(farc * h, h)])
                C["Q2"](i).start()

            C["P1"](i).wait()
            add(part(i, f * H, H), part(i, f * H, H), RP1.at[k7(i)])
            C["P2"](i).start()
            on_outer(lambda: C["Q1"](i).wait_send())

        def s3(i):
            C["P2"](i).wait()
            add(part(i, *pq(f, s)), part(i, *pq(f, s)), RP2.at[k7(i)])
            on_outer(lambda: C["PZ1"](i).start())

            @on_inner
            def _():
                C["Q2"](i).wait()
                add(part(i, *qn(near)), part(i, *qn(near)), RQ1.at[k8(i), ds(near * h, h)], RQ2.at[k8(i)])
                C["X1"](i).start()

        def s4(i):
            @on_inner
            def _():
                C["PZ1"](i).wait_recv()
                add(part(i, *pch(farc)), part(i, *pch(farc)), RZ1.at[k8(i), tch(farc)])
                C["PZ2"](i).start()
                C["X1"](i).wait()
                add(part(i, *qhalf(near, f)), part(i, *qhalf(near, f)), RX1.at[k7(i)])
                C["X2"](i).start()

            on_outer(lambda: C["PZ1"](i).wait_send())

        def s5(i):
            @on_inner
            def _():
                C["PZ2"](i).wait()
                add(TQ.at[k7(i), tch(near)], part(i, *pch(near)), RZ1.at[k8(i), tch(near)], RZ2.at[k7(i)])
                C["PT1"](i).start()
                C["PT2"](i).start()
                C["X2"](i).wait()
                add(part(i, *qquart(near, f, s)), part(i, *qquart(near, f, s)), RX2.at[k7(i)])
                C["X3"](i).start()

        def s6(i):
            @on_inner
            def _():
                C["PT1"](i).wait()
                C["PT3"](i).start()
                C["X3"](i).wait()
                part(i, *qquart(near, f, 1 - s))[...] = TX[k7(i)]
                C["X4"](i).start()

        def s7(i):
            @on_outer
            def _():
                C["PT2"](i).wait_recv()
                C["PT3"](i).wait_recv()

            @on_inner
            def _():
                C["PT2"](i).wait_send()
                C["PT3"](i).wait_send()

            part(i, *pq(f, s))[...] = TQ[k7(i)]
            C["G1"](i).start()

            @on_inner
            def _():
                C["X4"](i).wait()
                C["QT1"](i).start()
                C["QT2"](i).start()

        def s8(i):
            C["G1"](i).wait()
            C["G2"](i).start()

            @on_inner
            def _():
                C["QT1"](i).wait()
                C["QT3"](i).start()

        def s9(i):
            C["G2"](i).wait()

            @on_outer
            def _():
                C["QT2"](i).wait_recv()
                C["QT3"](i).wait_recv()

            @on_inner
            def _():
                C["QT2"](i).wait_send()
                C["QT3"](i).wait_send()

            final(i, True)

        def s10(i):
            final(i, False)

        stages = (s0, s1, s2, s3, s4, s5, s6, s7, s8, s9, s10)

        def step(t):
            for k, stage in enumerate(stages):
                i = t - k
                pl.when(jnp.logical_and(i >= 0, i < 2 * N))(functools.partial(stage, i))

        def finish():
            def one(j, _):
                i = jnp.where(c == 1, j, j + N)
                cp("F", i, part(i), out.at[c, ds(0, U)], peer).wait_recv()
                return 0

            lax.fori_loop(0, N, one, 0)

        def barrier():
            b = pltpu.get_barrier_semaphore()
            for d in plane(c, z, q) + [zp]:
                pl.semaphore_signal(b, inc=1, device_id=d, device_id_type=MESH)

            @on_inner
            def _():
                pl.semaphore_signal(b, inc=1, device_id=far, device_id_type=MESH)
                pl.semaphore_wait(b, 9)

            on_outer(lambda: pl.semaphore_wait(b, 8))

        self.step, self.finish, self.barrier, self.iters = step, finish, barrier, 2 * N + len(stages) - 1


class NoRing:
    def __init__(self, N, U):
        self.N, self.U, self.live, self.out_units = N, U, False, 2 * N * U

    def scratch(self):
        return []

    def bind(self, *refs):
        pass

    def barrier(self):
        greet(plane(lax.axis_index("section"), lax.axis_index("dp"), lax.axis_index("seq")))

    def step(self, t):
        pass


def plane(c, z, q):
    out = []
    for i in range(1, 8):
        n = lax.rem(c * 4 + q + i, 8)
        out.append((lax.div(n, 4), z, lax.rem(n, 4)))
    return out


def greet(ids):
    barrier = pltpu.get_barrier_semaphore()
    for d in ids:
        pl.semaphore_signal(barrier, inc=1, device_id=d, device_id_type=MESH)
    pl.semaphore_wait(barrier, len(ids))


def remote(src, dst, ss, rs, dev):
    return pltpu.make_async_remote_copy(src_ref=src, dst_ref=dst, send_sem=ss, recv_sem=rs, device_id=dev, device_id_type=MESH)


def both_ways(cond, here, there):
    @pl.when(cond)
    def _():
        here()

    @pl.when(jnp.logical_not(cond))
    def _():
        there()


class Spread:
    def __init__(self, c, z, q, ss, rs, ls):
        self.c, self.z, self.q, self.ss, self.rs, self.ls = c, z, q, ss, rs, ls

    def go(self, a, src, dst, m, start):
        c, z, q = self.c, self.z, self.q
        for h in range(2):
            s, d, j = src.at[m, :, h], dst(q), 2 * m + h
            far = remote(s, d, self.ss.at[a, j], self.rs.at[a, q], (jnp.int32(h), z, 2 * c + m))
            near = pltpu.make_async_copy(s, d, self.ls.at[a])
            both_ways(jnp.logical_and(h == c, 2 * c + m == q), near.start if start else near.wait, far.start if start else far.wait_send)

    def arrive(self, a, src, dst):
        c, z, q = self.c, self.z, self.q
        fc = lax.div(q, 2)
        for p in range(4):
            @pl.when(jnp.logical_not(jnp.logical_and(c == fc, p == q)))
            def _():
                remote(src.at[0, :, 0], dst(p), self.ss.at[a, 0], self.rs.at[a, p], (fc, z, jnp.int32(p))).wait_recv()

    def back(self, a, src, dst, p, start):
        c, z, q = self.c, self.z, self.q
        tc, slot = lax.div(q, 2), lax.rem(q, 2)
        s, d = src, dst.at[slot, :, c]
        far = remote(s, d, self.ss.at[a, p], self.rs.at[a, 2 * slot + c], (tc, z, jnp.int32(p)))
        near = pltpu.make_async_copy(s, d, self.ls.at[a])
        both_ways(jnp.logical_and(tc == c, p == q), near.start if start else near.wait, far.start if start else far.wait_send)

    def back_arrive(self, a, src, dst, m):
        c, z, q = self.c, self.z, self.q
        for h in range(2):
            @pl.when(jnp.logical_not(jnp.logical_and(h == c, 2 * c + m == q)))
            def _():
                remote(src.at[pl.ds(0, 2)], dst.at[m, :, h], self.ss.at[a, 0], self.rs.at[a, 2 * m + h], (jnp.int32(h), z, 2 * c + m)).wait_recv()


def edges(ref, m, seg, ss, rs, z, q, c):
    before = remote(ref.at[m, pl.ds(HALO, HALO)], ref.at[m, pl.ds(HALO + seg, HALO)], ss.at[0, m], rs.at[0, m], (c, z, q - 1))
    after = remote(ref.at[m, pl.ds(seg, HALO)], ref.at[m, pl.ds(0, HALO)], ss.at[1, m], rs.at[1, m], (c, z, q + 1))
    return ((q > 0, q < 3, before), (q < 3, q > 0, after))


def whole(lengths, inputs, cot_all, w_in, conv_w, w_out, gain_in, bias_in, gain_mid, bias_mid, dec, mask, types, act, igr, total, cnt,
          WI, WC, WO, PR, xe, cot, out1, first1, hidden1, sec1, mixed1, third1, first2, hidden2, sec2, dth2, sp, dthr, dpad,
          third2, dsec2, og, ge, hd, hold, dgbi, dgbm, counts, DG,
          ws, wr, wl, xs, xr, xl, ss, rs, ls, gs, gr, ps, pr, pw, *ring_refs, ring):
    c, z, q = lax.axis_index("section"), lax.axis_index("dp"), lax.axis_index("seq")
    peer = (1 - c, z, q)
    seg, D = cot.shape[1:]
    H = mixed1.shape[2]
    nd, nh = D // 128, H // 128
    rows = seg + 2 * HALO
    base = q * seg
    he, dme, me = hd.at[pl.ds(0, rows)], hd.at[pl.ds(rows, rows)], hd.at[pl.ds(rows, seg)]
    ring.bind(DG, total, *ring_refs)
    own = [pltpu.make_async_copy(inputs.at[2 * c + m, 0], xe.at[m, pl.ds(HALO, seg)], xl.at[m]) for m in range(2)]
    own += [pltpu.make_async_copy(cot_all.at[2 * c + m, 0], cot.at[m], xl.at[2 + m]) for m in range(2)]
    mats = [(PR.at[c], PR.at[c]), (w_in.at[0], WI.at[c])] + [(conv_w.at[0, k], WC.at[c, k]) for k in range(5)] + [(w_out.at[0], WO.at[c])]
    loads = [pltpu.make_async_copy(s, d, wl.at[i]) for i, (s, d) in enumerate(mats) if i > 0]
    for cp in own[:2] + loads + own[2:]:
        cp.start()
    PR[c, pl.ds(4, 4)] = jnp.zeros((4, D), F32)
    PR[c, pl.ds(0, 1)] = gain_in[...].astype(F32)
    PR[c, pl.ds(1, 1)] = bias_in[...].astype(F32)
    for k in range(2):
        PR[c, pl.ds(2, 1), pl.ds(k * H, H)] = gain_mid[0, pl.ds(k, 1)].astype(F32)
        PR[c, pl.ds(3, 1), pl.ds(k * H, H)] = bias_mid[0, pl.ds(k, 1)].astype(F32)
    ring.barrier()
    sends = [remote(s, d, ws.at[i], wr.at[i], peer) for i, (s, d) in enumerate(mats)]
    halos = []
    for m in range(2):
        x = inputs.at[2 * c + m, 0]
        halos.append((q > 0, q < 3, remote(x.at[pl.ds(0, HALO)], xe.at[m, pl.ds(HALO + seg, HALO)], xs.at[0, m], xr.at[0, m], (c, z, q - 1))))
        halos.append((q < 3, q > 0, remote(x.at[pl.ds(seg - HALO, HALO)], xe.at[m, pl.ds(0, HALO)], xs.at[1, m], xr.at[1, m], (c, z, q + 1))))
    for cond, _, cp in halos:
        pl.when(cond)(cp.start)
    sends[0].start()

    @pl.when(c == 0)
    def _():
        for cp in sends[1:]:
            cp.start()

    @pl.when(c == 1)
    def _():
        for cp in sends[7:] + sends[1:7]:
            cp.start()

    @pl.when(q == 0)
    def _():
        xe[:, pl.ds(0, HALO)] = jnp.zeros((2, HALO, D), BF)
        ge[:, pl.ds(0, HALO)] = jnp.zeros((2, HALO, D), BF)

    @pl.when(q == 3)
    def _():
        xe[:, pl.ds(HALO + seg, HALO)] = jnp.zeros((2, HALO, D), BF)
        ge[:, pl.ds(HALO + seg, HALO)] = jnp.zeros((2, HALO, D), BF)

    def have(i, layer):
        both_ways(c == layer, loads[i - 1].wait, sends[i].wait_recv)

    for ref in (dgbi, dgbm, counts):
        ref[...] = jnp.zeros_like(ref)
    zero = jnp.zeros((2, 64, H), BF)
    for ref in (sp, dpad):
        ref[pl.ds(0, 2)] = zero
        ref[pl.ds(10, 2)] = zero
    sec1[:, pl.ds(0, 8)] = jnp.zeros((2, 8, H), F32)
    sec1[:, pl.ds(rows + 8, 8)] = jnp.zeros((2, 8, H), F32)
    spread = Spread(c, z, q, ss, rs, ls)
    sp_at = lambda p: sp.at[pl.ds(2 + 2 * p, 2)]
    dthr_at = lambda p: dthr.at[pl.ds(2 * p, 2)]
    gi, bi = lambda l: row(PR.at[l], 0), lambda l: row(PR.at[l], 1)
    gm = lambda l, k: (lambda j: PR[l, pl.ds(2, 1), cols(k * nh + j)])
    bm = lambda l, k: (lambda j: PR[l, pl.ds(3, 1), cols(k * nh + j)])

    sends[0].wait_recv()
    for m in range(2):
        own[m].wait()
    for _, cond, cp in halos:
        pl.when(cond)(cp.wait_recv)

    def first_norm(m, _):
        def a(i, size):
            r = pl.ds(i, size)
            norm_gelu(view(xe, m, r), nd, gi(0), bi(0), put(first1, m, r))

        chunks(rows, a, unroll=3)
        return 0

    lax.fori_loop(0, 2, first_norm, 0)
    for m in range(2):
        own[2 + m].wait()
    have(7, 1)

    def third_grad(m, _):
        dth2[m] = dot_nt(cot[m], WO[1]).astype(BF).reshape(2, 2, 64, H)
        spread.go(1, dth2, dthr_at, m, True)
        return 0

    lax.fori_loop(0, 2, third_grad, 0)
    have(1, 0)

    def second_norm(m, _):
        he[...] = dot(first1[m], WI[0])
        hidden1[m] = he[pl.ds(HALO, seg)]

        def b(i, size):
            pos = positions(base - HALO, i, size)
            keep = jnp.logical_and(pos >= 0, pos < lengths[2 * c + m])

            def store(j, v):
                sec1[m, pl.ds(i + 8, size), cols(j)] = jnp.where(keep, v, 0.0).astype(BF).astype(F32)

            norm_gelu(view(he, pl.ds(i, size)), nh, gm(0, 0), bm(0, 0), store)

        chunks(rows, b, unroll=3)
        return 0

    lax.fori_loop(0, 2, second_norm, 0)
    for k in range(5):
        have(2 + k, 0)

    def forward(m, _):
        acc = None
        for k in range(5):
            term = dot(sec1[m, pl.ds(8 + DIL * (k - 2), rows)].astype(BF), WC[0, k])
            acc = term if acc is None else acc + term
        mixed1[m] = acc

        def e(i, size):
            norm_gelu(view(mixed1, m, pl.ds(i + HALO, size)), nh, gm(0, 1), bm(0, 1), put(third1, m, pl.ds(i, size)))

        chunks(seg, e, unroll=4)

        @pl.when(m == 0)
        def _():
            have(7, 0)

        he[pl.ds(0, seg)] = dot(third1[m], WO[0, :, :H])
        me[...] = dot(third1[m], WO[0, :, H:])

        def d(i, size):
            r = pl.ds(i, size)
            for j in range(nd):
                br = he[r, cols(j)] if j < nh else me[r, cols(j - nh)]
                out1[m, r, cols(j)] = (xe[m, pl.ds(i + HALO, size), cols(j)].astype(F32) + br).astype(BF)
            norm_gelu(view(out1, m, r), nd, gi(1), bi(1), put(first2, m, r))

        chunks(seg, d, unroll=4)

        @pl.when(m == 0)
        def _():
            have(1, 1)

        hidden2[m] = dot(first2[m], WI[1])

        def f(jj, _):
            i = pl.multiple_of(jj * 64, 64)
            pos = positions(base, i, 64)

            def store(j, v):
                sec2[m, lax.div(jj, 2), lax.rem(jj, 2), :, cols(j)] = jnp.where(pos < lengths[2 * c + m], v, 0.0).astype(BF)

            norm_gelu(view(hidden2, m, pl.ds(i, 64)), nh, gm(1, 0), bm(1, 0), store)
            return 0

        lax.fori_loop(0, seg // 64, f, 0, unroll=4)
        spread.go(0, sec2, sp_at, m, True)
        return 0

    lax.fori_loop(0, 2, forward, 0)
    for k in range(5):
        have(2 + k, 1)

    def place(i, src, dst, layer):
        to = dst.at[pl.ds(2 * c, 2)]
        here, there = pltpu.make_async_copy(src, to, pw.at[i]), remote(src, to, ps.at[i], pr.at[i // 2], peer)
        both_ways(c == layer, here.start, there.start)
        return lambda: both_ways(c == layer, here.wait, there.wait_send)

    placed = [place(0, out1, act, 0)]
    for m in range(2):
        spread.go(0, sec2, sp_at, m, False)
    spread.arrive(0, sec2, sp_at)

    def conv(r, _):
        acc = None
        for k in range(5):
            term = dot(sp[pl.ds(4 * r + k, 4)].reshape(256, H), WC[1, k])
            acc = term if acc is None else acc + term
        hd[pl.ds(256 * r, 256)] = acc
        return 0

    lax.fori_loop(0, 2, conv, 0)
    for m in range(2):
        spread.go(1, dth2, dthr_at, m, False)
    spread.arrive(1, dth2, dthr_at)

    def mid(i, _):
        every = pl.ds(0, 64)
        norm_gelu_both(view(hd, pl.ds(pl.multiple_of(64 * i, 64), 64)), view(dthr, i, every), nh, gm(1, 1), bm(1, 1), dgbm.at[2], dgbm.at[3], hold,
                       put(dth2, lax.div(i, 4), lax.rem(lax.div(i, 2), 2), lax.rem(i, 2), every), put(dpad, i + 2, every))
        return 0

    lax.fori_loop(0, 8, mid, 0, unroll=4)
    for p in range(4):
        spread.back(2, dth2.at[p // 2, p % 2], third2, p, True)
    dm2 = dpad[pl.ds(2, 8)].reshape(512, H)

    for k in range(5):
        put_grad(DG, c, CONV0 + k * 100, dot_tn(sp[pl.ds(k, 8)].reshape(512, H), dm2))
        if k in (1, 3):
            ring.step(k // 2)

    def conv_back(r, _):
        acc = None
        for k in range(5):
            term = dot_nt(dpad[pl.ds(4 * r + 4 - k, 4)].reshape(256, H), WC[1, k])
            acc = term if acc is None else acc + term
        dthr[pl.ds(4 * r, 4)] = acc.astype(BF).reshape(4, 64, H)
        return 0

    lax.fori_loop(0, 2, conv_back, 0)
    for p in range(4):
        spread.back(3, dthr.at[pl.ds(2 * p, 2)], dsec2, p, True)
    ring.step(2)
    for p in range(4):
        spread.back(2, dth2.at[p // 2, p % 2], third2, p, False)
    for m in range(2):
        spread.back_arrive(2, dthr, third2, m)
    flat = lambda v: v.reshape(2 * seg, v.shape[-1])
    t2 = flat(third2[...])
    for j in range(2):
        put_grad(DG, c, OUT0, dot_tn(t2, flat(cot[:, :, pl.ds(j * H, H)])), nh * j)
    ring.step(3)
    for p in range(4):
        spread.back(3, dthr.at[pl.ds(2 * p, 2)], dsec2, p, False)
    for m in range(2):
        spread.back_arrive(3, dthr, dsec2, m)
    dh = lambda m: dpad.at[pl.ds(4 * m, 4)]

    def two(m, _):
        def b(i, _):
            pos = positions(base, i * 64, 64)
            u, h = lax.div(i, 2), lax.rem(i, 2)
            ds = lambda j: jnp.where(pos < lengths[2 * c + m], dsec2[m, u, h, :, cols(j)].astype(F32), 0.0)
            norm_gelu_back(view(hidden2, m, pl.ds(pl.multiple_of(i * 64, 64), 64)), ds, nh, gm(1, 0), bm(1, 0), dgbm.at[0], dgbm.at[1], hold,
                           put(dpad, 4 * m + i, pl.ds(0, 64)))
            return 0

        lax.fori_loop(0, seg // 64, b, 0, unroll=2)
        dhm = dh(m)[...].reshape(seg, H)
        he[pl.ds(0, seg)] = dot_nt(dhm, WI[1, :H])
        me[...] = dot_nt(dhm, WI[1, H:])

        def e(i, size):
            r = pl.ds(i, size)
            df = lambda j: he[r, cols(j)] if j < nh else me[r, cols(j - nh)]

            def store(j, v):
                ge[m, pl.ds(i + HALO, size), cols(j)] = (cot[m, r, cols(j)].astype(F32) + v).astype(BF)

            norm_gelu_back(view(out1, m, r), df, nd, gi(1), bi(1), dgbi.at[0], dgbi.at[1], hold, store)

        chunks(seg, e, unroll=2)
        for cond, _, cp in edges(ge, m, seg, gs, gr, z, q, c):
            pl.when(cond)(cp.start)
        ring.step(4 + m)
        return 0

    lax.fori_loop(0, 2, two, 0)
    placed.append(place(2, ge.at[:, pl.ds(HALO, seg)], igr, 1))
    put_grad(DG, c, IN0, dot_tn(flat(first2[...]), dpad[pl.ds(0, 8)].reshape(2 * seg, H)))

    def extra(first_unit, with_counts):
        flat_rows = [dgbi[k, :, cols(j)] for k in range(2) for j in range(nd)]
        flat_rows += [dgbm[k, :, cols(j)] for k in range(4) for j in range(nh)]
        small = [jnp.sum(v, axis=0, keepdims=True) for v in flat_rows]
        if with_counts:
            small.append(jnp.pad(jnp.sum(counts[...], axis=0, keepdims=True), ((0, 0), (0, 128 - classes))))
        size = UNITS - EXTRA0
        small.append(jnp.zeros((48 - len(small), 128), F32))
        block = jnp.concatenate(small, axis=0).astype(BF).reshape(3, 16, 128)
        for h in range(2):
            DG[h, pl.ds(first_unit, 3)] = block
            DG[h, pl.ds(first_unit + 3, size - 3)] = jnp.zeros((size - 3, 16, 128), BF)

    extra(EXTRA0, False)
    ring.step(6)
    for ref in (dgbi, dgbm):
        ref[...] = jnp.zeros_like(ref)
    for m in range(2):
        for s_cond, r_cond, cp in edges(ge, m, seg, gs, gr, z, q, c):
            pl.when(s_cond)(cp.wait_send)
            pl.when(r_cond)(cp.wait_recv)
    dm = lambda m: dsec2.at[m]

    def one(m, _):
        he[...] = dot_nt(ge[m], WO[0])

        def a(i, _):
            r = pl.ds(pl.multiple_of(i * 64 + HALO, 16), 64)
            u, h = lax.div(i, 2), lax.rem(i, 2)

            def store(j, v):
                v = v.astype(BF)
                dme[r, cols(j)] = v.astype(F32)
                dsec2[m, u, h, :, cols(j)] = v

            norm_gelu_back(view(mixed1, m, r), view(he, r), nh, gm(0, 1), bm(0, 1), dgbm.at[2], dgbm.at[3], hold, store)
            return 0

        lax.fori_loop(0, seg // 64, a, 0, unroll=2)
        for edge in (0, rows - HALO):
            r = pl.ds(edge, HALO)
            pos = positions(base - HALO, edge, HALO)
            within = jnp.logical_and(pos >= 0, pos < 4 * seg)

            def store(j, v):
                dme[r, cols(j)] = jnp.where(within, v, 0.0).astype(BF).astype(F32)

            norm_gelu_back(view(mixed1, m, r), view(he, r), nh, gm(0, 1), bm(0, 1), None, None, hold.at[:, pl.ds(0, HALO)], store)
        acc = None
        for k in range(5):
            term = dot_nt(dme[pl.ds(HALO - DIL * (k - 2), seg)].astype(BF), WC[0, k])
            acc = term if acc is None else acc + term
        he[pl.ds(0, seg)] = acc

        def b(i, _):
            r = pl.ds(pl.multiple_of(i * 64, 64), 64)
            pos = positions(base, i * 64, 64)
            ds = lambda j: jnp.where(pos < lengths[2 * c + m], he[r, cols(j)], 0.0)
            norm_gelu_back(view(hidden1, m, r), ds, nh, gm(0, 0), bm(0, 0), dgbm.at[0], dgbm.at[1], hold, put(dpad, 4 * m + i, pl.ds(0, 64)))
            return 0

        lax.fori_loop(0, seg // 64, b, 0, unroll=2)
        ring.step(7 + m)
        return 0

    lax.fori_loop(0, 2, one, 0)
    low = UNITS
    t1 = flat(third1[...])
    for j in range(2):
        put_grad(DG, c, low + OUT0, dot_tn(t1, flat(ge[:, pl.ds(HALO, seg), pl.ds(j * H, H)])), nh * j)
    ring.step(9)
    d1 = flat(dsec2[...])
    for k in range(5):
        for m in range(2):
            sec2[m] = sec1[m, pl.ds(8 + HALO + DIL * (k - 2), seg)].astype(BF).reshape(2, 2, 64, H)
        put_grad(DG, c, low + CONV0 + k * 100, dot_tn(flat(sec2[...]), d1))
        if k in (1, 3):
            ring.step(10 + k // 2)
    put_grad(DG, c, low + IN0, dot_tn(flat(first1[:, pl.ds(HALO, seg)]), dpad[pl.ds(0, 8)].reshape(2 * seg, H)))
    ring.step(12)
    classes = dec.shape[0]
    labels = lax.broadcasted_iota(jnp.int32, (1, classes), 1).astype(F32)

    def two_out(m, _):
        t = third2[m].reshape(seg, H)
        he[pl.ds(0, seg)] = dot(t, WO[1, :, :H])
        me[...] = dot(t, WO[1, :, H:])

        def a(i, size):
            r = pl.ds(i, size)
            for j in range(nd):
                br = he[r, cols(j)] if j < nh else me[r, cols(j - nh)]
                og[m, r, cols(j)] = (out1[m, r, cols(j)].astype(F32) + br).astype(BF)

        chunks(seg, a)
        logits = dot_nt(og[m], dec[...])
        ex = jnp.exp(logits - jnp.max(logits, axis=-1, keepdims=True))
        probs = ex / jnp.sum(ex, axis=-1, keepdims=True)
        pos = base + lax.broadcasted_iota(jnp.int32, (1, seg), 1)
        live = jnp.logical_and(mask[2 * c + m] == 1, pos < lengths[2 * c + m])
        code = jnp.where(live, types[2 * c + m], -1).astype(F32)
        code = jnp.broadcast_to(code, (128, seg)).T[:, :classes]
        counts[...] += fold(jnp.where(code == labels, probs, 0.0))
        ring.step(13 + m)
        return 0

    lax.fori_loop(0, 2, two_out, 0)
    placed.append(place(1, og, act, 1))
    placed[-1]()

    def one_in(m, _):
        dhm = dh(m)[...].reshape(seg, H)
        he[pl.ds(0, seg)] = dot_nt(dhm, WI[0, :H])
        me[...] = dot_nt(dhm, WI[0, H:])
        ring.step(15 + m)

        def e(i, _):
            r, x = pl.ds(pl.multiple_of(i * 64, 64), 64), pl.ds(pl.multiple_of(i * 64 + HALO, 16), 64)
            df = lambda j: he[r, cols(j)] if j < nh else me[r, cols(j - nh)]

            def store(j, v):
                og[m, r, cols(j)] = (ge[m, x, cols(j)].astype(F32) + v).astype(BF)

            norm_gelu_back(view(xe, m, x), df, nd, gi(0), bi(0), dgbi.at[0], dgbi.at[1], hold, store)

            return 0

        lax.fori_loop(0, seg // 64, e, 0)
        return 0

    lax.fori_loop(0, 2, one_in, 0)
    placed.append(place(3, og, igr, 0))
    extra(low + EXTRA0, True)

    def rest(t, _):
        ring.step(t)
        return 0

    if ring.live:
        lax.fori_loop(17, ring.iters, rest, 0)
        ring.finish()
        cnt[...] = DG[0, pl.ds(UNITS + EXTRA0, 3)]
    else:
        everything = pltpu.make_async_copy(DG, total, pw.at[0])
        everything.start()
        everything.wait()
        cnt[...] = jnp.zeros_like(cnt)
    for i in (0, 1, 3):
        placed[i]()
    for i, dst in ((0, act), (1, igr)):
        remote(og, dst.at[pl.ds(2 * (1 - c), 2)], ps.at[0], pr.at[i], peer).wait_recv()
    for cp in sends:
        cp.wait_send()
    for cond, _, cp in halos:
        pl.when(cond)(cp.wait_send)


def run(ring, lengths, inputs, cot, w_in, conv_w, w_out, gain_in, bias_in, gain_mid, bias_mid, dec, mask, types):
    seg, D, H = inputs.shape[2], inputs.shape[3], w_in.shape[2]
    rows = seg + 2 * HALO
    any_, vm, sm = (pl.BlockSpec(memory_space=s) for s in (pl.ANY, pltpu.VMEM, pltpu.SMEM))
    sh = jax.ShapeDtypeStruct
    dma = lambda *s: pltpu.SemaphoreType.DMA(s)
    part = (2, 2, 2, 64, H)
    scratch = [((2, D, H), BF), ((2, 5, H, H), BF), ((2, H, D), BF), ((2, 8, D), F32), ((2, rows, D), BF), ((2, seg, D), BF),
               ((2, seg, D), BF), ((2, rows, D), BF), ((2, seg, H), F32), ((2, rows + 16, H), F32), ((2, rows, H), F32), ((2, seg, H), BF),
               ((2, seg, D), BF), ((2, seg, H), F32), (part, BF), (part, BF), ((12, 64, H), BF), ((8, 64, H), BF),
               ((12, 64, H), BF), (part, BF), (part, BF), ((2, seg, D), BF), ((2, rows, D), BF), ((2 * rows, H), F32),
               ((2, 64, D), F32), ((2, 8, D), F32), ((4, 8, H), F32), ((8, dec.shape[0]), F32), ((2, 2 * UNITS, 16, 128), BF)]
    return pl.pallas_call(
        functools.partial(whole, ring=ring),
        out_shape=[sh((4, seg, D), BF), sh((4, seg, D), BF), sh((2, ring.out_units, 16, 128), BF), sh((3, 16, 128), BF)],
        in_specs=[sm] + [any_] * 5 + [vm] * 7,
        out_specs=[any_, any_, any_, vm],
        scratch_shapes=[pltpu.VMEM(s, d) for s, d in scratch]
        + [dma(8), dma(8), dma(8), dma(2, 2), dma(2, 2), dma(4), dma(4, 4), dma(4, 4), dma(4), dma(2, 2), dma(2, 2), dma(4), dma(2), dma(4)]
        + ring.scratch(),
        compiler_params=pltpu.CompilerParams(collective_id=1, has_side_effects=True, vmem_limit_bytes=63 * 2**20 + 2**19),
    )(lengths, inputs, cot, w_in, conv_w, w_out, gain_in, bias_in, gain_mid, bias_mid, dec, mask, types)


def unpack_kernel(conv, w_out, w_in, extra, cnt, act, igr, s_conv, s_out, s_in, gi, bi, gm, bm, counts, act_o, igr_o):
    act_o[...] = act[...]
    igr_o[...] = igr[...]
    for j in range(5):
        for h in range(2):
            s_conv[0, 0, pl.ds(h * 320, 320), cols(j)] = conv[h, pl.ds(j * 20, 20)].reshape(320, 128).astype(F32)
    for j in range(2):
        for h in range(2):
            s_out[0, pl.ds(h * 320, 320), cols(j)] = w_out[h, pl.ds(j * 20, 20)].reshape(320, 128).astype(F32)
    for h in range(2):
        s_in[0, pl.ds(h * 640, 640)] = w_in[h].reshape(640, 128).astype(F32)

    @pl.when(pl.program_id(0) == 0)
    def _():
        small = extra[0, pl.ds(0, 3)].reshape(48, 128).astype(F32)
        for j in range(10):
            gi[:, cols(j)] = small[j : j + 1]
            bi[:, cols(j)] = small[10 + j : 11 + j]
        for k in range(2):
            for j in range(5):
                gm[0, pl.ds(k, 1), cols(j)] = small[20 + 10 * k + j : 21 + 10 * k + j]
                bm[0, pl.ds(k, 1), cols(j)] = small[25 + 10 * k + j : 26 + 10 * k + j]
        counts[...] = cnt[...].reshape(48, 128)[40, : counts.shape[0]].astype(F32)


def unpack(total, cnt, act, igr, D, H, classes):
    def spec(units, first, moves=1):
        return pl.BlockSpec(tuple(pl.Element(n) for n in (2, units, 16, 128)), lambda k: (0, first + units * k * moves, 0, 0))

    def full(*s):
        return pl.BlockSpec(s, lambda k: (0,) * len(s))

    block = pl.BlockSpec((1, *act.shape[1:]), lambda k: (jnp.minimum(k, act.shape[0] - 1), 0, 0))
    sh = lambda *s: jax.ShapeDtypeStruct(s, F32)
    return pl.pallas_call(
        unpack_kernel,
        grid=(5,),
        out_shape=[sh(1, 5, H, H), sh(1, H, D), sh(1, D, H), sh(1, D), sh(1, D), sh(1, 2, H), sh(1, 2, H), sh(classes),
                   jax.ShapeDtypeStruct(act.shape, BF), jax.ShapeDtypeStruct(igr.shape, BF)],
        in_specs=[spec(100, CONV0), spec(40, OUT0), spec(40, IN0), spec(36, EXTRA0, 0), full(3, 16, 128), block, block],
        out_specs=[pl.BlockSpec((1, 1, H, H), lambda k: (0, k, 0, 0)), pl.BlockSpec((1, H, 256), lambda k: (0, 0, k)),
                   pl.BlockSpec((1, D, 128), lambda k: (0, 0, k)), full(1, D), full(1, D), full(1, 2, H), full(1, 2, H), full(classes), block, block],
        compiler_params=pltpu.CompilerParams(vmem_limit_bytes=60 * 2**20),
    )(total, total, total, total, cnt, act, igr)


def body(inputs, lengths, mlm_mask, true_types, gain_in, bias_in, gain_mid, bias_mid, w_in, conv_w, w_out, decoder, cotangent, fast):
    D, H = inputs.shape[3], w_in.shape[2]
    ring = Ring(PIECES, PLANE_UNITS, Z_UNITS) if fast else NoRing(PIECES, PLANE_UNITS + Z_UNITS)
    act, igr, total, cnt = run(
        ring, lengths[:, 0], inputs, cotangent, w_in, conv_w, w_out, gain_in, bias_in, gain_mid, bias_mid, decoder.T, mlm_mask, true_types)
    if not fast:
        c = lax.axis_index("section")
        halves = jnp.where(c == 0, total, total[::-1])
        g_two, g_one = halves[:, :UNITS], halves[:, UNITS:]
        own, other = jnp.where(c == 0, g_one, g_two), jnp.where(c == 0, g_two, g_one)
        got = lax.ppermute(other, "section", [(0, 1), (1, 0)])
        total = lax.psum(own.astype(F32) + got.astype(F32), ("dp", "seq")).astype(BF)
        cnt = lax.psum(g_one[0, EXTRA0 : EXTRA0 + 3].astype(F32), ("section", "dp", "seq")).astype(BF)
    s_conv, s_out, s_in, s_gi, s_bi, s_gm, s_bm, s_cnt, act, igr = unpack(total, cnt, act, igr, D, H, decoder.shape[1])
    return (act[None, :, None], igr[None, :, None], s_gi, s_bi, s_gm, s_bm, s_in, s_conv, s_out, s_cnt)


def solution(mesh):
    fast = mesh.shape["dp"] == 4 and mesh.shape["seq"] == 4
    return jax.shard_map(
        functools.partial(body, fast=fast),
        mesh=mesh,
        in_specs=(P(None, "dp", "seq", None), P(None, "dp"), P(None, "dp", "seq"), P(None, "dp", "seq"), P("section", None),
                  P("section", None), P("section", None, None), P("section", None, None), P("section", None, None),
                  P("section", None, None, None), P("section", None, None), P(), P(None, "dp", "seq", None)),
        out_specs=(P("section", None, "dp", "seq", None), P("section", None, "dp", "seq", None), P("section", None), P("section", None),
                   P("section", None, None), P("section", None, None), P("section", None, None), P("section", None, None, None),
                   P("section", None, None), P()),
        check_vma=False,
    )
```

```python
import functools

import jax
import jax.numpy as jnp
from jax import lax
from jax.experimental import pallas as pl
from jax.experimental.pallas import tpu as pltpu
from jax.sharding import PartitionSpec as P


EPS = 1e-05
BF, F32 = jnp.bfloat16, jnp.float32
MESH = pl.DeviceIdType.MESH
G0 = 0.7978845608028654
G1 = 0.044715
DIL = 2
HALO = 16
OUT0, CONV0, IN0, EXTRA0, UNITS = 0, 200, 700, 900, 936
PIECES, PLANE_UNITS, Z_UNITS, SLOTS = 9, 80, 24, 7


def dot(a, b):
    return lax.dot_general(a, b, (((1,), (0,)), ((), ())), preferred_element_type=F32)


def dot_nt(a, b):
    return lax.dot_general(a, b, (((1,), (1,)), ((), ())), preferred_element_type=F32)


def dot_tn(a, b):
    return lax.dot_general(a, b, (((0,), (0,)), ((), ())), preferred_element_type=F32)


def chunks(rows, fn, size=None, unroll=1):
    size = size or (96 if rows % 96 == 0 else 64)

    def one(i, _):
        fn(pl.multiple_of(i * size, size), size)
        return 0

    lax.fori_loop(0, rows // size, one, 0, unroll=unroll)


def cols(j):
    return pl.ds(j * 128, 128)


def stats(load, n):
    total = load(0)
    for j in range(1, n):
        total = total + load(j)
    mean = jnp.sum(total, axis=-1, keepdims=True) * (1.0 / (128 * n))
    square = None
    for j in range(n):
        d = load(j) - mean
        square = d * d if square is None else square + d * d
    var = jnp.sum(square, axis=-1, keepdims=True) * (1.0 / (128 * n))
    return mean, lax.rsqrt(var + EPS)


def norm_gelu(load, n, gain, shift, store):
    mean, rstd = stats(load, n)
    for j in range(n):
        u = (load(j) - mean) * rstd * gain(j) + shift(j)
        t = jnp.tanh(u * (G0 + (G0 * G1) * (u * u)))
        h = 0.5 * u
        store(j, h + h * t)


def fold(v):
    rows, width = v.shape
    return jnp.sum(v.reshape(rows // 8, 8, width), axis=0)


def norm_gelu_back(load, dy, n, gain, shift, dgain, dshift, hold, store):
    mean, rstd = stats(load, n)
    s1 = s2 = None
    for j in range(n):
        g = gain(j)
        hat = (load(j) - mean) * rstd
        u = hat * g + shift(j)
        w = u * u
        t = jnp.tanh(u * (G0 + (G0 * G1) * w))
        slope = 0.5 + 0.5 * t + u * (1.0 - t * t) * (0.5 * G0 + (1.5 * G0 * G1) * w)
        du = dy(j) * slope
        if dgain is not None:
            dgain[:, cols(j)] += fold(du * hat)
            dshift[:, cols(j)] += fold(du)
        dh = du * g
        hold[0, :, cols(j)] = hat
        hold[1, :, cols(j)] = dh
        p = dh * hat
        s1 = dh if s1 is None else s1 + dh
        s2 = p if s2 is None else s2 + p
    m1 = jnp.sum(s1, axis=-1, keepdims=True) * (1.0 / (128 * n))
    m2 = jnp.sum(s2, axis=-1, keepdims=True) * (1.0 / (128 * n))
    for j in range(n):
        store(j, rstd * (hold[1, :, cols(j)] - m1 - hold[0, :, cols(j)] * m2))


def norm_gelu_both(load, dy, n, gain, shift, dgain, dshift, hold, store, store_back):
    mean, rstd = stats(load, n)
    s1 = s2 = None
    for j in range(n):
        g = gain(j)
        hat = (load(j) - mean) * rstd
        u = hat * g + shift(j)
        w = u * u
        t = jnp.tanh(u * (G0 + (G0 * G1) * w))
        half = 0.5 + 0.5 * t
        store(j, u * half)
        slope = half + u * (1.0 - t * t) * (0.5 * G0 + (1.5 * G0 * G1) * w)
        du = dy(j) * slope
        dgain[:, cols(j)] += fold(du * hat)
        dshift[:, cols(j)] += fold(du)
        dh = du * g
        hold[0, :, cols(j)] = hat
        hold[1, :, cols(j)] = dh
        p = dh * hat
        s1 = dh if s1 is None else s1 + dh
        s2 = p if s2 is None else s2 + p
    m1 = jnp.sum(s1, axis=-1, keepdims=True) * (1.0 / (128 * n))
    m2 = jnp.sum(s2, axis=-1, keepdims=True) * (1.0 / (128 * n))
    for j in range(n):
        store_back(j, rstd * (hold[1, :, cols(j)] - m1 - hold[0, :, cols(j)] * m2))


def row(ref, k):
    return lambda j: ref[pl.ds(k, 1), cols(j)]


def view(ref, *at):
    return lambda j: ref[(*at, cols(j))].astype(F32)


def put_grad(DG, c, unit, value, col0=0):
    m, n = value.shape
    per = m // 32
    value = value.astype(BF)
    for j in range(n // 128):
        block = value[:, j * 128 : (j + 1) * 128].reshape(m // 16, 16, 128)
        for h in range(2):
            DG[lax.rem(h + c, 2), pl.ds(unit + (col0 + j) * per, per)] = block[h * per : (h + 1) * per]


def put(ref, *at):
    def store(j, v):
        ref[(*at, cols(j))] = v.astype(ref.dtype)

    return store


def positions(first, i, size):
    return first + i + lax.broadcasted_iota(jnp.int32, (size, 1), 0)


class Ring:
    KINDS = ("D", "P1", "P2", "PZ1", "PZ2", "PT1", "PT2", "PT3", "G1", "G2", "Q1", "Q2", "X1", "X2", "X3", "X4", "QT1", "QT2", "QT3", "F")

    def __init__(self, N, PU, QU):
        self.N, self.PU, self.QU, self.U = N, PU, QU, PU + QU
        self.out_units, self.live = N * self.U, True

    def scratch(self):
        PU, QU, U = self.PU, self.QU, self.U
        b = lambda u, n=SLOTS - 1: pltpu.VMEM((n, u, 16, 128), BF)
        sems = pltpu.SemaphoreType.DMA((len(self.KINDS), 2 * self.N))
        return [b(U, 4), b(PU // 2), b(PU // 4), b(PU // 4, SLOTS), b(PU // 8), b(QU, SLOTS), b(QU // 2, SLOTS), b(QU // 4), b(QU // 8), b(PU // 4), b(QU // 8),
                sems, sems]

    def bind(self, DG, out, RD, RP1, RP2, RZ1, RZ2, RQ1, RQ2, RX1, RX2, TQ, TX, ss, rs):
        N, PU, QU, U, ds = self.N, self.PU, self.QU, self.U, pl.ds
        c, z, q = lax.axis_index("section"), lax.axis_index("dp"), lax.axis_index("seq")
        xb, yb = lax.rem(q, 2), lax.div(q, 2)
        f, s = jnp.where(c == 0, xb, yb), jnp.where(c == 0, yb, xb)
        qx, qy = yb * 2 + 1 - xb, (1 - yb) * 2 + xb
        n1 = (c, z, jnp.where(c == 0, qx, qy))
        n2 = (c, z, jnp.where(c == 0, qy, qx))
        side = lax.div(z, 2)
        near, farc = side, 1 - side
        zp = (c, side * 2 + 1 - lax.rem(z, 2), q)
        far = (c, 3 - z, q)
        peer = (1 - c, z, q)
        inner = jnp.logical_or(z == 1, z == 2)
        outer = jnp.logical_not(inner)
        order = {k: i for i, k in enumerate(self.KINDS)}

        def cp(k, i, src, dst, dev):
            return remote(src, dst, ss.at[order[k], i], rs.at[order[k], i], dev)

        def add(dst, *terms):
            acc = terms[0][...].astype(F32)
            for t in terms[1:]:
                acc = acc + t[...].astype(F32)
            dst[...] = acc.astype(BF)

        def phys(i):
            return jnp.where(i < 4, i + 2, jnp.where(i < 6, i - 4, i))

        def part(i, start=0, size=U):
            return DG.at[0, ds(phys(i) * U + start, size)]

        H, Q4, E8 = PU // 2, PU // 4, PU // 8
        h, h2, h4 = QU // 2, QU // 4, QU // 8
        pq = lambda a, b: ((2 * a + b) * Q4, Q4)
        pch = lambda k: ((2 * f + s) * Q4 + k * E8, E8)
        tch = lambda k: ds(k * E8, E8)
        qn = lambda k: (PU + k * h, h)
        qhalf = lambda k, a: (PU + k * h + a * h2, h2)
        qquart = lambda k, a, b: (PU + k * h + (2 * a + b) * h4, h4)
        k8 = lambda i: lax.rem(i, SLOTS)
        k7 = lambda i: lax.rem(i, SLOTS - 1)
        rd = lambda i: RD.at[lax.rem(i, 4)]
        same = lambda k, at, dev: (lambda i: cp(k, i, part(i, *at), part(i, *at), dev))
        C = dict(
            D=lambda i: cp("D", i, DG.at[1, ds(phys(i) * U, U)], rd(i), peer),
            P1=lambda i: cp("P1", i, part(i, (1 - f) * H, H), RP1.at[k7(i)], n1),
            P2=lambda i: cp("P2", i, part(i, *pq(f, 1 - s)), RP2.at[k7(i)], n2),
            PZ1=lambda i: cp("PZ1", i, part(i, *pq(f, s)), RZ1.at[k8(i)], zp),
            PZ2=lambda i: cp("PZ2", i, part(i, *pch(farc)), RZ2.at[k7(i)], far),
            PT1=lambda i: cp("PT1", i, TQ.at[k7(i), tch(near)], TQ.at[k7(i), tch(near)], far),
            PT2=lambda i: cp("PT2", i, TQ.at[k7(i), tch(near)], TQ.at[k7(i), tch(near)], zp),
            PT3=lambda i: cp("PT3", i, TQ.at[k7(i), tch(farc)], TQ.at[k7(i), tch(farc)], zp),
            G1=same("G1", pq(f, s), n2),
            G2=same("G2", (f * H, H), n1),
            Q1=lambda i: cp("Q1", i, part(i, PU, QU), RQ1.at[k8(i)], zp),
            Q2=lambda i: cp("Q2", i, part(i, *qn(farc)), RQ2.at[k8(i)], far),
            X1=lambda i: cp("X1", i, part(i, *qhalf(near, 1 - f)), RX1.at[k7(i)], n1),
            X2=lambda i: cp("X2", i, part(i, *qquart(near, f, 1 - s)), RX2.at[k7(i)], n2),
            X3=lambda i: cp("X3", i, part(i, *qquart(near, f, s)), TX.at[k7(i)], n2),
            X4=same("X4", qhalf(near, f), n1),
            QT1=same("QT1", qn(near), far),
            QT2=same("QT2", qn(near), zp),
            QT3=same("QT3", qn(farc), zp),
        )

        def final(i, start):
            to = out.at[c, ds(phys(i) * U - jnp.where(i < N, 0, N * U), U)]
            there, here = cp("F", i, part(i), to, peer), pltpu.make_async_copy(part(i), to, ss.at[order["F"], i])
            both_ways(jnp.where(i < N, 1, 0) == c, here.start if start else here.wait, there.start if start else there.wait_send)

        def on_inner(fn):
            pl.when(inner)(fn)

        def on_outer(fn):
            pl.when(outer)(fn)

        def s0(i):
            C["D"](i).start()

        def s1(i):
            C["D"](i).wait()
            add(part(i), part(i), rd(i))
            C["P1"](i).start()
            on_outer(lambda: C["Q1"](i).start())

        def s2(i):
            @on_inner
            def _():
                C["Q1"](i).wait_recv()
                add(part(i, *qn(farc)), part(i, *qn(farc)), RQ1.at[k8(i), ds(farc * h, h)])
                C["Q2"](i).start()

            C["P1"](i).wait()
            add(part(i, f * H, H), part(i, f * H, H), RP1.at[k7(i)])
            C["P2"](i).start()
            on_outer(lambda: C["Q1"](i).wait_send())

        def s3(i):
            C["P2"](i).wait()
            add(part(i, *pq(f, s)), part(i, *pq(f, s)), RP2.at[k7(i)])
            on_outer(lambda: C["PZ1"](i).start())

            @on_inner
            def _():
                C["Q2"](i).wait()
                add(part(i, *qn(near)), part(i, *qn(near)), RQ1.at[k8(i), ds(near * h, h)], RQ2.at[k8(i)])
                C["X1"](i).start()

        def s4(i):
            @on_inner
            def _():
                C["PZ1"](i).wait_recv()
                add(part(i, *pch(farc)), part(i, *pch(farc)), RZ1.at[k8(i), tch(farc)])
                C["PZ2"](i).start()
                C["X1"](i).wait()
                add(part(i, *qhalf(near, f)), part(i, *qhalf(near, f)), RX1.at[k7(i)])
                C["X2"](i).start()

            on_outer(lambda: C["PZ1"](i).wait_send())

        def s5(i):
            @on_inner
            def _():
                C["PZ2"](i).wait()
                add(TQ.at[k7(i), tch(near)], part(i, *pch(near)), RZ1.at[k8(i), tch(near)], RZ2.at[k7(i)])
                C["PT1"](i).start()
                C["PT2"](i).start()
                C["X2"](i).wait()
                add(part(i, *qquart(near, f, s)), part(i, *qquart(near, f, s)), RX2.at[k7(i)])
                C["X3"](i).start()

        def s6(i):
            @on_inner
            def _():
                C["PT1"](i).wait()
                C["PT3"](i).start()
                C["X3"](i).wait()
                part(i, *qquart(near, f, 1 - s))[...] = TX[k7(i)]
                C["X4"](i).start()

        def s7(i):
            @on_outer
            def _():
                C["PT2"](i).wait_recv()
                C["PT3"](i).wait_recv()

            @on_inner
            def _():
                C["PT2"](i).wait_send()
                C["PT3"](i).wait_send()

            part(i, *pq(f, s))[...] = TQ[k7(i)]
            C["G1"](i).start()

            @on_inner
            def _():
                C["X4"](i).wait()
                C["QT1"](i).start()
                C["QT2"](i).start()

        def s8(i):
            C["G1"](i).wait()
            C["G2"](i).start()

            @on_inner
            def _():
                C["QT1"](i).wait()
                C["QT3"](i).start()

        def s9(i):
            C["G2"](i).wait()

            @on_outer
            def _():
                C["QT2"](i).wait_recv()
                C["QT3"](i).wait_recv()

            @on_inner
            def _():
                C["QT2"](i).wait_send()
                C["QT3"](i).wait_send()

            final(i, True)

        def s10(i):
            final(i, False)

        stages = (s0, s1, s2, s3, s4, s5, s6, s7, s8, s9, s10)

        def step(t):
            for k, stage in enumerate(stages):
                i = t - k
                pl.when(jnp.logical_and(i >= 0, i < 2 * N))(functools.partial(stage, i))

        def finish():
            def one(j, _):
                i = jnp.where(c == 1, j, j + N)
                cp("F", i, part(i), out.at[c, ds(0, U)], peer).wait_recv()
                return 0

            lax.fori_loop(0, N, one, 0)

        def barrier():
            b = pltpu.get_barrier_semaphore()
            for d in plane(c, z, q) + [zp]:
                pl.semaphore_signal(b, inc=1, device_id=d, device_id_type=MESH)

            @on_inner
            def _():
                pl.semaphore_signal(b, inc=1, device_id=far, device_id_type=MESH)
                pl.semaphore_wait(b, 9)

            on_outer(lambda: pl.semaphore_wait(b, 8))

        self.step, self.finish, self.barrier, self.iters = step, finish, barrier, 2 * N + len(stages) - 1


class NoRing:
    def __init__(self, N, U):
        self.N, self.U, self.live, self.out_units = N, U, False, 2 * N * U

    def scratch(self):
        return []

    def bind(self, *refs):
        pass

    def barrier(self):
        greet(plane(lax.axis_index("section"), lax.axis_index("dp"), lax.axis_index("seq")))

    def step(self, t):
        pass


def plane(c, z, q):
    out = []
    for i in range(1, 8):
        n = lax.rem(c * 4 + q + i, 8)
        out.append((lax.div(n, 4), z, lax.rem(n, 4)))
    return out


def greet(ids):
    barrier = pltpu.get_barrier_semaphore()
    for d in ids:
        pl.semaphore_signal(barrier, inc=1, device_id=d, device_id_type=MESH)
    pl.semaphore_wait(barrier, len(ids))


def remote(src, dst, ss, rs, dev):
    return pltpu.make_async_remote_copy(src_ref=src, dst_ref=dst, send_sem=ss, recv_sem=rs, device_id=dev, device_id_type=MESH)


def both_ways(cond, here, there):
    @pl.when(cond)
    def _():
        here()

    @pl.when(jnp.logical_not(cond))
    def _():
        there()


class Spread:
    def __init__(self, c, z, q, ss, rs, ls):
        self.c, self.z, self.q, self.ss, self.rs, self.ls = c, z, q, ss, rs, ls

    def go(self, a, src, dst, m, start):
        c, z, q = self.c, self.z, self.q
        for h in range(2):
            s, d, j = src.at[m, :, h], dst(q), 2 * m + h
            far = remote(s, d, self.ss.at[a, j], self.rs.at[a, q], (jnp.int32(h), z, 2 * c + m))
            near = pltpu.make_async_copy(s, d, self.ls.at[a])
            both_ways(jnp.logical_and(h == c, 2 * c + m == q), near.start if start else near.wait, far.start if start else far.wait_send)

    def arrive(self, a, src, dst):
        c, z, q = self.c, self.z, self.q
        fc = lax.div(q, 2)
        for p in range(4):
            @pl.when(jnp.logical_not(jnp.logical_and(c == fc, p == q)))
            def _():
                remote(src.at[0, :, 0], dst(p), self.ss.at[a, 0], self.rs.at[a, p], (fc, z, jnp.int32(p))).wait_recv()

    def back(self, a, src, dst, p, start):
        c, z, q = self.c, self.z, self.q
        tc, slot = lax.div(q, 2), lax.rem(q, 2)
        s, d = src, dst.at[slot, :, c]
        far = remote(s, d, self.ss.at[a, p], self.rs.at[a, 2 * slot + c], (tc, z, jnp.int32(p)))
        near = pltpu.make_async_copy(s, d, self.ls.at[a])
        both_ways(jnp.logical_and(tc == c, p == q), near.start if start else near.wait, far.start if start else far.wait_send)

    def back_arrive(self, a, src, dst, m):
        c, z, q = self.c, self.z, self.q
        for h in range(2):
            @pl.when(jnp.logical_not(jnp.logical_and(h == c, 2 * c + m == q)))
            def _():
                remote(src.at[pl.ds(0, 2)], dst.at[m, :, h], self.ss.at[a, 0], self.rs.at[a, 2 * m + h], (jnp.int32(h), z, 2 * c + m)).wait_recv()


def edges(ref, m, seg, ss, rs, z, q, c):
    before = remote(ref.at[m, pl.ds(HALO, HALO)], ref.at[m, pl.ds(HALO + seg, HALO)], ss.at[0, m], rs.at[0, m], (c, z, q - 1))
    after = remote(ref.at[m, pl.ds(seg, HALO)], ref.at[m, pl.ds(0, HALO)], ss.at[1, m], rs.at[1, m], (c, z, q + 1))
    return ((q > 0, q < 3, before), (q < 3, q > 0, after))


def whole(lengths, inputs, cot_all, w_in, conv_w, w_out, gain_in, bias_in, gain_mid, bias_mid, dec, mask, types, act, igr, total, cnt,
          WI, WC, WO, PR, xe, cot, out1, first1, hidden1, sec1, mixed1, third1, first2, hidden2, sec2, dth2, sp, dthr, dpad,
          third2, dsec2, og, ge, hd, hold, dgbi, dgbm, counts, DG,
          ws, wr, wl, xs, xr, xl, ss, rs, ls, gs, gr, ps, pr, pw, *ring_refs, ring):
    c, z, q = lax.axis_index("section"), lax.axis_index("dp"), lax.axis_index("seq")
    peer = (1 - c, z, q)
    seg, D = cot.shape[1:]
    H = mixed1.shape[2]
    nd, nh = D // 128, H // 128
    rows = seg + 2 * HALO
    base = q * seg
    he, dme, me = hd.at[pl.ds(0, rows)], hd.at[pl.ds(rows, rows)], hd.at[pl.ds(rows, seg)]
    ring.bind(DG, total, *ring_refs)
    own = [pltpu.make_async_copy(inputs.at[2 * c + m, 0], xe.at[m, pl.ds(HALO, seg)], xl.at[m]) for m in range(2)]
    own += [pltpu.make_async_copy(cot_all.at[2 * c + m, 0], cot.at[m], xl.at[2 + m]) for m in range(2)]
    mats = [(PR.at[c], PR.at[c]), (w_in.at[0], WI.at[c])] + [(conv_w.at[0, k], WC.at[c, k]) for k in range(5)] + [(w_out.at[0], WO.at[c])]
    loads = [pltpu.make_async_copy(s, d, wl.at[i]) for i, (s, d) in enumerate(mats) if i > 0]
    for cp in own[:2] + loads + own[2:]:
        cp.start()
    PR[c, pl.ds(4, 4)] = jnp.zeros((4, D), F32)
    PR[c, pl.ds(0, 1)] = gain_in[...].astype(F32)
    PR[c, pl.ds(1, 1)] = bias_in[...].astype(F32)
    for k in range(2):
        PR[c, pl.ds(2, 1), pl.ds(k * H, H)] = gain_mid[0, pl.ds(k, 1)].astype(F32)
        PR[c, pl.ds(3, 1), pl.ds(k * H, H)] = bias_mid[0, pl.ds(k, 1)].astype(F32)
    ring.barrier()
    sends = [remote(s, d, ws.at[i], wr.at[i], peer) for i, (s, d) in enumerate(mats)]
    halos = []
    for m in range(2):
        x = inputs.at[2 * c + m, 0]
        halos.append((q > 0, q < 3, remote(x.at[pl.ds(0, HALO)], xe.at[m, pl.ds(HALO + seg, HALO)], xs.at[0, m], xr.at[0, m], (c, z, q - 1))))
        halos.append((q < 3, q > 0, remote(x.at[pl.ds(seg - HALO, HALO)], xe.at[m, pl.ds(0, HALO)], xs.at[1, m], xr.at[1, m], (c, z, q + 1))))
    for cond, _, cp in halos:
        pl.when(cond)(cp.start)
    sends[0].start()

    @pl.when(c == 0)
    def _():
        for cp in sends[1:]:
            cp.start()

    @pl.when(c == 1)
    def _():
        for cp in sends[7:] + sends[1:7]:
            cp.start()

    @pl.when(q == 0)
    def _():
        xe[:, pl.ds(0, HALO)] = jnp.zeros((2, HALO, D), BF)
        ge[:, pl.ds(0, HALO)] = jnp.zeros((2, HALO, D), BF)

    @pl.when(q == 3)
    def _():
        xe[:, pl.ds(HALO + seg, HALO)] = jnp.zeros((2, HALO, D), BF)
        ge[:, pl.ds(HALO + seg, HALO)] = jnp.zeros((2, HALO, D), BF)

    def have(i, layer):
        both_ways(c == layer, loads[i - 1].wait, sends[i].wait_recv)

    for ref in (dgbi, dgbm, counts):
        ref[...] = jnp.zeros_like(ref)
    zero = jnp.zeros((2, 64, H), BF)
    for ref in (sp, dpad):
        ref[pl.ds(0, 2)] = zero
        ref[pl.ds(10, 2)] = zero
    sec1[:, pl.ds(0, 8)] = jnp.zeros((2, 8, H), F32)
    sec1[:, pl.ds(rows + 8, 8)] = jnp.zeros((2, 8, H), F32)
    spread = Spread(c, z, q, ss, rs, ls)
    sp_at = lambda p: sp.at[pl.ds(2 + 2 * p, 2)]
    dthr_at = lambda p: dthr.at[pl.ds(2 * p, 2)]
    gi, bi = lambda l: row(PR.at[l], 0), lambda l: row(PR.at[l], 1)
    gm = lambda l, k: (lambda j: PR[l, pl.ds(2, 1), cols(k * nh + j)])
    bm = lambda l, k: (lambda j: PR[l, pl.ds(3, 1), cols(k * nh + j)])

    sends[0].wait_recv()
    for m in range(2):
        own[m].wait()
    for _, cond, cp in halos:
        pl.when(cond)(cp.wait_recv)

    def first_norm(m, _):
        def a(i, size):
            r = pl.ds(i, size)
            norm_gelu(view(xe, m, r), nd, gi(0), bi(0), put(first1, m, r))

        chunks(rows, a, unroll=3)
        return 0

    lax.fori_loop(0, 2, first_norm, 0)
    for m in range(2):
        own[2 + m].wait()
    have(7, 1)

    def third_grad(m, _):
        dth2[m] = dot_nt(cot[m], WO[1]).astype(BF).reshape(2, 2, 64, H)
        spread.go(1, dth2, dthr_at, m, True)
        return 0

    lax.fori_loop(0, 2, third_grad, 0)
    have(1, 0)

    def second_norm(m, _):
        he[...] = dot(first1[m], WI[0])
        hidden1[m] = he[pl.ds(HALO, seg)]

        def b(i, size):
            pos = positions(base - HALO, i, size)
            keep = jnp.logical_and(pos >= 0, pos < lengths[2 * c + m])

            def store(j, v):
                sec1[m, pl.ds(i + 8, size), cols(j)] = jnp.where(keep, v, 0.0).astype(BF).astype(F32)

            norm_gelu(view(he, pl.ds(i, size)), nh, gm(0, 0), bm(0, 0), store)

        chunks(rows, b, unroll=3)
        return 0

    lax.fori_loop(0, 2, second_norm, 0)
    for k in range(5):
        have(2 + k, 0)

    def forward(m, _):
        acc = None
        for k in range(5):
            term = dot(sec1[m, pl.ds(8 + DIL * (k - 2), rows)].astype(BF), WC[0, k])
            acc = term if acc is None else acc + term
        mixed1[m] = acc

        def e(i, size):
            norm_gelu(view(mixed1, m, pl.ds(i + HALO, size)), nh, gm(0, 1), bm(0, 1), put(third1, m, pl.ds(i, size)))

        chunks(seg, e, unroll=4)

        @pl.when(m == 0)
        def _():
            have(7, 0)

        he[pl.ds(0, seg)] = dot(third1[m], WO[0, :, :H])
        me[...] = dot(third1[m], WO[0, :, H:])

        def d(i, size):
            r = pl.ds(i, size)
            for j in range(nd):
                br = he[r, cols(j)] if j < nh else me[r, cols(j - nh)]
                out1[m, r, cols(j)] = (xe[m, pl.ds(i + HALO, size), cols(j)].astype(F32) + br).astype(BF)
            norm_gelu(view(out1, m, r), nd, gi(1), bi(1), put(first2, m, r))

        chunks(seg, d, unroll=4)

        @pl.when(m == 0)
        def _():
            have(1, 1)

        hidden2[m] = dot(first2[m], WI[1])

        def f(jj, _):
            i = pl.multiple_of(jj * 64, 64)
            pos = positions(base, i, 64)

            def store(j, v):
                sec2[m, lax.div(jj, 2), lax.rem(jj, 2), :, cols(j)] = jnp.where(pos < lengths[2 * c + m], v, 0.0).astype(BF)

            norm_gelu(view(hidden2, m, pl.ds(i, 64)), nh, gm(1, 0), bm(1, 0), store)
            return 0

        lax.fori_loop(0, seg // 64, f, 0, unroll=4)
        spread.go(0, sec2, sp_at, m, True)
        return 0

    lax.fori_loop(0, 2, forward, 0)
    for k in range(5):
        have(2 + k, 1)

    def place(i, src, dst, layer):
        to = dst.at[pl.ds(2 * c, 2)]
        here, there = pltpu.make_async_copy(src, to, pw.at[i]), remote(src, to, ps.at[i], pr.at[i // 2], peer)
        both_ways(c == layer, here.start, there.start)
        return lambda: both_ways(c == layer, here.wait, there.wait_send)

    placed = [place(0, out1, act, 0)]
    for m in range(2):
        spread.go(0, sec2, sp_at, m, False)
    spread.arrive(0, sec2, sp_at)

    def conv(r, _):
        acc = None
        for k in range(5):
            term = dot(sp[pl.ds(4 * r + k, 4)].reshape(256, H), WC[1, k])
            acc = term if acc is None else acc + term
        hd[pl.ds(256 * r, 256)] = acc
        return 0

    lax.fori_loop(0, 2, conv, 0)
    for m in range(2):
        spread.go(1, dth2, dthr_at, m, False)
    spread.arrive(1, dth2, dthr_at)

    def mid(i, _):
        every = pl.ds(0, 64)
        norm_gelu_both(view(hd, pl.ds(pl.multiple_of(64 * i, 64), 64)), view(dthr, i, every), nh, gm(1, 1), bm(1, 1), dgbm.at[2], dgbm.at[3], hold,
                       put(dth2, lax.div(i, 4), lax.rem(lax.div(i, 2), 2), lax.rem(i, 2), every), put(dpad, i + 2, every))
        return 0

    lax.fori_loop(0, 8, mid, 0, unroll=4)
    for p in range(4):
        spread.back(2, dth2.at[p // 2, p % 2], third2, p, True)
    dm2 = dpad[pl.ds(2, 8)].reshape(512, H)

    for k in range(5):
        put_grad(DG, c, CONV0 + k * 100, dot_tn(sp[pl.ds(k, 8)].reshape(512, H), dm2))
        if k in (1, 3):
            ring.step(k // 2)

    def conv_back(r, _):
        acc = None
        for k in range(5):
            term = dot_nt(dpad[pl.ds(4 * r + 4 - k, 4)].reshape(256, H), WC[1, k])
            acc = term if acc is None else acc + term
        dthr[pl.ds(4 * r, 4)] = acc.astype(BF).reshape(4, 64, H)
        return 0

    lax.fori_loop(0, 2, conv_back, 0)
    for p in range(4):
        spread.back(3, dthr.at[pl.ds(2 * p, 2)], dsec2, p, True)
    ring.step(2)
    for p in range(4):
        spread.back(2, dth2.at[p // 2, p % 2], third2, p, False)
    for m in range(2):
        spread.back_arrive(2, dthr, third2, m)
    flat = lambda v: v.reshape(2 * seg, v.shape[-1])
    t2 = flat(third2[...])
    for j in range(2):
        put_grad(DG, c, OUT0, dot_tn(t2, flat(cot[:, :, pl.ds(j * H, H)])), nh * j)
    ring.step(3)
    for p in range(4):
        spread.back(3, dthr.at[pl.ds(2 * p, 2)], dsec2, p, False)
    for m in range(2):
        spread.back_arrive(3, dthr, dsec2, m)
    dh = lambda m: dpad.at[pl.ds(4 * m, 4)]

    def two(m, _):
        def b(i, _):
            pos = positions(base, i * 64, 64)
            u, h = lax.div(i, 2), lax.rem(i, 2)
            ds = lambda j: jnp.where(pos < lengths[2 * c + m], dsec2[m, u, h, :, cols(j)].astype(F32), 0.0)
            norm_gelu_back(view(hidden2, m, pl.ds(pl.multiple_of(i * 64, 64), 64)), ds, nh, gm(1, 0), bm(1, 0), dgbm.at[0], dgbm.at[1], hold,
                           put(dpad, 4 * m + i, pl.ds(0, 64)))
            return 0

        lax.fori_loop(0, seg // 64, b, 0, unroll=4)
        dhm = dh(m)[...].reshape(seg, H)
        he[pl.ds(0, seg)] = dot_nt(dhm, WI[1, :H])
        me[...] = dot_nt(dhm, WI[1, H:])

        def e(i, size):
            r = pl.ds(i, size)
            df = lambda j: he[r, cols(j)] if j < nh else me[r, cols(j - nh)]

            def store(j, v):
                ge[m, pl.ds(i + HALO, size), cols(j)] = (cot[m, r, cols(j)].astype(F32) + v).astype(BF)

            norm_gelu_back(view(out1, m, r), df, nd, gi(1), bi(1), dgbi.at[0], dgbi.at[1], hold, store)

        chunks(seg, e, unroll=4)
        for cond, _, cp in edges(ge, m, seg, gs, gr, z, q, c):
            pl.when(cond)(cp.start)
        ring.step(4 + m)
        return 0

    lax.fori_loop(0, 2, two, 0)
    placed.append(place(2, ge.at[:, pl.ds(HALO, seg)], igr, 1))
    put_grad(DG, c, IN0, dot_tn(flat(first2[...]), dpad[pl.ds(0, 8)].reshape(2 * seg, H)))

    def extra(first_unit, with_counts):
        flat_rows = [dgbi[k, :, cols(j)] for k in range(2) for j in range(nd)]
        flat_rows += [dgbm[k, :, cols(j)] for k in range(4) for j in range(nh)]
        small = [jnp.sum(v, axis=0, keepdims=True) for v in flat_rows]
        if with_counts:
            small.append(jnp.pad(jnp.sum(counts[...], axis=0, keepdims=True), ((0, 0), (0, 128 - classes))))
        size = UNITS - EXTRA0
        small.append(jnp.zeros((48 - len(small), 128), F32))
        block = jnp.concatenate(small, axis=0).astype(BF).reshape(3, 16, 128)
        for h in range(2):
            DG[h, pl.ds(first_unit, 3)] = block
            DG[h, pl.ds(first_unit + 3, size - 3)] = jnp.zeros((size - 3, 16, 128), BF)

    extra(EXTRA0, False)
    ring.step(6)
    for ref in (dgbi, dgbm):
        ref[...] = jnp.zeros_like(ref)
    for m in range(2):
        for s_cond, r_cond, cp in edges(ge, m, seg, gs, gr, z, q, c):
            pl.when(s_cond)(cp.wait_send)
            pl.when(r_cond)(cp.wait_recv)
    dm = lambda m: dsec2.at[m]

    def one(m, _):
        he[...] = dot_nt(ge[m], WO[0])

        def a(i, _):
            r = pl.ds(pl.multiple_of(i * 64 + HALO, 16), 64)
            u, h = lax.div(i, 2), lax.rem(i, 2)

            def store(j, v):
                v = v.astype(BF)
                dme[r, cols(j)] = v.astype(F32)
                dsec2[m, u, h, :, cols(j)] = v

            norm_gelu_back(view(mixed1, m, r), view(he, r), nh, gm(0, 1), bm(0, 1), dgbm.at[2], dgbm.at[3], hold, store)
            return 0

        lax.fori_loop(0, seg // 64, a, 0, unroll=4)
        for edge in (0, rows - HALO):
            r = pl.ds(edge, HALO)
            pos = positions(base - HALO, edge, HALO)
            within = jnp.logical_and(pos >= 0, pos < 4 * seg)

            def store(j, v):
                dme[r, cols(j)] = jnp.where(within, v, 0.0).astype(BF).astype(F32)

            norm_gelu_back(view(mixed1, m, r), view(he, r), nh, gm(0, 1), bm(0, 1), None, None, hold.at[:, pl.ds(0, HALO)], store)
        acc = None
        for k in range(5):
            term = dot_nt(dme[pl.ds(HALO - DIL * (k - 2), seg)].astype(BF), WC[0, k])
            acc = term if acc is None else acc + term
        he[pl.ds(0, seg)] = acc

        def b(i, _):
            r = pl.ds(pl.multiple_of(i * 64, 64), 64)
            pos = positions(base, i * 64, 64)
            ds = lambda j: jnp.where(pos < lengths[2 * c + m], he[r, cols(j)], 0.0)
            norm_gelu_back(view(hidden1, m, r), ds, nh, gm(0, 0), bm(0, 0), dgbm.at[0], dgbm.at[1], hold, put(dpad, 4 * m + i, pl.ds(0, 64)))
            return 0

        lax.fori_loop(0, seg // 64, b, 0, unroll=4)
        ring.step(7 + m)
        return 0

    lax.fori_loop(0, 2, one, 0)
    low = UNITS
    t1 = flat(third1[...])
    for j in range(2):
        put_grad(DG, c, low + OUT0, dot_tn(t1, flat(ge[:, pl.ds(HALO, seg), pl.ds(j * H, H)])), nh * j)
    ring.step(9)
    d1 = flat(dsec2[...])
    for k in range(5):
        for m in range(2):
            sec2[m] = sec1[m, pl.ds(8 + HALO + DIL * (k - 2), seg)].astype(BF).reshape(2, 2, 64, H)
        put_grad(DG, c, low + CONV0 + k * 100, dot_tn(flat(sec2[...]), d1))
        if k in (1, 3):
            ring.step(10 + k // 2)
    put_grad(DG, c, low + IN0, dot_tn(flat(first1[:, pl.ds(HALO, seg)]), dpad[pl.ds(0, 8)].reshape(2 * seg, H)))
    ring.step(12)
    classes = dec.shape[0]
    labels = lax.broadcasted_iota(jnp.int32, (1, classes), 1).astype(F32)

    def two_out(m, _):
        t = third2[m].reshape(seg, H)
        he[pl.ds(0, seg)] = dot(t, WO[1, :, :H])
        me[...] = dot(t, WO[1, :, H:])

        def a(i, size):
            r = pl.ds(i, size)
            for j in range(nd):
                br = he[r, cols(j)] if j < nh else me[r, cols(j - nh)]
                og[m, r, cols(j)] = (out1[m, r, cols(j)].astype(F32) + br).astype(BF)

        chunks(seg, a)
        logits = dot_nt(og[m], dec[...])
        ex = jnp.exp(logits - jnp.max(logits, axis=-1, keepdims=True))
        probs = ex / jnp.sum(ex, axis=-1, keepdims=True)
        pos = base + lax.broadcasted_iota(jnp.int32, (1, seg), 1)
        live = jnp.logical_and(mask[2 * c + m] == 1, pos < lengths[2 * c + m])
        code = jnp.where(live, types[2 * c + m], -1).astype(F32)
        code = jnp.broadcast_to(code, (128, seg)).T[:, :classes]
        counts[...] += fold(jnp.where(code == labels, probs, 0.0))
        ring.step(13 + m)
        return 0

    lax.fori_loop(0, 2, two_out, 0)
    placed.append(place(1, og, act, 1))
    placed[-1]()

    def one_in(m, _):
        dhm = dh(m)[...].reshape(seg, H)
        he[pl.ds(0, seg)] = dot_nt(dhm, WI[0, :H])
        me[...] = dot_nt(dhm, WI[0, H:])
        ring.step(15 + m)

        def e(i, _):
            r, x = pl.ds(pl.multiple_of(i * 64, 64), 64), pl.ds(pl.multiple_of(i * 64 + HALO, 16), 64)
            df = lambda j: he[r, cols(j)] if j < nh else me[r, cols(j - nh)]

            def store(j, v):
                og[m, r, cols(j)] = (ge[m, x, cols(j)].astype(F32) + v).astype(BF)

            norm_gelu_back(view(xe, m, x), df, nd, gi(0), bi(0), dgbi.at[0], dgbi.at[1], hold, store)

            return 0

        lax.fori_loop(0, seg // 64, e, 0)
        return 0

    lax.fori_loop(0, 2, one_in, 0)
    placed.append(place(3, og, igr, 0))
    extra(low + EXTRA0, True)

    def rest(t, _):
        ring.step(t)
        return 0

    if ring.live:
        lax.fori_loop(17, ring.iters, rest, 0)
        ring.finish()
        cnt[...] = DG[0, pl.ds(UNITS + EXTRA0, 3)]
    else:
        everything = pltpu.make_async_copy(DG, total, pw.at[0])
        everything.start()
        everything.wait()
        cnt[...] = jnp.zeros_like(cnt)
    for i in (0, 1, 3):
        placed[i]()
    for i, dst in ((0, act), (1, igr)):
        remote(og, dst.at[pl.ds(2 * (1 - c), 2)], ps.at[0], pr.at[i], peer).wait_recv()
    for cp in sends:
        cp.wait_send()
    for cond, _, cp in halos:
        pl.when(cond)(cp.wait_send)


def run(ring, lengths, inputs, cot, w_in, conv_w, w_out, gain_in, bias_in, gain_mid, bias_mid, dec, mask, types):
    seg, D, H = inputs.shape[2], inputs.shape[3], w_in.shape[2]
    rows = seg + 2 * HALO
    any_, vm, sm = (pl.BlockSpec(memory_space=s) for s in (pl.ANY, pltpu.VMEM, pltpu.SMEM))
    sh = jax.ShapeDtypeStruct
    dma = lambda *s: pltpu.SemaphoreType.DMA(s)
    part = (2, 2, 2, 64, H)
    scratch = [((2, D, H), BF), ((2, 5, H, H), BF), ((2, H, D), BF), ((2, 8, D), F32), ((2, rows, D), BF), ((2, seg, D), BF),
               ((2, seg, D), BF), ((2, rows, D), BF), ((2, seg, H), F32), ((2, rows + 16, H), F32), ((2, rows, H), F32), ((2, seg, H), BF),
               ((2, seg, D), BF), ((2, seg, H), F32), (part, BF), (part, BF), ((12, 64, H), BF), ((8, 64, H), BF),
               ((12, 64, H), BF), (part, BF), (part, BF), ((2, seg, D), BF), ((2, rows, D), BF), ((2 * rows, H), F32),
               ((2, 64, D), F32), ((2, 8, D), F32), ((4, 8, H), F32), ((8, dec.shape[0]), F32), ((2, 2 * UNITS, 16, 128), BF)]
    return pl.pallas_call(
        functools.partial(whole, ring=ring),
        out_shape=[sh((4, seg, D), BF), sh((4, seg, D), BF), sh((2, ring.out_units, 16, 128), BF), sh((3, 16, 128), BF)],
        in_specs=[sm] + [any_] * 5 + [vm] * 7,
        out_specs=[any_, any_, any_, vm],
        scratch_shapes=[pltpu.VMEM(s, d) for s, d in scratch]
        + [dma(8), dma(8), dma(8), dma(2, 2), dma(2, 2), dma(4), dma(4, 4), dma(4, 4), dma(4), dma(2, 2), dma(2, 2), dma(4), dma(2), dma(4)]
        + ring.scratch(),
        compiler_params=pltpu.CompilerParams(collective_id=1, has_side_effects=True, vmem_limit_bytes=63 * 2**20 + 2**19),
    )(lengths, inputs, cot, w_in, conv_w, w_out, gain_in, bias_in, gain_mid, bias_mid, dec, mask, types)


def unpack_kernel(conv, w_out, w_in, extra, cnt, act, igr, s_conv, s_out, s_in, gi, bi, gm, bm, counts, act_o, igr_o):
    act_o[...] = act[...]
    igr_o[...] = igr[...]
    for j in range(5):
        for h in range(2):
            s_conv[0, 0, pl.ds(h * 320, 320), cols(j)] = conv[h, pl.ds(j * 20, 20)].reshape(320, 128).astype(F32)
    for j in range(2):
        for h in range(2):
            s_out[0, pl.ds(h * 320, 320), cols(j)] = w_out[h, pl.ds(j * 20, 20)].reshape(320, 128).astype(F32)
    for h in range(2):
        s_in[0, pl.ds(h * 640, 640)] = w_in[h].reshape(640, 128).astype(F32)

    @pl.when(pl.program_id(0) == 0)
    def _():
        small = extra[0, pl.ds(0, 3)].reshape(48, 128).astype(F32)
        for j in range(10):
            gi[:, cols(j)] = small[j : j + 1]
            bi[:, cols(j)] = small[10 + j : 11 + j]
        for k in range(2):
            for j in range(5):
                gm[0, pl.ds(k, 1), cols(j)] = small[20 + 10 * k + j : 21 + 10 * k + j]
                bm[0, pl.ds(k, 1), cols(j)] = small[25 + 10 * k + j : 26 + 10 * k + j]
        counts[...] = cnt[...].reshape(48, 128)[40, : counts.shape[0]].astype(F32)


def unpack(total, cnt, act, igr, D, H, classes):
    def spec(units, first, moves=1):
        return pl.BlockSpec(tuple(pl.Element(n) for n in (2, units, 16, 128)), lambda k: (0, first + units * k * moves, 0, 0))

    def full(*s):
        return pl.BlockSpec(s, lambda k: (0,) * len(s))

    block = pl.BlockSpec((1, *act.shape[1:]), lambda k: (jnp.minimum(k, act.shape[0] - 1), 0, 0))
    sh = lambda *s: jax.ShapeDtypeStruct(s, F32)
    return pl.pallas_call(
        unpack_kernel,
        grid=(5,),
        out_shape=[sh(1, 5, H, H), sh(1, H, D), sh(1, D, H), sh(1, D), sh(1, D), sh(1, 2, H), sh(1, 2, H), sh(classes),
                   jax.ShapeDtypeStruct(act.shape, BF), jax.ShapeDtypeStruct(igr.shape, BF)],
        in_specs=[spec(100, CONV0), spec(40, OUT0), spec(40, IN0), spec(36, EXTRA0, 0), full(3, 16, 128), block, block],
        out_specs=[pl.BlockSpec((1, 1, H, H), lambda k: (0, k, 0, 0)), pl.BlockSpec((1, H, 256), lambda k: (0, 0, k)),
                   pl.BlockSpec((1, D, 128), lambda k: (0, 0, k)), full(1, D), full(1, D), full(1, 2, H), full(1, 2, H), full(classes), block, block],
        compiler_params=pltpu.CompilerParams(vmem_limit_bytes=60 * 2**20),
    )(total, total, total, total, cnt, act, igr)


def body(inputs, lengths, mlm_mask, true_types, gain_in, bias_in, gain_mid, bias_mid, w_in, conv_w, w_out, decoder, cotangent, fast):
    D, H = inputs.shape[3], w_in.shape[2]
    ring = Ring(PIECES, PLANE_UNITS, Z_UNITS) if fast else NoRing(PIECES, PLANE_UNITS + Z_UNITS)
    act, igr, total, cnt = run(
        ring, lengths[:, 0], inputs, cotangent, w_in, conv_w, w_out, gain_in, bias_in, gain_mid, bias_mid, decoder.T, mlm_mask, true_types)
    if not fast:
        c = lax.axis_index("section")
        halves = jnp.where(c == 0, total, total[::-1])
        g_two, g_one = halves[:, :UNITS], halves[:, UNITS:]
        own, other = jnp.where(c == 0, g_one, g_two), jnp.where(c == 0, g_two, g_one)
        got = lax.ppermute(other, "section", [(0, 1), (1, 0)])
        total = lax.psum(own.astype(F32) + got.astype(F32), ("dp", "seq")).astype(BF)
        cnt = lax.psum(g_one[0, EXTRA0 : EXTRA0 + 3].astype(F32), ("section", "dp", "seq")).astype(BF)
    s_conv, s_out, s_in, s_gi, s_bi, s_gm, s_bm, s_cnt, act, igr = unpack(total, cnt, act, igr, D, H, decoder.shape[1])
    return (act[None, :, None], igr[None, :, None], s_gi, s_bi, s_gm, s_bm, s_in, s_conv, s_out, s_cnt)


def solution(mesh):
    fast = mesh.shape["dp"] == 4 and mesh.shape["seq"] == 4
    return jax.shard_map(
        functools.partial(body, fast=fast),
        mesh=mesh,
        in_specs=(P(None, "dp", "seq", None), P(None, "dp"), P(None, "dp", "seq"), P(None, "dp", "seq"), P("section", None),
                  P("section", None), P("section", None, None), P("section", None, None), P("section", None, None),
                  P("section", None, None, None), P("section", None, None), P(), P(None, "dp", "seq", None)),
        out_specs=(P("section", None, "dp", "seq", None), P("section", None, "dp", "seq", None), P("section", None), P("section", None),
                   P("section", None, None), P("section", None, None), P("section", None, None), P("section", None, None, None),
                   P("section", None, None), P()),
        check_vma=False,
    )
```
